32 devices in a mesh: grp: 2 (over y), freq: 4 (over z), shot: 2 (over x), rcv: 2 (over core).
Axes of the slice: x: 2, y: 2, z: 4, core: 2. Of those that a mesh axis runs over, the one named last changes fastest.
Arguments:
- data: bfloat16 [2, 256, 32, 4096], P(None, 'freq', ('grp', 'shot'), 'rcv'), parts along dimension 2, may hold values from -6 to 6
- estimate: bfloat16 [2, 256, 32, 4096], P(None, 'freq', ('grp', 'shot'), 'rcv'), parts along dimension 2, may hold values from -0.09375 to 0.09375
- window_data: bfloat16 [2, 256, 32, 16], P(None, 'freq', ('grp', 'shot')), parts along dimension 2, may hold values from -6 to 6
- wavelet: float32 [2, 512], P(None, ('grp', 'freq')), parts along dimension 1, may hold values from -24 to 24
- positions: int32 [32], P(('grp', 'shot')), parts along dimension 0, may hold values from 0 to 4095
- bins: int32 [512], P('grp'), parts along dimension 0, may hold values from 0 to 399
- threshold: int32 [2], P('grp'), parts along dimension 0, may hold values from 8 to 40
- step: float32 [2], P('grp'), parts along dimension 0, may hold values from 0.25 to 1
Outputs:
- primaries: bfloat16 [1024, 32, 4096], P('freq', ('grp', 'shot'), 'rcv'), parts along dimension 1
The draws below stay inside these ranges and needn't reach their ends.
There are 2 independent parts, one for each index of `grp`. The reference program is written for one: setup_inputs(seed, part) draws one part's arguments, and reference() takes and returns one part's arrays. A program takes and returns all parts, laid end to end along the dimension named above; each array names one. Nothing has to cross between parts.
All inputs are finite; a program needn't handle non-finite values.
Results may differ from the reference program's by a relative error of at most 0.0059.
The reference program's roundings to bfloat16 on the way count: a program that leaves them out, or rounds other values in their place, can miss the bound.
Values may be sent and summed in bfloat16 or wider, within the bound.
A program may use at most 64 MiB of HBM per device.

```python
import math
import jax
import jax.numpy as jnp
from jax import lax

NF = 256
RCV = 4096
NT = 1024
NBIN = 400
ROWS = 16
SHOTS = 16


def touch_ends(result, stream_key, smallest, top_value):
    extent = result.shape
    index_at = [jax.random.randint(jax.random.fold_in(stream_key, axis), (), 0, extent[axis]) for axis in range(len(extent))]
    result = result.at[tuple(index_at)].set(smallest)
    longest = extent.index(max(extent))
    index_at[longest] = (index_at[longest] + 1) % extent[longest]
    return result.at[tuple(index_at)].set(top_value)


def steps_of(own_key, extent, split, smallest, high):
    loudness, own = 1.0, jax.random.fold_in(own_key, 6)
    for axis_at, blocks in split:
        heights = jnp.exp(jax.random.uniform(jax.random.fold_in(own, axis_at), (blocks,), jnp.float32, smallest / len(split), high / len(split)))
        loudness = loudness * jnp.repeat(heights, extent[axis_at] // blocks).reshape([-1 if axis == axis_at else 1 for axis in range(len(extent))])
    return loudness


def scatter_about(own_key, extent, spread, reach, pieces=(), kind=jnp.bfloat16):
    gain = steps_of(own_key, extent, pieces, -0.22, 0.18) if pieces else 1.0
    array = jax.random.normal(own_key, extent, jnp.float32) * spread * gain
    return jnp.minimum(jnp.maximum(array, -reach), reach).astype(kind)


def setup_inputs(seed: int = 0, part: int = 0) -> dict:
    keys = jax.random.split(jax.random.key(seed), 9)
    part_splits = jax.random.split(jax.random.fold_in(keys[8], part), 9)
    return {
        "data": scatter_about(part_splits[0], (2, NF, SHOTS, RCV), 1.0, 6.0, ((1, 4), (2, 2), (3, 2))),
        "estimate": scatter_about(part_splits[1], (2, NF, ROWS, RCV), RCV ** -0.5, 0.09375, ((1, 4), (2, 2), (3, 2))),
        "window_data": scatter_about(part_splits[2], (2, NF, ROWS, SHOTS), 1.0, 6.0, ((1, 4), (2, 2))),
        "wavelet": scatter_about(part_splits[3], (2, NF), 4.0, 24.0, ((1, 4),), jnp.float32),
        "positions": touch_ends(jax.random.randint(part_splits[4], (SHOTS,), 0, RCV), jax.random.fold_in(part_splits[4], 1), 0, RCV - 1).astype(jnp.int32),
        "bins": touch_ends(jax.random.randint(part_splits[5], (NF,), 0, NBIN), jax.random.fold_in(part_splits[5], 1), 0, NBIN - 1).astype(jnp.int32),
        "threshold": jax.random.randint(part_splits[6], (1,), 8, 41).astype(jnp.int32),
        "step": jnp.clip(jnp.exp(jax.random.uniform(part_splits[7], (1,), jnp.float32, math.log(0.25), math.log(1.0))), 0.25, 1.0),
    }


def reference(data, estimate, window_data, wavelet, positions, bins, threshold, step):
    norm = 1.0 / math.sqrt(SHOTS * RCV)
    step_size = step[0]
    select = (jnp.arange(RCV, dtype=jnp.int32)[None, :] == positions[:, None]).astype(jnp.float32)

    def per_freq(items):
        est_re, est_im, line_re, line_im, rec_re, rec_im, source = items
        down_re = (source[0] * select - line_re.astype(jnp.float32)).astype(jnp.bfloat16)
        down_im = (source[1] * select - line_im.astype(jnp.float32)).astype(jnp.bfloat16)
        model_re = jnp.dot(est_re, down_re.T, preferred_element_type=jnp.float32) - jnp.dot(est_im, down_im.T, preferred_element_type=jnp.float32)
        model_im = jnp.dot(est_re, down_im.T, preferred_element_type=jnp.float32) + jnp.dot(est_im, down_re.T, preferred_element_type=jnp.float32)
        err_re = (rec_re.astype(jnp.float32) - model_re).astype(jnp.bfloat16)
        err_im = (rec_im.astype(jnp.float32) - model_im).astype(jnp.bfloat16)
        grad_re = jnp.dot(err_re, down_re, preferred_element_type=jnp.float32) + jnp.dot(err_im, down_im, preferred_element_type=jnp.float32)
        grad_im = jnp.dot(err_im, down_re, preferred_element_type=jnp.float32) - jnp.dot(err_re, down_im, preferred_element_type=jnp.float32)
        upd_re = (est_re.astype(jnp.float32) - step_size * (grad_re * norm)).astype(jnp.bfloat16)
        upd_im = (est_im.astype(jnp.float32) - step_size * (grad_im * norm)).astype(jnp.bfloat16)
        return (upd_re, upd_im)
    upd_re, upd_im = lax.map(per_freq, (estimate[0], estimate[1], data[0], data[1], window_data[0], window_data[1], wavelet.T))
    times = jnp.arange(NT, dtype=jnp.int32)
    phase = bins[:, None] * times[None, :] % NT
    angle = 2.0 * math.pi / NT * phase.astype(jnp.float32)
    table = jnp.concatenate([jnp.cos(angle), -jnp.sin(angle)], axis=0).astype(jnp.bfloat16)
    stacked = jnp.concatenate([upd_re, upd_im], axis=0).reshape(2 * NF, ROWS * RCV)
    trace = jnp.dot(table.T, stacked, preferred_element_type=jnp.float32) * math.sqrt(RCV / NF)
    trace = trace.reshape(NT, ROWS, RCV)
    level = threshold[0].astype(jnp.float32) / 64.0
    return (jnp.sign(trace) * jnp.maximum(jnp.abs(trace) - level, 0.0)).astype(jnp.bfloat16)
```

```python
from functools import partial
import math

import jax
import jax.numpy as jnp
from jax import lax
from jax.experimental import pallas as pl
from jax.experimental.pallas import tpu as pltpu
from jax.sharding import PartitionSpec as P

NF = 256
RCV = 4096
NT = 1024
FC = 8
BLOCK = 256
LAG = 1
MESH = pl.DeviceIdType.MESH


def iota(shape, dim):
    return lax.broadcasted_iota(jnp.int32, shape, dim)


def make_traces(u, table, lv, gain, rows, t_group, sparse, out):
    groups, _, width = u.shape
    part = 2 * FC
    nt = table.shape[0]
    for i in range(rows):
        ui = u[:, i * part:(i + 1) * part, :].reshape(groups * part, width)
        tr = jnp.dot(table[...], ui, preferred_element_type=jnp.float32) * gain
        sparse[i] = (jnp.maximum(tr - lv, 0.0) + jnp.minimum(tr + lv, 0.0)).astype(jnp.bfloat16)
    n = t_group * rows
    dst, src = iota((n, n), 0), iota((n, n), 1)
    perm = (src == (dst % rows) * t_group + dst // rows).astype(jnp.bfloat16)
    for g in range(nt // t_group):
        x = sparse[:, g * t_group:(g + 1) * t_group, :].reshape(n, width)
        out[g * n:(g + 1) * n, :] = jnp.dot(
            perm, x, preferred_element_type=jnp.float32
        ).astype(jnp.bfloat16)


def update_kernel(
    nx, nz, nchunk, rows, lines, norm, blocks, helped, gain, t_group,
    data, est, win, wav, pos, step, level, table, out, given,
    down, est_p, upd, mod_mine, mod_other, ubuf, sparse, made,
    x_send, x_recv, c_send, c_recv, za_send, za_recv, zb_send, zb_recv,
    zc_send, zc_recv, g_send, g_recv, own_sem, ubuf_sem,
):
    mx = lax.axis_index("shot")
    mz = lax.axis_index("freq")
    mc = lax.axis_index("rcv")
    width = data.shape[2]
    fl = FC * lines
    fi = FC * rows

    barrier = pltpu.get_barrier_semaphore()
    for d in range(1, nx):
        pl.semaphore_signal(
            barrier, inc=1, device_id={"shot": lax.rem(mx + d, nx)}, device_id_type=MESH
        )
    pl.semaphore_signal(barrier, inc=1, device_id={"rcv": 1 - mc}, device_id_type=MESH)

    @pl.when(mz > 0)
    def _():
        pl.semaphore_signal(barrier, inc=1, device_id={"freq": mz - 1}, device_id_type=MESH)

    @pl.when(mz < nz - 1)
    def _():
        pl.semaphore_signal(barrier, inc=1, device_id={"freq": mz + 1}, device_id_type=MESH)

    ends = (mz > 0).astype(jnp.int32) + (mz < nz - 1).astype(jnp.int32)
    pl.semaphore_wait(barrier, nx + ends)

    def x_copy(d, k):
        piece = down.at[k, :, pl.ds(mx * fl, fl)]
        return pltpu.make_async_remote_copy(
            src_ref=piece, dst_ref=piece,
            send_sem=x_send.at[d, k], recv_sem=x_recv.at[d, k],
            device_id={"shot": lax.rem(mx + d, nx)}, device_id_type=MESH,
        )

    def c_copy(k):
        return pltpu.make_async_remote_copy(
            src_ref=mod_mine.at[k], dst_ref=mod_other.at[k],
            send_sem=c_send.at[k], recv_sem=c_recv.at[k],
            device_id={"rcv": 1 - mc}, device_id_type=MESH,
        )

    def w_of(way):
        return 0 if way > 0 else 1

    def last(z, way):
        return z == (nz - 1 if way > 0 else 0)

    def a_copy(src, slot, k, way):
        return pltpu.make_async_remote_copy(
            src_ref=src, dst_ref=out.at[pl.ds(0, helped), slot, k],
            send_sem=za_send.at[w_of(way), slot, k], recv_sem=za_recv.at[w_of(way), slot, k],
            device_id={"freq": mz + way}, device_id_type=MESH,
        )

    def b_copy(src, slot, k, way):
        return pltpu.make_async_remote_copy(
            src_ref=src, dst_ref=out.at[pl.ds(helped, blocks - helped), slot, k],
            send_sem=zb_send.at[w_of(way), slot, k], recv_sem=zb_recv.at[w_of(way), slot, k],
            device_id={"freq": mz + way}, device_id_type=MESH,
        )

    def block_copy(slot, b, way):
        piece = out.at[b, slot]
        return pltpu.make_async_remote_copy(
            src_ref=piece, dst_ref=piece,
            send_sem=zc_send.at[w_of(way), slot, b], recv_sem=zc_recv.at[w_of(way), slot, b],
            device_id={"freq": mz + way}, device_id_type=MESH,
        )

    def given_copy(b, way):
        return pltpu.make_async_remote_copy(
            src_ref=made.at[b], dst_ref=given.at[b],
            send_sem=g_send.at[b], recv_sem=g_recv.at[b],
            device_id={"freq": mz + way}, device_id_type=MESH,
        )

    a_own = lambda k: upd.at[k, pl.ds(0, helped)]
    b_own = lambda k: upd.at[k, pl.ds(helped, blocks - helped)]
    a_out = lambda slot, k: out.at[pl.ds(0, helped), slot, k]
    b_out = lambda slot, k: out.at[pl.ds(helped, blocks - helped), slot, k]

    def own_copy(k):
        return pltpu.make_async_copy(upd.at[k], out.at[:, mz, k], own_sem.at[k])

    column = mc * width + iota((lines, width), 1)
    select = (column == pos[:, :]).astype(jnp.float32)

    def make_down(k, carry):
        for c in range(2):
            parts = []
            lines_k = data[c, pl.ds(pl.multiple_of(k * fl, fl), fl)].astype(jnp.float32)
            for f in range(FC):
                w = wav[c, k * FC + f]
                parts.append(w * select - lines_k[f * lines:(f + 1) * lines])
            down[k, c, pl.ds(pl.multiple_of(mx * fl, fl), fl)] = jnp.concatenate(
                parts, axis=0
            ).astype(jnp.bfloat16)
        for d in range(1, nx):
            x_copy(d, k).start()
        return carry

    lax.fori_loop(0, nchunk, make_down, 0)

    n = 2 * fi
    dst, src = iota((n, n), 0), iota((n, n), 1)
    want = (dst // FC % 2) * fi + (dst % FC) * rows + dst // (2 * FC)
    perm = (src == want).astype(jnp.bfloat16)

    def chunk_of(ref, k):
        part = pl.ds(pl.multiple_of(k * fi, fi), fi)
        return jnp.concatenate([ref[0, part], ref[1, part]], axis=0)

    def permute(k, carry):
        est_p[k] = jnp.dot(
            perm, chunk_of(est, k), preferred_element_type=jnp.float32
        ).astype(jnp.bfloat16)
        return carry

    lax.fori_loop(0, nchunk, permute, 0)

    cols = nx * fl
    shots = win.shape[2]
    s_row, s_col = iota((shots, cols), 0), iota((shots, cols), 1)
    spread = (s_row == (s_col // fl) * lines + s_col % lines).astype(jnp.bfloat16)
    shape3 = (rows, FC, cols)
    same = iota(shape3, 1) == iota(shape3, 2) % fl // lines
    scale = step[0]

    def model(k):
        for d in range(1, nx):
            here = down.at[k, :, pl.ds(lax.rem(mx + nx - d, nx) * fl, fl)]
            pltpu.make_async_remote_copy(
                src_ref=here, dst_ref=here,
                send_sem=x_send.at[d, k], recv_sem=x_recv.at[d, k],
                device_id={"shot": lax.rem(mx + d, nx)}, device_id_type=MESH,
            ).wait_recv()
        lines_k = down[k].reshape(2 * cols, width)
        m = lax.dot_general(
            est_p[k], lines_k, (((1,), (1,)), ((), ())), preferred_element_type=jnp.float32
        ).reshape(rows, 2, FC, 2 * cols)
        mod_mine[k, 0] = m[:, 0, :, :cols] - m[:, 1, :, cols:]
        mod_mine[k, 1] = m[:, 0, :, cols:] + m[:, 1, :, :cols]
        c_copy(k).start()

    def update(k):
        c_copy(k).wait_recv()
        total_re = mod_mine[k, 0] + mod_other[k, 0]
        total_im = mod_mine[k, 1] + mod_other[k, 1]
        w = jnp.dot(perm, chunk_of(win, k), preferred_element_type=jnp.float32).astype(jnp.bfloat16)
        w = jnp.dot(w, spread, preferred_element_type=jnp.float32).reshape(rows, 2, FC, cols)
        e_re = jnp.where(same, w[:, 0] - total_re, 0.0)
        e_im = jnp.where(same, w[:, 1] - total_im, 0.0)
        e = jnp.stack(
            [jnp.concatenate([e_re, e_im], axis=2), jnp.concatenate([e_im, -e_re], axis=2)], axis=1
        ).reshape(n, 2 * cols).astype(jnp.bfloat16)
        grad = jnp.dot(e, down[k].reshape(2 * cols, width), preferred_element_type=jnp.float32)
        new = (est_p[k].astype(jnp.float32) - scale * (grad * norm)).astype(jnp.bfloat16)
        for b in range(blocks):
            upd[k, b] = new[:, b * BLOCK:(b + 1) * BLOCK]
        own_copy(k).start()
        for way in (1, -1):
            @pl.when(jnp.logical_not(last(mz, way)))
            def _():
                b_copy(b_own(k), mz, k, way).start()

                if helped:
                    @pl.when(jnp.logical_not(last(mz + way, way)))
                    def _():
                        a_copy(a_own(k), mz, k, way).start()

    def near(k):
        for way in (1, -1):
            slot = mz - way

            @pl.when((slot >= 0) & (slot < nz))
            def _():
                b_copy(b_out(slot, k), slot, k, way).wait_recv()

                if helped:
                    @pl.when(jnp.logical_not(last(mz, way)))
                    def _():
                        a_copy(a_out(slot, k), slot, k, way).wait_recv()

                @pl.when(last(mz + way, way))
                def _():
                    b_copy(b_out(slot, k), slot, k, way).start()

    def step_of(k, carry):
        @pl.when(k < nchunk)
        def _():
            model(k)
            update(k)

        @pl.when(k >= LAG)
        def _():
            near(k - LAG)

        return carry

    lax.fori_loop(0, nchunk + LAG, step_of, 0)

    def own_done(k, carry):
        own_copy(k).wait()
        return carry

    lax.fori_loop(0, nchunk, own_done, 0)

    def hand_on(b, carry):
        for way in (1, -1):
            slot = mz - way
            inside = (slot >= 0) & (slot < nz)
            nxt = mz + way

            @pl.when(inside & (nxt > 0) & (nxt < nz - 1))
            def _():
                block_copy(slot, b, way).start()

        return carry

    lax.fori_loop(0, blocks, hand_on, 0)

    def far(h, carry):
        def one(b, carry):
            for way in (1, -1):
                slot = mz - way * h
                nxt = mz + way
                inside = (slot >= 0) & (slot < nz)
                at_end = last(mz, way)

                @pl.when(inside & jnp.logical_not(at_end))
                def _():
                    block_copy(slot, b, way).wait_recv()

                    @pl.when(jnp.logical_not(last(nxt, way)) | (b >= helped))
                    def _():
                        block_copy(slot, b, way).start()

                    if helped:
                        @pl.when(last(nxt, way) & (b < helped) & last(slot, -way))
                        def _():
                            load = pltpu.make_async_copy(out.at[b], ubuf, ubuf_sem)
                            load.start()
                            load.wait()
                            make_traces(
                                ubuf.reshape(nz * nchunk, ubuf.shape[2], BLOCK), table, level[0],
                                gain, rows, t_group, sparse, made.at[b],
                            )
                            given_copy(b, way).start()

                @pl.when(inside & at_end & (b >= helped))
                def _():
                    if not near_by:
                        block_copy(slot, b, way).wait_recv()

            return carry

        near_by = isinstance(h, int)
        return lax.fori_loop(0, blocks, one, carry)

    def end_chunk(k, carry):
        for way in (1, -1):
            slot = mz - 2 * way

            @pl.when((slot >= 0) & (slot < nz) & last(mz, way))
            def _():
                b_copy(b_out(slot, k), slot, k, way).wait_recv()

        return carry

    if nz > 2:
        lax.fori_loop(0, nchunk, end_chunk, 0)
        far(2, 0)
    lax.fori_loop(3, nz, far, 0)

    if helped:
        def take(b, carry):
            for way in (1, -1):
                @pl.when(last(mz, way))
                def _():
                    given_copy(b, way).wait_recv()

                @pl.when(last(mz + way, way))
                def _():
                    given_copy(b, way).wait_send()

            return carry

        lax.fori_loop(0, helped, take, 0)

    def drain(k, carry):
        for d in range(1, nx):
            x_copy(d, k).wait_send()
        c_copy(k).wait_send()
        for way in (1, -1):
            nxt = mz + way

            @pl.when(jnp.logical_not(last(mz, way)))
            def _():
                b_copy(b_own(k), mz, k, way).wait_send()

                if helped:
                    @pl.when(jnp.logical_not(last(nxt, way)))
                    def _():
                        a_copy(a_own(k), mz, k, way).wait_send()

            slot = mz - way

            @pl.when((slot >= 0) & (slot < nz) & last(nxt, way))
            def _():
                b_copy(b_own(k), slot, k, way).wait_send()

        return carry

    lax.fori_loop(0, nchunk, drain, 0)

    def drain_far(h, carry):
        def one(b, carry):
            for way in (1, -1):
                slot = mz - way * h
                nxt = mz + way
                inside = (slot >= 0) & (slot < nz) & (nxt >= 0) & (nxt < nz)
                to_end = last(nxt, way)

                @pl.when(inside & (jnp.logical_not(to_end) | ((b >= helped) & (h > 1))))
                def _():
                    block_copy(slot, b, way).wait_send()

            return carry

        return lax.fori_loop(0, blocks, one, carry)

    lax.fori_loop(1, nz, drain_far, 0)


def trace_kernel(rows, t_group, gain, helped, level, taken, table, u, given, out, sparse):
    ready = (pl.program_id(0) < helped) & (taken[0] > 0)

    @pl.when(ready)
    def _():
        out[...] = given[...]

    @pl.when(jnp.logical_not(ready))
    def _():
        make_traces(u, table, level[0], gain, rows, t_group, sparse, out)


def body(nx, nz, data, estimate, window_data, wavelet, positions, bins, threshold, step):
    _, nf, lines, width = data.shape
    rows = estimate.shape[2]
    shots = window_data.shape[3]
    nchunk = nf // FC
    norm = 1.0 / math.sqrt(shots * RCV)
    fi, cols = FC * rows, nx * FC * lines
    mz = lax.axis_index("freq")
    nt = NT // nz
    blocks, groups = width // BLOCK, nz * nchunk
    helped = 3 * blocks // 8 if nz >= 4 else 0
    held = max(helped, 1)
    gain, t_group = math.sqrt(RCV / NF), 32
    level = threshold.astype(jnp.float32) / 64.0

    def table_of(z):
        times = z * nt + lax.iota(jnp.int32, nt)
        phase = times[:, None] * bins[None, :] % NT
        angle = 2.0 * math.pi / NT * phase.astype(jnp.float32)
        table = jnp.stack([jnp.cos(angle), -jnp.sin(angle)], axis=1).astype(jnp.bfloat16)
        table = table.reshape(nt, 2, groups, FC).transpose(0, 2, 1, 3)
        return table.reshape(nt, 2 * nz * nf)

    vmem = pl.BlockSpec(memory_space=pltpu.VMEM)
    smem = pl.BlockSpec(memory_space=pltpu.SMEM)
    hbm = pl.BlockSpec(memory_space=pl.ANY)
    dma = pltpu.SemaphoreType.DMA
    spectra, given = pl.pallas_call(
        partial(
            update_kernel, nx, nz, nchunk, rows, lines, norm, blocks, helped, gain, t_group
        ),
        out_shape=(
            jax.ShapeDtypeStruct((blocks, nz, nchunk, 2 * fi, BLOCK), jnp.bfloat16),
            jax.ShapeDtypeStruct((held, nt * rows, BLOCK), jnp.bfloat16),
        ),
        in_specs=[vmem, vmem, vmem, smem, vmem, smem, smem, vmem],
        out_specs=(hbm, hbm),
        scratch_shapes=[
            pltpu.VMEM((nchunk, 2, cols, width), jnp.bfloat16),
            pltpu.VMEM((nchunk, 2 * fi, width), jnp.bfloat16),
            pltpu.VMEM((nchunk, blocks, 2 * fi, BLOCK), jnp.bfloat16),
            pltpu.VMEM((nchunk, 2, rows, FC, cols), jnp.float32),
            pltpu.VMEM((nchunk, 2, rows, FC, cols), jnp.float32),
            pltpu.VMEM((nz, nchunk, 2 * fi, BLOCK), jnp.bfloat16),
            pltpu.VMEM((rows, nt, BLOCK), jnp.bfloat16),
            pltpu.VMEM((held, nt * rows, BLOCK), jnp.bfloat16),
            dma((nx, nchunk)), dma((nx, nchunk)),
            dma((nchunk,)), dma((nchunk,)),
            dma((2, nz, nchunk)), dma((2, nz, nchunk)),
            dma((2, nz, nchunk)), dma((2, nz, nchunk)),
            dma((2, nz, blocks)), dma((2, nz, blocks)),
            dma((held,)), dma((held,)),
            dma((nchunk,)), dma,
        ],
        compiler_params=pltpu.CompilerParams(
            collective_id=0, has_side_effects=True, vmem_limit_bytes=58 << 20
        ),
        name="update",
    )(
        data.reshape(2, nf * lines, width),
        estimate.reshape(2, nf * rows, width),
        window_data.reshape(2, nf * rows, shots),
        wavelet,
        positions[:, None],
        step,
        level,
        table_of(jnp.where(mz < nz // 2, 0, nz - 1)),
    )
    taken = ((mz == 0) | (mz == nz - 1)).astype(jnp.int32)[None]
    traces = pl.pallas_call(
        partial(trace_kernel, rows, t_group, gain, helped),
        out_shape=jax.ShapeDtypeStruct((nt * rows, width), jnp.bfloat16),
        grid=(blocks,),
        in_specs=[
            smem,
            smem,
            pl.BlockSpec((nt, 2 * nz * nf), lambda j: (0, 0)),
            pl.BlockSpec((None, groups, 2 * fi, BLOCK), lambda j: (j, 0, 0, 0)),
            pl.BlockSpec(
                (None, nt * rows, BLOCK), lambda j: (jnp.minimum(j, held - 1), 0, 0)
            ),
        ],
        out_specs=pl.BlockSpec((nt * rows, BLOCK), lambda j: (0, j)),
        scratch_shapes=[pltpu.VMEM((rows, nt, BLOCK), jnp.bfloat16)],
        compiler_params=pltpu.CompilerParams(vmem_limit_bytes=60 << 20),
        name="traces",
    )(level, taken, table_of(mz), spectra.reshape(blocks, groups, 2 * fi, BLOCK), given)
    return traces.reshape(nt, rows, width)


def relay_kernel(
    nx, nz, nchunk, rows, lines, shots, norm, blocks, plain, early, gain, t_group,
    data, est, win, wav, pos, bins, thr, step, out,
    dbuf, ebuf, down, est_p, spec, mod_mine, mod_other, tables, sparse, made, obuf,
    d_sem, e_sem, x_send, x_recv, c_send, c_recv, z_send, z_recv, o_sem,
):
    mx = lax.axis_index("shot")
    mz = lax.axis_index("freq")
    mc = lax.axis_index("rcv")
    width = data.shape[2]
    fl = FC * lines
    fi = FC * rows
    n = 2 * fi
    part = nchunk * n
    end = jnp.where(mz < 2, 0, 3)
    inner = jnp.where(mz < 2, 1, 2)
    is_end = mz == end
    is_inner = jnp.logical_not(is_end)
    level = thr[0].astype(jnp.float32) / 64.0

    def load(ref, buf, sem, k):
        return pltpu.make_async_copy(
            ref.at[:, pl.ds(pl.multiple_of(k * fl, fl), fl)], buf.at[k], sem.at[k]
        )

    def load_all(k, carry):
        load(data, dbuf, d_sem, k).start()
        load(est, ebuf, e_sem, k).start()
        return carry

    lax.fori_loop(0, nchunk, load_all, 0)

    barrier = pltpu.get_barrier_semaphore()
    for d in range(1, nx):
        pl.semaphore_signal(
            barrier, inc=1, device_id={"shot": lax.rem(mx + d, nx)}, device_id_type=MESH
        )
    pl.semaphore_signal(barrier, inc=1, device_id={"rcv": 1 - mc}, device_id_type=MESH)
    pl.semaphore_signal(
        barrier, inc=1, device_id={"freq": jnp.where(is_end, inner, end)}, device_id_type=MESH
    )

    @pl.when(is_inner)
    def _():
        pl.semaphore_signal(barrier, inc=1, device_id={"freq": 3 - mz}, device_id_type=MESH)

    pl.semaphore_wait(barrier, nx + 1 + is_inner.astype(jnp.int32))

    def x_copy(d, k, piece):
        here = down.at[k, :, pl.ds(piece * fl, fl)]
        return pltpu.make_async_remote_copy(
            src_ref=here, dst_ref=here,
            send_sem=x_send.at[d, k], recv_sem=x_recv.at[d, k],
            device_id={"shot": lax.rem(mx + d, nx)}, device_id_type=MESH,
        )

    def c_copy(k):
        return pltpu.make_async_remote_copy(
            src_ref=mod_mine.at[k], dst_ref=mod_other.at[k],
            send_sem=c_send.at[k], recv_sem=c_recv.at[k],
            device_id={"rcv": 1 - mc}, device_id_type=MESH,
        )

    def z_copy(kind, at, here, there, to):
        return pltpu.make_async_remote_copy(
            src_ref=here, dst_ref=there,
            send_sem=z_send.at[kind, at], recv_sem=z_recv.at[kind, at],
            device_id={"freq": to}, device_id_type=MESH,
        )

    def chunk_copy(kind, slot, k, lo, count, to):
        row = pl.multiple_of(slot * part + k * n, n)
        here = spec.at[pl.ds(lo, count), pl.ds(row, n)]
        return z_copy(kind, k, here, here, to)

    def block_copy(kind, slot, b, to):
        here = spec.at[b, pl.ds(pl.multiple_of(slot * part, part), part)]
        return z_copy(kind, b, here, here, to)

    late = blocks - early
    to_inner_early = lambda k: chunk_copy(0, end, k, 0, early, inner)
    to_inner_late = lambda k: chunk_copy(1, end, k, early, late, inner)
    across_own = lambda k, own: chunk_copy(2, own, k, 0, early, 3 - mz)
    across_end = lambda k, of: chunk_copy(3, of, k, 0, early, 3 - mz)
    out_own = lambda k: chunk_copy(4, inner, k, 0, plain, end)
    out_opp = lambda k: chunk_copy(5, 3 - inner, k, 0, plain, end)
    out_far = lambda k: chunk_copy(6, 3 - end, k, 0, plain, end)
    block_own = lambda b, own: block_copy(7, own, b, 3 - mz)
    block_end = lambda b, of: block_copy(8, of, b, 3 - mz)
    landing = lambda b: spec.at[b, pl.ds(part, 2 * part)]
    trace_copy = lambda b: z_copy(9, b, made.at[b - plain], landing(b), end)

    def out_copy(src, b, sem):
        return pltpu.make_async_copy(
            src, out.at[:, pl.ds(pl.multiple_of(b * BLOCK, BLOCK), BLOCK)], sem
        )

    line, column = iota((lines, width), 0), mc * width + iota((lines, width), 1)
    select = jnp.zeros((lines, width), jnp.float32)
    for s in range(lines):
        select = jnp.where((line == s) & (column == pos[s]), 1.0, select)

    def make_down(k):
        load(data, dbuf, d_sem, k).wait()
        for c in range(2):
            parts = []
            lines_k = dbuf[k, c].astype(jnp.float32)
            for f in range(FC):
                w = wav[c, k * FC + f]
                parts.append(w * select - lines_k[f * lines:(f + 1) * lines])
            down[k, c, pl.ds(pl.multiple_of(mx * fl, fl), fl)] = jnp.concatenate(
                parts, axis=0
            ).astype(jnp.bfloat16)
        for d in range(1, nx):
            x_copy(d, k, mx).start()

    dst, src = iota((n, n), 0), iota((n, n), 1)
    want = (dst // FC % 2) * fi + (dst % FC) * rows + dst // (2 * FC)
    perm = (src == want).astype(jnp.bfloat16)

    def permute(k):
        load(est, ebuf, e_sem, k).wait()
        est_p[k] = jnp.dot(
            perm, ebuf[k].reshape(n, width), preferred_element_type=jnp.float32
        ).astype(jnp.bfloat16)

    cols = nx * fl
    nf = nchunk * FC
    col3 = iota((2 * rows, shots, cols), 2)
    shot_of = col3 // fl * lines + col3 % lines
    own_shot = iota((2 * rows, shots, cols), 1) == shot_of
    f_row, f_col = iota((nf, cols), 0), iota((nf, cols), 1) % fl // lines
    shape3 = (rows, FC, cols)
    same = iota(shape3, 1) == iota(shape3, 2) % fl // lines
    scale = step[0]

    def make_tables():
        size = nz * nf
        row, col = iota((size, 2 * size), 0), iota((size, 2 * size), 1)
        match = row == col // (2 * FC) * FC + col % FC
        to_re = (match & (col // FC % 2 == 0)).astype(jnp.bfloat16)
        to_im = (match & (col // FC % 2 == 1)).astype(jnp.bfloat16)
        nt = tables.shape[1]
        for j, z in enumerate((mz, end)):
            times = z * nt + iota((nt, size), 0)
            phase = times * bins[...] % NT
            angle = 2.0 * math.pi / NT * phase.astype(jnp.float32)
            tables[j] = (
                jnp.dot(jnp.cos(angle).astype(jnp.bfloat16), to_re,
                        preferred_element_type=jnp.float32)
                + jnp.dot((-jnp.sin(angle)).astype(jnp.bfloat16), to_im,
                          preferred_element_type=jnp.float32)
            ).astype(jnp.bfloat16)

    def model(k):
        for d in range(1, nx):
            x_copy(d, k, lax.rem(mx + nx - d, nx)).wait_recv()
        lines_k = down[k].reshape(2 * cols, width)
        m = lax.dot_general(
            est_p[k], lines_k, (((1,), (1,)), ((), ())), preferred_element_type=jnp.float32
        ).reshape(rows, 2, FC, 2 * cols)
        mod_mine[k, 0] = m[:, 0, :, :cols] - m[:, 1, :, cols:]
        mod_mine[k, 1] = m[:, 0, :, cols:] + m[:, 1, :, :cols]
        c_copy(k).start()

    def update(k):
        pick = (f_row == k * FC + f_col).astype(jnp.bfloat16)
        w = jnp.dot(win[...], pick, preferred_element_type=jnp.float32)
        w = jnp.where(own_shot, w.reshape(2 * rows, shots, cols), 0.0).sum(axis=1)
        c_copy(k).wait_recv()
        total_re = mod_mine[k, 0] + mod_other[k, 0]
        total_im = mod_mine[k, 1] + mod_other[k, 1]
        e_re = jnp.where(same, w[:rows, None, :] - total_re, 0.0)
        e_im = jnp.where(same, w[rows:, None, :] - total_im, 0.0)
        e = jnp.stack(
            [jnp.concatenate([e_re, e_im], axis=2), jnp.concatenate([e_im, -e_re], axis=2)], axis=1
        ).reshape(n, 2 * cols).astype(jnp.bfloat16)
        grad = jnp.dot(e, down[k].reshape(2 * cols, width), preferred_element_type=jnp.float32)
        new = (est_p[k].astype(jnp.float32) - scale * (grad * norm)).astype(jnp.bfloat16)
        row = pl.multiple_of(mz * part + k * n, n)
        for b in range(blocks):
            spec[b, pl.ds(row, n)] = new[:, b * BLOCK:(b + 1) * BLOCK]

    def send(k):
        @pl.when(is_end)
        def _():
            to_inner_early(k).start()
            to_inner_late(k).start()

        @pl.when(is_inner)
        def _():
            across_own(k, mz).start()
            out_own(k).start()

    def relay(k):
        @pl.when(is_inner & (k >= 1) & (k <= nchunk))
        def _():
            to_inner_early(k - 1).wait_recv()
            across_end(k - 1, end).start()
            across_own(k - 1, 3 - mz).wait_recv()
            out_opp(k - 1).start()

        @pl.when(is_inner & (k >= 2))
        def _():
            across_end(k - 2, 3 - end).wait_recv()
            out_far(k - 2).start()

    make_down(0)
    make_down(1)
    permute(0)

    def step_of(k, carry):
        @pl.when(k < nchunk - 2)
        def _():
            make_down(k + 2)

        @pl.when(k < nchunk - 1)
        def _():
            permute(k + 1)

        @pl.when(k == 2)
        def _():
            make_tables()

        @pl.when(k < nchunk)
        def _():
            model(k)
            update(k)
            send(k)

        relay(k)
        return carry

    lax.fori_loop(0, nchunk + 2, step_of, 0)

    def traces(b, table, to):
        make_traces(
            spec.at[b].reshape(nz * nchunk, n, BLOCK), table, level, gain, rows, t_group,
            sparse, to,
        )

    def own_block(b):
        at = lax.rem(b, 2)

        @pl.when(b >= 2)
        def _():
            out_copy(obuf.at[at], b - 2, o_sem.at[b - 2]).wait()

        traces(b, tables.at[0], obuf.at[at])
        out_copy(obuf.at[at], b, o_sem.at[b]).start()

    def help_block(b):
        traces(b, tables.at[1], made.at[b - plain])
        trace_copy(b).start()

    def loop(lo, hi, f):
        def one(i, carry):
            f(i)
            return carry

        lax.fori_loop(lo, hi, one, 0)

    @pl.when(is_inner)
    def _():
        loop(0, nchunk, lambda k: to_inner_late(k).wait_recv())

        def hand_on(b):
            block_own(b, mz).start()
            block_end(b, end).start()

        loop(early, blocks, hand_on)

        loop(plain, early, help_block)
        loop(0, early, own_block)

        def rest(b):
            block_own(b, 3 - mz).wait_recv()
            block_end(b, 3 - end).wait_recv()
            help_block(b)
            own_block(b)

        loop(early, blocks, rest)
        loop(blocks - 2, blocks, lambda b: out_copy(obuf.at[lax.rem(b, 2)], b, o_sem.at[b]).wait())

        def drain(k):
            across_own(k, mz).wait_send()
            across_end(k, end).wait_send()
            out_own(k).wait_send()
            out_opp(k).wait_send()
            out_far(k).wait_send()

        loop(0, nchunk, drain)

        def drain_block(b):
            block_own(b, mz).wait_send()
            block_end(b, end).wait_send()

        loop(early, blocks, drain_block)
        loop(plain, blocks, lambda b: trace_copy(b).wait_send())

    @pl.when(is_end)
    def _():
        def arrived(k):
            out_own(k).wait_recv()
            out_opp(k).wait_recv()
            out_far(k).wait_recv()

        loop(0, nchunk, arrived)
        loop(0, plain, own_block)
        loop(plain - 2, plain, lambda b: out_copy(obuf.at[lax.rem(b, 2)], b, o_sem.at[b]).wait())

        def take(b):
            trace_copy(b).wait_recv()
            out_copy(landing(b), b, o_sem.at[b]).start()

        loop(plain, blocks, take)
        loop(plain, blocks, lambda b: out_copy(landing(b), b, o_sem.at[b]).wait())

        def drain(k):
            to_inner_early(k).wait_send()
            to_inner_late(k).wait_send()

        loop(0, nchunk, drain)

    def drain(k):
        for d in range(1, nx):
            x_copy(d, k, mx).wait_send()
        c_copy(k).wait_send()

    loop(0, nchunk, drain)


def relay_body(nx, nz, data, estimate, window_data, wavelet, positions, bins, threshold, step):
    _, nf, lines, width = data.shape
    rows = estimate.shape[2]
    shots = window_data.shape[3]
    nchunk = nf // FC
    norm = 1.0 / math.sqrt(shots * RCV)
    fi, cols = FC * rows, nx * FC * lines
    nt = NT // nz
    blocks = width // BLOCK
    plain, early = 3 * blocks // 8, blocks // 2
    gain, t_group = math.sqrt(RCV / NF), 32

    vmem = pl.BlockSpec(memory_space=pltpu.VMEM)
    smem = pl.BlockSpec(memory_space=pltpu.SMEM)
    hbm = pl.BlockSpec(memory_space=pl.ANY)
    dma = pltpu.SemaphoreType.DMA
    traces = pl.pallas_call(
        partial(
            relay_kernel, nx, nz, nchunk, rows, lines, shots, norm, blocks, plain, early,
            gain, t_group,
        ),
        out_shape=jax.ShapeDtypeStruct((nt * rows, width), jnp.bfloat16),
        in_specs=[hbm, hbm, vmem, smem, smem, vmem, smem, smem],
        out_specs=hbm,
        scratch_shapes=[
            pltpu.VMEM((nchunk, 2, FC * lines, width), jnp.bfloat16),
            pltpu.VMEM((nchunk, 2, FC * rows, width), jnp.bfloat16),
            pltpu.VMEM((nchunk, 2, cols, width), jnp.bfloat16),
            pltpu.VMEM((nchunk, 2 * fi, width), jnp.bfloat16),
            pltpu.VMEM((blocks, nz * nchunk * 2 * fi, BLOCK), jnp.bfloat16),
            pltpu.VMEM((nchunk, 2, rows, FC, cols), jnp.float32),
            pltpu.VMEM((nchunk, 2, rows, FC, cols), jnp.float32),
            pltpu.VMEM((2, nt, 2 * nz * nf), jnp.bfloat16),
            pltpu.VMEM((rows, nt, BLOCK), jnp.bfloat16),
            pltpu.VMEM((blocks - plain, nt * rows, BLOCK), jnp.bfloat16),
            pltpu.VMEM((2, nt * rows, BLOCK), jnp.bfloat16),
            dma((nchunk,)), dma((nchunk,)),
            dma((nx, nchunk)), dma((nx, nchunk)),
            dma((nchunk,)), dma((nchunk,)),
            dma((10, max(nchunk, blocks))), dma((10, max(nchunk, blocks))),
            dma((blocks,)),
        ],
        compiler_params=pltpu.CompilerParams(
            collective_id=1, has_side_effects=True, vmem_limit_bytes=60 << 20
        ),
        name="relay",
    )(
        data.reshape(2, nf * lines, width),
        estimate.reshape(2, nf * rows, width),
        window_data.transpose(0, 2, 3, 1).reshape(2 * rows * shots, nf),
        wavelet,
        positions,
        bins.reshape(1, nz * nf),
        threshold,
        step,
    )
    return traces.reshape(nt, rows, width)


def solution(mesh):
    nz = mesh.shape["freq"]
    return jax.shard_map(
        partial(relay_body if nz == 4 else body, mesh.shape["shot"], nz),
        mesh=mesh,
        in_specs=(
            P(None, "freq", ("grp", "shot"), "rcv"),
            P(None, "freq", ("grp", "shot"), "rcv"),
            P(None, "freq", ("grp", "shot"), None),
            P(None, ("grp", "freq")),
            P(("grp", "shot")),
            P("grp"),
            P("grp"),
            P("grp"),
        ),
        out_specs=P("freq", ("grp", "shot"), "rcv"),
        check_vma=False,
    )
```

```python
from functools import partial
import math

import jax
import jax.numpy as jnp
from jax import lax
from jax.experimental import pallas as pl
from jax.experimental.pallas import tpu as pltpu
from jax.sharding import PartitionSpec as P

NF = 256
RCV = 4096
NT = 1024
FC = 8
GF = 4
PAIR = 2
BLOCK = 256
LAG = 1
MESH = pl.DeviceIdType.MESH


def iota(shape, dim):
    return lax.broadcasted_iota(jnp.int32, shape, dim)


def make_traces(u, table, lv, gain, rows, t_group, sparse, out):
    groups, _, width = u.shape
    part = 2 * FC
    nt = table.shape[0]
    for i in range(rows):
        ui = u[:, i * part:(i + 1) * part, :].reshape(groups * part, width)
        tr = jnp.dot(table[...], ui, preferred_element_type=jnp.float32) * gain
        sparse[i] = (jnp.maximum(tr - lv, 0.0) + jnp.minimum(tr + lv, 0.0)).astype(jnp.bfloat16)
    n = t_group * rows
    dst, src = iota((n, n), 0), iota((n, n), 1)
    perm = (src == (dst % rows) * t_group + dst // rows).astype(jnp.bfloat16)
    for g in range(nt // t_group):
        x = sparse[:, g * t_group:(g + 1) * t_group, :].reshape(n, width)
        out[g * n:(g + 1) * n, :] = jnp.dot(
            perm, x, preferred_element_type=jnp.float32
        ).astype(jnp.bfloat16)


def update_kernel(
    nx, nz, nchunk, rows, lines, norm, blocks, helped, gain, t_group,
    data, est, win, wav, pos, step, level, table, out, given,
    down, est_p, upd, mod_mine, mod_other, ubuf, sparse, made,
    x_send, x_recv, c_send, c_recv, za_send, za_recv, zb_send, zb_recv,
    zc_send, zc_recv, g_send, g_recv, own_sem, ubuf_sem,
):
    mx = lax.axis_index("shot")
    mz = lax.axis_index("freq")
    mc = lax.axis_index("rcv")
    width = data.shape[2]
    fl = FC * lines
    fi = FC * rows

    barrier = pltpu.get_barrier_semaphore()
    for d in range(1, nx):
        pl.semaphore_signal(
            barrier, inc=1, device_id={"shot": lax.rem(mx + d, nx)}, device_id_type=MESH
        )
    pl.semaphore_signal(barrier, inc=1, device_id={"rcv": 1 - mc}, device_id_type=MESH)

    @pl.when(mz > 0)
    def _():
        pl.semaphore_signal(barrier, inc=1, device_id={"freq": mz - 1}, device_id_type=MESH)

    @pl.when(mz < nz - 1)
    def _():
        pl.semaphore_signal(barrier, inc=1, device_id={"freq": mz + 1}, device_id_type=MESH)

    ends = (mz > 0).astype(jnp.int32) + (mz < nz - 1).astype(jnp.int32)
    pl.semaphore_wait(barrier, nx + ends)

    def x_copy(d, k):
        piece = down.at[k, :, pl.ds(mx * fl, fl)]
        return pltpu.make_async_remote_copy(
            src_ref=piece, dst_ref=piece,
            send_sem=x_send.at[d, k], recv_sem=x_recv.at[d, k],
            device_id={"shot": lax.rem(mx + d, nx)}, device_id_type=MESH,
        )

    def c_copy(k):
        return pltpu.make_async_remote_copy(
            src_ref=mod_mine.at[k], dst_ref=mod_other.at[k],
            send_sem=c_send.at[k], recv_sem=c_recv.at[k],
            device_id={"rcv": 1 - mc}, device_id_type=MESH,
        )

    def w_of(way):
        return 0 if way > 0 else 1

    def last(z, way):
        return z == (nz - 1 if way > 0 else 0)

    def a_copy(src, slot, k, way):
        return pltpu.make_async_remote_copy(
            src_ref=src, dst_ref=out.at[pl.ds(0, helped), slot, k],
            send_sem=za_send.at[w_of(way), slot, k], recv_sem=za_recv.at[w_of(way), slot, k],
            device_id={"freq": mz + way}, device_id_type=MESH,
        )

    def b_copy(src, slot, k, way):
        return pltpu.make_async_remote_copy(
            src_ref=src, dst_ref=out.at[pl.ds(helped, blocks - helped), slot, k],
            send_sem=zb_send.at[w_of(way), slot, k], recv_sem=zb_recv.at[w_of(way), slot, k],
            device_id={"freq": mz + way}, device_id_type=MESH,
        )

    def block_copy(slot, b, way):
        piece = out.at[b, slot]
        return pltpu.make_async_remote_copy(
            src_ref=piece, dst_ref=piece,
            send_sem=zc_send.at[w_of(way), slot, b], recv_sem=zc_recv.at[w_of(way), slot, b],
            device_id={"freq": mz + way}, device_id_type=MESH,
        )

    def given_copy(b, way):
        return pltpu.make_async_remote_copy(
            src_ref=made.at[b], dst_ref=given.at[b],
            send_sem=g_send.at[b], recv_sem=g_recv.at[b],
            device_id={"freq": mz + way}, device_id_type=MESH,
        )

    a_own = lambda k: upd.at[k, pl.ds(0, helped)]
    b_own = lambda k: upd.at[k, pl.ds(helped, blocks - helped)]
    a_out = lambda slot, k: out.at[pl.ds(0, helped), slot, k]
    b_out = lambda slot, k: out.at[pl.ds(helped, blocks - helped), slot, k]

    def own_copy(k):
        return pltpu.make_async_copy(upd.at[k], out.at[:, mz, k], own_sem.at[k])

    column = mc * width + iota((lines, width), 1)
    select = (column == pos[:, :]).astype(jnp.float32)

    def make_down(k, carry):
        for c in range(2):
            parts = []
            lines_k = data[c, pl.ds(pl.multiple_of(k * fl, fl), fl)].astype(jnp.float32)
            for f in range(FC):
                w = wav[c, k * FC + f]
                parts.append(w * select - lines_k[f * lines:(f + 1) * lines])
            down[k, c, pl.ds(pl.multiple_of(mx * fl, fl), fl)] = jnp.concatenate(
                parts, axis=0
            ).astype(jnp.bfloat16)
        for d in range(1, nx):
            x_copy(d, k).start()
        return carry

    lax.fori_loop(0, nchunk, make_down, 0)

    n = 2 * fi
    dst, src = iota((n, n), 0), iota((n, n), 1)
    want = (dst // FC % 2) * fi + (dst % FC) * rows + dst // (2 * FC)
    perm = (src == want).astype(jnp.bfloat16)

    def chunk_of(ref, k):
        part = pl.ds(pl.multiple_of(k * fi, fi), fi)
        return jnp.concatenate([ref[0, part], ref[1, part]], axis=0)

    def permute(k, carry):
        est_p[k] = jnp.dot(
            perm, chunk_of(est, k), preferred_element_type=jnp.float32
        ).astype(jnp.bfloat16)
        return carry

    lax.fori_loop(0, nchunk, permute, 0)

    cols = nx * fl
    shots = win.shape[2]
    s_row, s_col = iota((shots, cols), 0), iota((shots, cols), 1)
    spread = (s_row == (s_col // fl) * lines + s_col % lines).astype(jnp.bfloat16)
    shape3 = (rows, FC, cols)
    same = iota(shape3, 1) == iota(shape3, 2) % fl // lines
    scale = step[0]

    def model(k):
        for d in range(1, nx):
            here = down.at[k, :, pl.ds(lax.rem(mx + nx - d, nx) * fl, fl)]
            pltpu.make_async_remote_copy(
                src_ref=here, dst_ref=here,
                send_sem=x_send.at[d, k], recv_sem=x_recv.at[d, k],
                device_id={"shot": lax.rem(mx + d, nx)}, device_id_type=MESH,
            ).wait_recv()
        lines_k = down[k].reshape(2 * cols, width)
        m = lax.dot_general(
            est_p[k], lines_k, (((1,), (1,)), ((), ())), preferred_element_type=jnp.float32
        ).reshape(rows, 2, FC, 2 * cols)
        mod_mine[k, 0] = m[:, 0, :, :cols] - m[:, 1, :, cols:]
        mod_mine[k, 1] = m[:, 0, :, cols:] + m[:, 1, :, :cols]
        c_copy(k).start()

    def update(k):
        c_copy(k).wait_recv()
        total_re = mod_mine[k, 0] + mod_other[k, 0]
        total_im = mod_mine[k, 1] + mod_other[k, 1]
        w = jnp.dot(perm, chunk_of(win, k), preferred_element_type=jnp.float32).astype(jnp.bfloat16)
        w = jnp.dot(w, spread, preferred_element_type=jnp.float32).reshape(rows, 2, FC, cols)
        e_re = jnp.where(same, w[:, 0] - total_re, 0.0)
        e_im = jnp.where(same, w[:, 1] - total_im, 0.0)
        e = jnp.stack(
            [jnp.concatenate([e_re, e_im], axis=2), jnp.concatenate([e_im, -e_re], axis=2)], axis=1
        ).reshape(n, 2 * cols).astype(jnp.bfloat16)
        grad = jnp.dot(e, down[k].reshape(2 * cols, width), preferred_element_type=jnp.float32)
        new = (est_p[k].astype(jnp.float32) - scale * (grad * norm)).astype(jnp.bfloat16)
        for b in range(blocks):
            upd[k, b] = new[:, b * BLOCK:(b + 1) * BLOCK]
        own_copy(k).start()
        for way in (1, -1):
            @pl.when(jnp.logical_not(last(mz, way)))
            def _():
                b_copy(b_own(k), mz, k, way).start()

                if helped:
                    @pl.when(jnp.logical_not(last(mz + way, way)))
                    def _():
                        a_copy(a_own(k), mz, k, way).start()

    def near(k):
        for way in (1, -1):
            slot = mz - way

            @pl.when((slot >= 0) & (slot < nz))
            def _():
                b_copy(b_out(slot, k), slot, k, way).wait_recv()

                if helped:
                    @pl.when(jnp.logical_not(last(mz, way)))
                    def _():
                        a_copy(a_out(slot, k), slot, k, way).wait_recv()

                @pl.when(last(mz + way, way))
                def _():
                    b_copy(b_out(slot, k), slot, k, way).start()

    def step_of(k, carry):
        @pl.when(k < nchunk)
        def _():
            model(k)
            update(k)

        @pl.when(k >= LAG)
        def _():
            near(k - LAG)

        return carry

    lax.fori_loop(0, nchunk + LAG, step_of, 0)

    def own_done(k, carry):
        own_copy(k).wait()
        return carry

    lax.fori_loop(0, nchunk, own_done, 0)

    def hand_on(b, carry):
        for way in (1, -1):
            slot = mz - way
            inside = (slot >= 0) & (slot < nz)
            nxt = mz + way

            @pl.when(inside & (nxt > 0) & (nxt < nz - 1))
            def _():
                block_copy(slot, b, way).start()

        return carry

    lax.fori_loop(0, blocks, hand_on, 0)

    def far(h, carry):
        def one(b, carry):
            for way in (1, -1):
                slot = mz - way * h
                nxt = mz + way
                inside = (slot >= 0) & (slot < nz)
                at_end = last(mz, way)

                @pl.when(inside & jnp.logical_not(at_end))
                def _():
                    block_copy(slot, b, way).wait_recv()

                    @pl.when(jnp.logical_not(last(nxt, way)) | (b >= helped))
                    def _():
                        block_copy(slot, b, way).start()

                    if helped:
                        @pl.when(last(nxt, way) & (b < helped) & last(slot, -way))
                        def _():
                            load = pltpu.make_async_copy(out.at[b], ubuf, ubuf_sem)
                            load.start()
                            load.wait()
                            make_traces(
                                ubuf.reshape(nz * nchunk, ubuf.shape[2], BLOCK), table, level[0],
                                gain, rows, t_group, sparse, made.at[b],
                            )
                            given_copy(b, way).start()

                @pl.when(inside & at_end & (b >= helped))
                def _():
                    if not near_by:
                        block_copy(slot, b, way).wait_recv()

            return carry

        near_by = isinstance(h, int)
        return lax.fori_loop(0, blocks, one, carry)

    def end_chunk(k, carry):
        for way in (1, -1):
            slot = mz - 2 * way

            @pl.when((slot >= 0) & (slot < nz) & last(mz, way))
            def _():
                b_copy(b_out(slot, k), slot, k, way).wait_recv()

        return carry

    if nz > 2:
        lax.fori_loop(0, nchunk, end_chunk, 0)
        far(2, 0)
    lax.fori_loop(3, nz, far, 0)

    if helped:
        def take(b, carry):
            for way in (1, -1):
                @pl.when(last(mz, way))
                def _():
                    given_copy(b, way).wait_recv()

                @pl.when(last(mz + way, way))
                def _():
                    given_copy(b, way).wait_send()

            return carry

        lax.fori_loop(0, helped, take, 0)

    def drain(k, carry):
        for d in range(1, nx):
            x_copy(d, k).wait_send()
        c_copy(k).wait_send()
        for way in (1, -1):
            nxt = mz + way

            @pl.when(jnp.logical_not(last(mz, way)))
            def _():
                b_copy(b_own(k), mz, k, way).wait_send()

                if helped:
                    @pl.when(jnp.logical_not(last(nxt, way)))
                    def _():
                        a_copy(a_own(k), mz, k, way).wait_send()

            slot = mz - way

            @pl.when((slot >= 0) & (slot < nz) & last(nxt, way))
            def _():
                b_copy(b_own(k), slot, k, way).wait_send()

        return carry

    lax.fori_loop(0, nchunk, drain, 0)

    def drain_far(h, carry):
        def one(b, carry):
            for way in (1, -1):
                slot = mz - way * h
                nxt = mz + way
                inside = (slot >= 0) & (slot < nz) & (nxt >= 0) & (nxt < nz)
                to_end = last(nxt, way)

                @pl.when(inside & (jnp.logical_not(to_end) | ((b >= helped) & (h > 1))))
                def _():
                    block_copy(slot, b, way).wait_send()

            return carry

        return lax.fori_loop(0, blocks, one, carry)

    lax.fori_loop(1, nz, drain_far, 0)


def trace_kernel(rows, t_group, gain, helped, level, taken, table, u, given, out, sparse):
    ready = (pl.program_id(0) < helped) & (taken[0] > 0)

    @pl.when(ready)
    def _():
        out[...] = given[...]

    @pl.when(jnp.logical_not(ready))
    def _():
        make_traces(u, table, level[0], gain, rows, t_group, sparse, out)


def body(nx, nz, data, estimate, window_data, wavelet, positions, bins, threshold, step):
    _, nf, lines, width = data.shape
    rows = estimate.shape[2]
    shots = window_data.shape[3]
    nchunk = nf // FC
    norm = 1.0 / math.sqrt(shots * RCV)
    fi, cols = FC * rows, nx * FC * lines
    mz = lax.axis_index("freq")
    nt = NT // nz
    blocks, groups = width // BLOCK, nz * nchunk
    helped = 3 * blocks // 8 if nz >= 4 else 0
    held = max(helped, 1)
    gain, t_group = math.sqrt(RCV / NF), 32
    level = threshold.astype(jnp.float32) / 64.0

    def table_of(z):
        times = z * nt + lax.iota(jnp.int32, nt)
        phase = times[:, None] * bins[None, :] % NT
        angle = 2.0 * math.pi / NT * phase.astype(jnp.float32)
        table = jnp.stack([jnp.cos(angle), -jnp.sin(angle)], axis=1).astype(jnp.bfloat16)
        table = table.reshape(nt, 2, groups, FC).transpose(0, 2, 1, 3)
        return table.reshape(nt, 2 * nz * nf)

    vmem = pl.BlockSpec(memory_space=pltpu.VMEM)
    smem = pl.BlockSpec(memory_space=pltpu.SMEM)
    hbm = pl.BlockSpec(memory_space=pl.ANY)
    dma = pltpu.SemaphoreType.DMA
    spectra, given = pl.pallas_call(
        partial(
            update_kernel, nx, nz, nchunk, rows, lines, norm, blocks, helped, gain, t_group
        ),
        out_shape=(
            jax.ShapeDtypeStruct((blocks, nz, nchunk, 2 * fi, BLOCK), jnp.bfloat16),
            jax.ShapeDtypeStruct((held, nt * rows, BLOCK), jnp.bfloat16),
        ),
        in_specs=[vmem, vmem, vmem, smem, vmem, smem, smem, vmem],
        out_specs=(hbm, hbm),
        scratch_shapes=[
            pltpu.VMEM((nchunk, 2, cols, width), jnp.bfloat16),
            pltpu.VMEM((nchunk, 2 * fi, width), jnp.bfloat16),
            pltpu.VMEM((nchunk, blocks, 2 * fi, BLOCK), jnp.bfloat16),
            pltpu.VMEM((nchunk, 2, rows, FC, cols), jnp.float32),
            pltpu.VMEM((nchunk, 2, rows, FC, cols), jnp.float32),
            pltpu.VMEM((nz, nchunk, 2 * fi, BLOCK), jnp.bfloat16),
            pltpu.VMEM((rows, nt, BLOCK), jnp.bfloat16),
            pltpu.VMEM((held, nt * rows, BLOCK), jnp.bfloat16),
            dma((nx, nchunk)), dma((nx, nchunk)),
            dma((nchunk,)), dma((nchunk,)),
            dma((2, nz, nchunk)), dma((2, nz, nchunk)),
            dma((2, nz, nchunk)), dma((2, nz, nchunk)),
            dma((2, nz, blocks)), dma((2, nz, blocks)),
            dma((held,)), dma((held,)),
            dma((nchunk,)), dma,
        ],
        compiler_params=pltpu.CompilerParams(
            collective_id=0, has_side_effects=True, vmem_limit_bytes=58 << 20
        ),
        name="update",
    )(
        data.reshape(2, nf * lines, width),
        estimate.reshape(2, nf * rows, width),
        window_data.reshape(2, nf * rows, shots),
        wavelet,
        positions[:, None],
        step,
        level,
        table_of(jnp.where(mz < nz // 2, 0, nz - 1)),
    )
    taken = ((mz == 0) | (mz == nz - 1)).astype(jnp.int32)[None]
    traces = pl.pallas_call(
        partial(trace_kernel, rows, t_group, gain, helped),
        out_shape=jax.ShapeDtypeStruct((nt * rows, width), jnp.bfloat16),
        grid=(blocks,),
        in_specs=[
            smem,
            smem,
            pl.BlockSpec((nt, 2 * nz * nf), lambda j: (0, 0)),
            pl.BlockSpec((None, groups, 2 * fi, BLOCK), lambda j: (j, 0, 0, 0)),
            pl.BlockSpec(
                (None, nt * rows, BLOCK), lambda j: (jnp.minimum(j, held - 1), 0, 0)
            ),
        ],
        out_specs=pl.BlockSpec((nt * rows, BLOCK), lambda j: (0, j)),
        scratch_shapes=[pltpu.VMEM((rows, nt, BLOCK), jnp.bfloat16)],
        compiler_params=pltpu.CompilerParams(vmem_limit_bytes=60 << 20),
        name="traces",
    )(level, taken, table_of(mz), spectra.reshape(blocks, groups, 2 * fi, BLOCK), given)
    return traces.reshape(nt, rows, width)


def make_pairs(u, table, lv, gain, rows, t_group, sparse, out):
    groups, _, width = u.shape
    part = 2 * GF * PAIR
    nt = table.shape[0] // PAIR
    for p in range(rows // PAIR):
        up = u[:, p * part:(p + 1) * part, :].reshape(groups * part, width)
        tr = jnp.dot(table[...], up, preferred_element_type=jnp.float32) * gain
        sparse[p] = (jnp.maximum(tr - lv, 0.0) + jnp.minimum(tr + lv, 0.0)).astype(jnp.bfloat16)
    lined = sparse.reshape(rows, nt, width)
    n = t_group * rows
    dst, src = iota((n, n), 0), iota((n, n), 1)
    perm = (src == (dst % rows) * t_group + dst // rows).astype(jnp.bfloat16)
    for g in range(nt // t_group):
        x = lined[:, g * t_group:(g + 1) * t_group, :].reshape(n, width)
        out[g * n:(g + 1) * n, :] = jnp.dot(
            perm, x, preferred_element_type=jnp.float32
        ).astype(jnp.bfloat16)


def relay_kernel(
    nx, nz, nchunk, rows, lines, shots, norm, blocks, plain, early, gain, t_group,
    data, est, win, wav, pos, bins, thr, step, out,
    dbuf, ebuf, down, spec, mod_mine, mod_other, tables, sparse, made,
    d_sem, e_sem, x_send, x_recv, c_send, c_recv, z_send, z_recv,
):
    mx = lax.axis_index("shot")
    mz = lax.axis_index("freq")
    mc = lax.axis_index("rcv")
    width = data.shape[2]
    fl = GF * lines
    fi = GF * rows
    n = 2 * fi
    part = nchunk * n
    end = jnp.where(mz < 2, 0, 3)
    inner = jnp.where(mz < 2, 1, 2)
    is_end = mz == end
    is_inner = jnp.logical_not(is_end)
    level = thr[0].astype(jnp.float32) / 64.0

    def load(ref, buf, sem, k):
        return pltpu.make_async_copy(
            ref.at[:, pl.ds(pl.multiple_of(k * fl, fl), fl)], buf.at[k], sem.at[k]
        )

    def load_all(k, carry):
        load(data, dbuf, d_sem, k).start()
        load(est, ebuf, e_sem, k).start()
        return carry

    lax.fori_loop(0, nchunk, load_all, 0)

    barrier = pltpu.get_barrier_semaphore()
    for d in range(1, nx):
        pl.semaphore_signal(
            barrier, inc=1, device_id={"shot": lax.rem(mx + d, nx)}, device_id_type=MESH
        )
    pl.semaphore_signal(barrier, inc=1, device_id={"rcv": 1 - mc}, device_id_type=MESH)
    pl.semaphore_signal(
        barrier, inc=1, device_id={"freq": jnp.where(is_end, inner, end)}, device_id_type=MESH
    )

    @pl.when(is_inner)
    def _():
        pl.semaphore_signal(barrier, inc=1, device_id={"freq": 3 - mz}, device_id_type=MESH)

    pl.semaphore_wait(barrier, nx + 1 + is_inner.astype(jnp.int32))

    def x_copy(d, k, piece):
        here = down.at[k, :, pl.ds(piece * fl, fl)]
        return pltpu.make_async_remote_copy(
            src_ref=here, dst_ref=here,
            send_sem=x_send.at[d, k], recv_sem=x_recv.at[d, k],
            device_id={"shot": lax.rem(mx + d, nx)}, device_id_type=MESH,
        )

    def c_copy(k):
        return pltpu.make_async_remote_copy(
            src_ref=mod_mine.at[k], dst_ref=mod_other.at[k],
            send_sem=c_send.at[k], recv_sem=c_recv.at[k],
            device_id={"rcv": 1 - mc}, device_id_type=MESH,
        )

    def z_copy(kind, at, here, there, to):
        return pltpu.make_async_remote_copy(
            src_ref=here, dst_ref=there,
            send_sem=z_send.at[kind, at], recv_sem=z_recv.at[kind, at],
            device_id={"freq": to}, device_id_type=MESH,
        )

    def chunk_copy(kind, slot, k, lo, count, to):
        row = pl.multiple_of(slot * part + k * n, n)
        here = spec.at[pl.ds(lo, count), pl.ds(row, n)]
        return z_copy(kind, k, here, here, to)

    def block_copy(kind, slot, b, to):
        here = spec.at[b, pl.ds(pl.multiple_of(slot * part, part), part)]
        return z_copy(kind, b, here, here, to)

    late = blocks - early
    to_inner_early = lambda k: chunk_copy(0, end, k, 0, early, inner)
    to_inner_late = lambda k: chunk_copy(1, end, k, early, late, inner)
    across_own = lambda k, own: chunk_copy(2, own, k, 0, early, 3 - mz)
    across_end = lambda k, of: chunk_copy(3, of, k, 0, early, 3 - mz)
    out_own = lambda k: chunk_copy(4, inner, k, 0, plain, end)
    out_opp = lambda k: chunk_copy(5, 3 - inner, k, 0, plain, end)
    out_far = lambda k: chunk_copy(6, 3 - end, k, 0, plain, end)
    block_own = lambda b, own: block_copy(7, own, b, 3 - mz)
    block_end = lambda b, of: block_copy(8, of, b, 3 - mz)
    trace_copy = lambda b: z_copy(9, b, made.at[b - plain], out.at[b], end)

    line, column = iota((lines, width), 0), mc * width + iota((lines, width), 1)
    select = jnp.zeros((lines, width), jnp.float32)
    for s in range(lines):
        select = jnp.where((line == s) & (column == pos[s]), 1.0, select)

    def make_down(k):
        load(data, dbuf, d_sem, k).wait()
        for c in range(2):
            parts = []
            lines_k = dbuf[k, c].astype(jnp.float32)
            for f in range(GF):
                w = wav[c, k * GF + f]
                parts.append(w * select - lines_k[f * lines:(f + 1) * lines])
            down[k, c, pl.ds(pl.multiple_of(mx * fl, fl), fl)] = jnp.concatenate(
                parts, axis=0
            ).astype(jnp.bfloat16)
        for d in range(1, nx):
            x_copy(d, k, mx).start()

    dst, src = iota((n, n), 0), iota((n, n), 1)
    want = (dst // GF % 2) * fi + (dst % GF) * rows + dst // (2 * GF)
    perm = (src == want).astype(jnp.bfloat16)

    cols = nx * fl
    nf = nchunk * GF
    col3 = iota((2 * rows, shots, cols), 2)
    shot_of = col3 // fl * lines + col3 % lines
    own_shot = iota((2 * rows, shots, cols), 1) == shot_of
    f_row, f_col = iota((nf, cols), 0), iota((nf, cols), 1) % fl // lines
    shape3 = (GF, rows, cols)
    same = iota(shape3, 0) == iota(shape3, 2) % fl // lines
    scale = step[0]

    def make_table(j, z):
        size, nt = nz * nf, sparse.shape[1] // PAIR
        wide = 2 * PAIR * size
        row, col = iota((size, wide), 0), iota((size, wide), 1)
        match = row == col // (2 * GF * PAIR) * GF + col % GF
        to_re = (match & (col // GF % 2 == 0)).astype(jnp.bfloat16)
        to_im = (match & (col // GF % 2 == 1)).astype(jnp.bfloat16)
        times = z * nt + iota((nt, size), 0)
        phase = times * bins[...] % NT
        angle = 2.0 * math.pi / NT * phase.astype(jnp.float32)
        full = jnp.dot(
            jnp.cos(angle).astype(jnp.bfloat16), to_re, preferred_element_type=jnp.float32
        ) + jnp.dot(
            (-jnp.sin(angle)).astype(jnp.bfloat16), to_im, preferred_element_type=jnp.float32
        )
        member = iota((nt, wide), 1) // (2 * GF) % PAIR
        for a in range(PAIR):
            tables[j, a * nt:(a + 1) * nt] = jnp.where(member == a, full, 0.0).astype(
                jnp.bfloat16
            )

    def spectra_of(k):
        return ebuf[k].reshape(n, width)

    def model(k):
        load(est, ebuf, e_sem, k).wait()
        for d in range(1, nx):
            x_copy(d, k, lax.rem(mx + nx - d, nx)).wait_recv()
        m_re, m_im = [
            lax.dot_general(
                spectra_of(k), down[k, c], (((1,), (1,)), ((), ())),
                preferred_element_type=jnp.float32,
            )
            for c in range(2)
        ]
        mod_mine[k, 0] = m_re[:fi] - m_im[fi:]
        mod_mine[k, 1] = m_im[:fi] + m_re[fi:]
        c_copy(k).start()

    def update(k):
        pick = (f_row == k * GF + f_col).astype(jnp.bfloat16)
        w = jnp.dot(win[...], pick, preferred_element_type=jnp.float32)
        w = jnp.where(own_shot, w.reshape(2 * rows, shots, cols), 0.0).sum(axis=1)
        c_copy(k).wait_recv()
        total_re = (mod_mine[k, 0] + mod_other[k, 0]).reshape(shape3)
        total_im = (mod_mine[k, 1] + mod_other[k, 1]).reshape(shape3)
        e_re = jnp.where(same, w[None, :rows] - total_re, 0.0).reshape(fi, cols)
        e_im = jnp.where(same, w[None, rows:] - total_im, 0.0).reshape(fi, cols)
        e = jnp.concatenate(
            [jnp.concatenate([e_re, e_im], axis=1), jnp.concatenate([e_im, -e_re], axis=1)], axis=0
        ).astype(jnp.bfloat16)
        grad = jnp.dot(e, down[k].reshape(2 * cols, width), preferred_element_type=jnp.float32)
        new = (spectra_of(k).astype(jnp.float32) - scale * (grad * norm)).astype(jnp.bfloat16)
        new = jnp.dot(perm, new, preferred_element_type=jnp.float32).astype(jnp.bfloat16)
        row = pl.multiple_of(mz * part + k * n, n)
        for b in range(blocks):
            spec[b, pl.ds(row, n)] = new[:, b * BLOCK:(b + 1) * BLOCK]

    def send(k):
        @pl.when(is_end)
        def _():
            to_inner_early(k).start()
            to_inner_late(k).start()

        @pl.when(is_inner)
        def _():
            across_own(k, mz).start()
            out_own(k).start()

    def relay(k):
        @pl.when(is_inner & (k >= 1) & (k <= nchunk))
        def _():
            to_inner_early(k - 1).wait_recv()
            across_end(k - 1, end).start()
            across_own(k - 1, 3 - mz).wait_recv()
            out_opp(k - 1).start()

        @pl.when(is_inner & (k >= 2))
        def _():
            across_end(k - 2, 3 - end).wait_recv()
            out_far(k - 2).start()

    make_down(0)
    make_down(1)

    def step_of(k, carry):
        @pl.when(k < nchunk - 2)
        def _():
            make_down(k + 2)

        for j, z in enumerate((mz, end)):
            @pl.when(k == nchunk // 4 * (j + 1))
            def _():
                make_table(j, z)

        @pl.when(k < nchunk)
        def _():
            model(k)
            update(k)
            send(k)

        relay(k)
        return carry

    lax.fori_loop(0, nchunk + 2, step_of, 0)

    def traces(b, table, to):
        make_pairs(
            spec.at[b].reshape(nz * nchunk, n, BLOCK), table, level, gain, rows, t_group,
            sparse, to,
        )

    def own_block(b):
        traces(b, tables.at[0], out.at[b])

    def help_block(b):
        traces(b, tables.at[1], made.at[b - plain])
        trace_copy(b).start()

    def loop(lo, hi, f):
        def one(i, carry):
            f(i)
            return carry

        lax.fori_loop(lo, hi, one, 0)

    @pl.when(is_inner)
    def _():
        loop(0, nchunk, lambda k: to_inner_late(k).wait_recv())

        def hand_on(b):
            block_own(b, mz).start()
            block_end(b, end).start()

        loop(early, blocks, hand_on)

        loop(plain, early, help_block)
        loop(0, early, own_block)

        def rest(b):
            block_own(b, 3 - mz).wait_recv()
            block_end(b, 3 - end).wait_recv()
            help_block(b)
            own_block(b)

        loop(early, blocks, rest)

        def drain(k):
            across_own(k, mz).wait_send()
            across_end(k, end).wait_send()
            out_own(k).wait_send()
            out_opp(k).wait_send()
            out_far(k).wait_send()

        loop(0, nchunk, drain)

        def drain_block(b):
            block_own(b, mz).wait_send()
            block_end(b, end).wait_send()

        loop(early, blocks, drain_block)
        loop(plain, blocks, lambda b: trace_copy(b).wait_send())

    @pl.when(is_end)
    def _():
        def arrived(k):
            out_own(k).wait_recv()
            out_opp(k).wait_recv()
            out_far(k).wait_recv()

        loop(0, nchunk, arrived)
        loop(0, plain, own_block)
        loop(plain, blocks, lambda b: trace_copy(b).wait_recv())

        def drain(k):
            to_inner_early(k).wait_send()
            to_inner_late(k).wait_send()

        loop(0, nchunk, drain)

    def drain(k):
        for d in range(1, nx):
            x_copy(d, k, mx).wait_send()
        c_copy(k).wait_send()

    loop(0, nchunk, drain)


def place_kernel(traces, out, sem):
    copies = [
        pltpu.make_async_copy(
            traces.at[b], out.at[:, pl.ds(b * BLOCK, BLOCK)], sem.at[b]
        )
        for b in range(traces.shape[0])
    ]
    for copy in copies:
        copy.start()
    for copy in copies:
        copy.wait()


def relay_body(nx, nz, data, estimate, window_data, wavelet, positions, bins, threshold, step):
    _, nf, lines, width = data.shape
    rows = estimate.shape[2]
    shots = window_data.shape[3]
    nchunk = nf // GF
    norm = 1.0 / math.sqrt(shots * RCV)
    fi, cols = GF * rows, nx * GF * lines
    size = nz * nf
    nt = NT // nz
    blocks = width // BLOCK
    plain, early = 3 * blocks // 8, blocks // 2
    gain, t_group = math.sqrt(RCV / NF), 32

    vmem = pl.BlockSpec(memory_space=pltpu.VMEM)
    smem = pl.BlockSpec(memory_space=pltpu.SMEM)
    hbm = pl.BlockSpec(memory_space=pl.ANY)
    dma = pltpu.SemaphoreType.DMA
    traces = pl.pallas_call(
        partial(
            relay_kernel, nx, nz, nchunk, rows, lines, shots, norm, blocks, plain, early,
            gain, t_group,
        ),
        out_shape=pltpu.VMEM((blocks, nt * rows, BLOCK), jnp.bfloat16),
        in_specs=[hbm, hbm, vmem, smem, smem, vmem, smem, smem],
        out_specs=vmem,
        scratch_shapes=[
            pltpu.VMEM((nchunk, 2, GF * lines, width), jnp.bfloat16),
            pltpu.VMEM((nchunk, 2, fi, width), jnp.bfloat16),
            pltpu.VMEM((nchunk, 2, cols, width), jnp.bfloat16),
            pltpu.VMEM((blocks, nz * nchunk * 2 * fi, BLOCK), jnp.bfloat16),
            pltpu.VMEM((nchunk, 2, fi, cols), jnp.float32),
            pltpu.VMEM((nchunk, 2, fi, cols), jnp.float32),
            pltpu.VMEM((2, PAIR * nt, 2 * PAIR * size), jnp.bfloat16),
            pltpu.VMEM((rows // PAIR, PAIR * nt, BLOCK), jnp.bfloat16),
            pltpu.VMEM((blocks - plain, nt * rows, BLOCK), jnp.bfloat16),
            dma((nchunk,)), dma((nchunk,)),
            dma((nx, nchunk)), dma((nx, nchunk)),
            dma((nchunk,)), dma((nchunk,)),
            dma((10, max(nchunk, blocks))), dma((10, max(nchunk, blocks))),
        ],
        compiler_params=pltpu.CompilerParams(
            collective_id=1, has_side_effects=True, vmem_limit_bytes=48 << 20
        ),
        name="relay",
    )(
        data.reshape(2, nf * lines, width),
        estimate.reshape(2, nf * rows, width),
        window_data.transpose(0, 2, 3, 1).reshape(2 * rows * shots, nf),
        wavelet,
        positions,
        bins.reshape(1, size),
        threshold,
        step,
    )
    placed = pl.pallas_call(
        place_kernel,
        out_shape=jax.ShapeDtypeStruct((nt * rows, width), jnp.bfloat16),
        in_specs=[vmem],
        out_specs=hbm,
        scratch_shapes=[dma((blocks,))],
        compiler_params=pltpu.CompilerParams(vmem_limit_bytes=4 << 20),
        name="place",
    )(traces)
    return placed.reshape(nt, rows, width)


def solution(mesh):
    nz = mesh.shape["freq"]
    return jax.shard_map(
        partial(relay_body if nz == 4 else body, mesh.shape["shot"], nz),
        mesh=mesh,
        in_specs=(
            P(None, "freq", ("grp", "shot"), "rcv"),
            P(None, "freq", ("grp", "shot"), "rcv"),
            P(None, "freq", ("grp", "shot"), None),
            P(None, ("grp", "freq")),
            P(("grp", "shot")),
            P("grp"),
            P("grp"),
            P("grp"),
        ),
        out_specs=P("freq", ("grp", "shot"), "rcv"),
        check_vma=False,
    )
```

```python
from functools import partial
import math

import jax
import jax.numpy as jnp
from jax import lax
from jax.experimental import pallas as pl
from jax.experimental.pallas import tpu as pltpu
from jax.sharding import PartitionSpec as P

NF = 256
RCV = 4096
NT = 1024
FC = 8
GF = 4
PAIR = 2
TILE = 128
PLAIN = 5
BLOCK = 256
LAG = 1
MESH = pl.DeviceIdType.MESH


def iota(shape, dim):
    return lax.broadcasted_iota(jnp.int32, shape, dim)


def make_traces(u, table, lv, gain, rows, t_group, sparse, out):
    groups, _, width = u.shape
    part = 2 * FC
    nt = table.shape[0]
    for i in range(rows):
        ui = u[:, i * part:(i + 1) * part, :].reshape(groups * part, width)
        tr = jnp.dot(table[...], ui, preferred_element_type=jnp.float32) * gain
        sparse[i] = (jnp.maximum(tr - lv, 0.0) + jnp.minimum(tr + lv, 0.0)).astype(jnp.bfloat16)
    n = t_group * rows
    dst, src = iota((n, n), 0), iota((n, n), 1)
    perm = (src == (dst % rows) * t_group + dst // rows).astype(jnp.bfloat16)
    for g in range(nt // t_group):
        x = sparse[:, g * t_group:(g + 1) * t_group, :].reshape(n, width)
        out[g * n:(g + 1) * n, :] = jnp.dot(
            perm, x, preferred_element_type=jnp.float32
        ).astype(jnp.bfloat16)


def update_kernel(
    nx, nz, nchunk, rows, lines, norm, blocks, helped, gain, t_group,
    data, est, win, wav, pos, step, level, table, out, given,
    down, est_p, upd, mod_mine, mod_other, ubuf, sparse, made,
    x_send, x_recv, c_send, c_recv, za_send, za_recv, zb_send, zb_recv,
    zc_send, zc_recv, g_send, g_recv, own_sem, ubuf_sem,
):
    mx = lax.axis_index("shot")
    mz = lax.axis_index("freq")
    mc = lax.axis_index("rcv")
    width = data.shape[2]
    fl = FC * lines
    fi = FC * rows

    barrier = pltpu.get_barrier_semaphore()
    for d in range(1, nx):
        pl.semaphore_signal(
            barrier, inc=1, device_id={"shot": lax.rem(mx + d, nx)}, device_id_type=MESH
        )
    pl.semaphore_signal(barrier, inc=1, device_id={"rcv": 1 - mc}, device_id_type=MESH)

    @pl.when(mz > 0)
    def _():
        pl.semaphore_signal(barrier, inc=1, device_id={"freq": mz - 1}, device_id_type=MESH)

    @pl.when(mz < nz - 1)
    def _():
        pl.semaphore_signal(barrier, inc=1, device_id={"freq": mz + 1}, device_id_type=MESH)

    ends = (mz > 0).astype(jnp.int32) + (mz < nz - 1).astype(jnp.int32)
    pl.semaphore_wait(barrier, nx + ends)

    def x_copy(d, k):
        piece = down.at[k, :, pl.ds(mx * fl, fl)]
        return pltpu.make_async_remote_copy(
            src_ref=piece, dst_ref=piece,
            send_sem=x_send.at[d, k], recv_sem=x_recv.at[d, k],
            device_id={"shot": lax.rem(mx + d, nx)}, device_id_type=MESH,
        )

    def c_copy(k):
        return pltpu.make_async_remote_copy(
            src_ref=mod_mine.at[k], dst_ref=mod_other.at[k],
            send_sem=c_send.at[k], recv_sem=c_recv.at[k],
            device_id={"rcv": 1 - mc}, device_id_type=MESH,
        )

    def w_of(way):
        return 0 if way > 0 else 1

    def last(z, way):
        return z == (nz - 1 if way > 0 else 0)

    def a_copy(src, slot, k, way):
        return pltpu.make_async_remote_copy(
            src_ref=src, dst_ref=out.at[pl.ds(0, helped), slot, k],
            send_sem=za_send.at[w_of(way), slot, k], recv_sem=za_recv.at[w_of(way), slot, k],
            device_id={"freq": mz + way}, device_id_type=MESH,
        )

    def b_copy(src, slot, k, way):
        return pltpu.make_async_remote_copy(
            src_ref=src, dst_ref=out.at[pl.ds(helped, blocks - helped), slot, k],
            send_sem=zb_send.at[w_of(way), slot, k], recv_sem=zb_recv.at[w_of(way), slot, k],
            device_id={"freq": mz + way}, device_id_type=MESH,
        )

    def block_copy(slot, b, way):
        piece = out.at[b, slot]
        return pltpu.make_async_remote_copy(
            src_ref=piece, dst_ref=piece,
            send_sem=zc_send.at[w_of(way), slot, b], recv_sem=zc_recv.at[w_of(way), slot, b],
            device_id={"freq": mz + way}, device_id_type=MESH,
        )

    def given_copy(b, way):
        return pltpu.make_async_remote_copy(
            src_ref=made.at[b], dst_ref=given.at[b],
            send_sem=g_send.at[b], recv_sem=g_recv.at[b],
            device_id={"freq": mz + way}, device_id_type=MESH,
        )

    a_own = lambda k: upd.at[k, pl.ds(0, helped)]
    b_own = lambda k: upd.at[k, pl.ds(helped, blocks - helped)]
    a_out = lambda slot, k: out.at[pl.ds(0, helped), slot, k]
    b_out = lambda slot, k: out.at[pl.ds(helped, blocks - helped), slot, k]

    def own_copy(k):
        return pltpu.make_async_copy(upd.at[k], out.at[:, mz, k], own_sem.at[k])

    column = mc * width + iota((lines, width), 1)
    select = (column == pos[:, :]).astype(jnp.float32)

    def make_down(k, carry):
        for c in range(2):
            parts = []
            lines_k = data[c, pl.ds(pl.multiple_of(k * fl, fl), fl)].astype(jnp.float32)
            for f in range(FC):
                w = wav[c, k * FC + f]
                parts.append(w * select - lines_k[f * lines:(f + 1) * lines])
            down[k, c, pl.ds(pl.multiple_of(mx * fl, fl), fl)] = jnp.concatenate(
                parts, axis=0
            ).astype(jnp.bfloat16)
        for d in range(1, nx):
            x_copy(d, k).start()
        return carry

    lax.fori_loop(0, nchunk, make_down, 0)

    n = 2 * fi
    dst, src = iota((n, n), 0), iota((n, n), 1)
    want = (dst // FC % 2) * fi + (dst % FC) * rows + dst // (2 * FC)
    perm = (src == want).astype(jnp.bfloat16)

    def chunk_of(ref, k):
        part = pl.ds(pl.multiple_of(k * fi, fi), fi)
        return jnp.concatenate([ref[0, part], ref[1, part]], axis=0)

    def permute(k, carry):
        est_p[k] = jnp.dot(
            perm, chunk_of(est, k), preferred_element_type=jnp.float32
        ).astype(jnp.bfloat16)
        return carry

    lax.fori_loop(0, nchunk, permute, 0)

    cols = nx * fl
    shots = win.shape[2]
    s_row, s_col = iota((shots, cols), 0), iota((shots, cols), 1)
    spread = (s_row == (s_col // fl) * lines + s_col % lines).astype(jnp.bfloat16)
    shape3 = (rows, FC, cols)
    same = iota(shape3, 1) == iota(shape3, 2) % fl // lines
    scale = step[0]

    def model(k):
        for d in range(1, nx):
            here = down.at[k, :, pl.ds(lax.rem(mx + nx - d, nx) * fl, fl)]
            pltpu.make_async_remote_copy(
                src_ref=here, dst_ref=here,
                send_sem=x_send.at[d, k], recv_sem=x_recv.at[d, k],
                device_id={"shot": lax.rem(mx + d, nx)}, device_id_type=MESH,
            ).wait_recv()
        lines_k = down[k].reshape(2 * cols, width)
        m = lax.dot_general(
            est_p[k], lines_k, (((1,), (1,)), ((), ())), preferred_element_type=jnp.float32
        ).reshape(rows, 2, FC, 2 * cols)
        mod_mine[k, 0] = m[:, 0, :, :cols] - m[:, 1, :, cols:]
        mod_mine[k, 1] = m[:, 0, :, cols:] + m[:, 1, :, :cols]
        c_copy(k).start()

    def update(k):
        c_copy(k).wait_recv()
        total_re = mod_mine[k, 0] + mod_other[k, 0]
        total_im = mod_mine[k, 1] + mod_other[k, 1]
        w = jnp.dot(perm, chunk_of(win, k), preferred_element_type=jnp.float32).astype(jnp.bfloat16)
        w = jnp.dot(w, spread, preferred_element_type=jnp.float32).reshape(rows, 2, FC, cols)
        e_re = jnp.where(same, w[:, 0] - total_re, 0.0)
        e_im = jnp.where(same, w[:, 1] - total_im, 0.0)
        e = jnp.stack(
            [jnp.concatenate([e_re, e_im], axis=2), jnp.concatenate([e_im, -e_re], axis=2)], axis=1
        ).reshape(n, 2 * cols).astype(jnp.bfloat16)
        grad = jnp.dot(e, down[k].reshape(2 * cols, width), preferred_element_type=jnp.float32)
        new = (est_p[k].astype(jnp.float32) - scale * (grad * norm)).astype(jnp.bfloat16)
        for b in range(blocks):
            upd[k, b] = new[:, b * BLOCK:(b + 1) * BLOCK]
        own_copy(k).start()
        for way in (1, -1):
            @pl.when(jnp.logical_not(last(mz, way)))
            def _():
                b_copy(b_own(k), mz, k, way).start()

                if helped:
                    @pl.when(jnp.logical_not(last(mz + way, way)))
                    def _():
                        a_copy(a_own(k), mz, k, way).start()

    def near(k):
        for way in (1, -1):
            slot = mz - way

            @pl.when((slot >= 0) & (slot < nz))
            def _():
                b_copy(b_out(slot, k), slot, k, way).wait_recv()

                if helped:
                    @pl.when(jnp.logical_not(last(mz, way)))
                    def _():
                        a_copy(a_out(slot, k), slot, k, way).wait_recv()

                @pl.when(last(mz + way, way))
                def _():
                    b_copy(b_out(slot, k), slot, k, way).start()

    def step_of(k, carry):
        @pl.when(k < nchunk)
        def _():
            model(k)
            update(k)

        @pl.when(k >= LAG)
        def _():
            near(k - LAG)

        return carry

    lax.fori_loop(0, nchunk + LAG, step_of, 0)

    def own_done(k, carry):
        own_copy(k).wait()
        return carry

    lax.fori_loop(0, nchunk, own_done, 0)

    def hand_on(b, carry):
        for way in (1, -1):
            slot = mz - way
            inside = (slot >= 0) & (slot < nz)
            nxt = mz + way

            @pl.when(inside & (nxt > 0) & (nxt < nz - 1))
            def _():
                block_copy(slot, b, way).start()

        return carry

    lax.fori_loop(0, blocks, hand_on, 0)

    def far(h, carry):
        def one(b, carry):
            for way in (1, -1):
                slot = mz - way * h
                nxt = mz + way
                inside = (slot >= 0) & (slot < nz)
                at_end = last(mz, way)

                @pl.when(inside & jnp.logical_not(at_end))
                def _():
                    block_copy(slot, b, way).wait_recv()

                    @pl.when(jnp.logical_not(last(nxt, way)) | (b >= helped))
                    def _():
                        block_copy(slot, b, way).start()

                    if helped:
                        @pl.when(last(nxt, way) & (b < helped) & last(slot, -way))
                        def _():
                            load = pltpu.make_async_copy(out.at[b], ubuf, ubuf_sem)
                            load.start()
                            load.wait()
                            make_traces(
                                ubuf.reshape(nz * nchunk, ubuf.shape[2], BLOCK), table, level[0],
                                gain, rows, t_group, sparse, made.at[b],
                            )
                            given_copy(b, way).start()

                @pl.when(inside & at_end & (b >= helped))
                def _():
                    if not near_by:
                        block_copy(slot, b, way).wait_recv()

            return carry

        near_by = isinstance(h, int)
        return lax.fori_loop(0, blocks, one, carry)

    def end_chunk(k, carry):
        for way in (1, -1):
            slot = mz - 2 * way

            @pl.when((slot >= 0) & (slot < nz) & last(mz, way))
            def _():
                b_copy(b_out(slot, k), slot, k, way).wait_recv()

        return carry

    if nz > 2:
        lax.fori_loop(0, nchunk, end_chunk, 0)
        far(2, 0)
    lax.fori_loop(3, nz, far, 0)

    if helped:
        def take(b, carry):
            for way in (1, -1):
                @pl.when(last(mz, way))
                def _():
                    given_copy(b, way).wait_recv()

                @pl.when(last(mz + way, way))
                def _():
                    given_copy(b, way).wait_send()

            return carry

        lax.fori_loop(0, helped, take, 0)

    def drain(k, carry):
        for d in range(1, nx):
            x_copy(d, k).wait_send()
        c_copy(k).wait_send()
        for way in (1, -1):
            nxt = mz + way

            @pl.when(jnp.logical_not(last(mz, way)))
            def _():
                b_copy(b_own(k), mz, k, way).wait_send()

                if helped:
                    @pl.when(jnp.logical_not(last(nxt, way)))
                    def _():
                        a_copy(a_own(k), mz, k, way).wait_send()

            slot = mz - way

            @pl.when((slot >= 0) & (slot < nz) & last(nxt, way))
            def _():
                b_copy(b_own(k), slot, k, way).wait_send()

        return carry

    lax.fori_loop(0, nchunk, drain, 0)

    def drain_far(h, carry):
        def one(b, carry):
            for way in (1, -1):
                slot = mz - way * h
                nxt = mz + way
                inside = (slot >= 0) & (slot < nz) & (nxt >= 0) & (nxt < nz)
                to_end = last(nxt, way)

                @pl.when(inside & (jnp.logical_not(to_end) | ((b >= helped) & (h > 1))))
                def _():
                    block_copy(slot, b, way).wait_send()

            return carry

        return lax.fori_loop(0, blocks, one, carry)

    lax.fori_loop(1, nz, drain_far, 0)


def trace_kernel(rows, t_group, gain, helped, level, taken, table, u, given, out, sparse):
    ready = (pl.program_id(0) < helped) & (taken[0] > 0)

    @pl.when(ready)
    def _():
        out[...] = given[...]

    @pl.when(jnp.logical_not(ready))
    def _():
        make_traces(u, table, level[0], gain, rows, t_group, sparse, out)


def body(nx, nz, data, estimate, window_data, wavelet, positions, bins, threshold, step):
    _, nf, lines, width = data.shape
    rows = estimate.shape[2]
    shots = window_data.shape[3]
    nchunk = nf // FC
    norm = 1.0 / math.sqrt(shots * RCV)
    fi, cols = FC * rows, nx * FC * lines
    mz = lax.axis_index("freq")
    nt = NT // nz
    blocks, groups = width // BLOCK, nz * nchunk
    helped = 3 * blocks // 8 if nz >= 4 else 0
    held = max(helped, 1)
    gain, t_group = math.sqrt(RCV / NF), 32
    level = threshold.astype(jnp.float32) / 64.0

    def table_of(z):
        times = z * nt + lax.iota(jnp.int32, nt)
        phase = times[:, None] * bins[None, :] % NT
        angle = 2.0 * math.pi / NT * phase.astype(jnp.float32)
        table = jnp.stack([jnp.cos(angle), -jnp.sin(angle)], axis=1).astype(jnp.bfloat16)
        table = table.reshape(nt, 2, groups, FC).transpose(0, 2, 1, 3)
        return table.reshape(nt, 2 * nz * nf)

    vmem = pl.BlockSpec(memory_space=pltpu.VMEM)
    smem = pl.BlockSpec(memory_space=pltpu.SMEM)
    hbm = pl.BlockSpec(memory_space=pl.ANY)
    dma = pltpu.SemaphoreType.DMA
    spectra, given = pl.pallas_call(
        partial(
            update_kernel, nx, nz, nchunk, rows, lines, norm, blocks, helped, gain, t_group
        ),
        out_shape=(
            jax.ShapeDtypeStruct((blocks, nz, nchunk, 2 * fi, BLOCK), jnp.bfloat16),
            jax.ShapeDtypeStruct((held, nt * rows, BLOCK), jnp.bfloat16),
        ),
        in_specs=[vmem, vmem, vmem, smem, vmem, smem, smem, vmem],
        out_specs=(hbm, hbm),
        scratch_shapes=[
            pltpu.VMEM((nchunk, 2, cols, width), jnp.bfloat16),
            pltpu.VMEM((nchunk, 2 * fi, width), jnp.bfloat16),
            pltpu.VMEM((nchunk, blocks, 2 * fi, BLOCK), jnp.bfloat16),
            pltpu.VMEM((nchunk, 2, rows, FC, cols), jnp.float32),
            pltpu.VMEM((nchunk, 2, rows, FC, cols), jnp.float32),
            pltpu.VMEM((nz, nchunk, 2 * fi, BLOCK), jnp.bfloat16),
            pltpu.VMEM((rows, nt, BLOCK), jnp.bfloat16),
            pltpu.VMEM((held, nt * rows, BLOCK), jnp.bfloat16),
            dma((nx, nchunk)), dma((nx, nchunk)),
            dma((nchunk,)), dma((nchunk,)),
            dma((2, nz, nchunk)), dma((2, nz, nchunk)),
            dma((2, nz, nchunk)), dma((2, nz, nchunk)),
            dma((2, nz, blocks)), dma((2, nz, blocks)),
            dma((held,)), dma((held,)),
            dma((nchunk,)), dma,
        ],
        compiler_params=pltpu.CompilerParams(
            collective_id=0, has_side_effects=True, vmem_limit_bytes=58 << 20
        ),
        name="update",
    )(
        data.reshape(2, nf * lines, width),
        estimate.reshape(2, nf * rows, width),
        window_data.reshape(2, nf * rows, shots),
        wavelet,
        positions[:, None],
        step,
        level,
        table_of(jnp.where(mz < nz // 2, 0, nz - 1)),
    )
    taken = ((mz == 0) | (mz == nz - 1)).astype(jnp.int32)[None]
    traces = pl.pallas_call(
        partial(trace_kernel, rows, t_group, gain, helped),
        out_shape=jax.ShapeDtypeStruct((nt * rows, width), jnp.bfloat16),
        grid=(blocks,),
        in_specs=[
            smem,
            smem,
            pl.BlockSpec((nt, 2 * nz * nf), lambda j: (0, 0)),
            pl.BlockSpec((None, groups, 2 * fi, BLOCK), lambda j: (j, 0, 0, 0)),
            pl.BlockSpec(
                (None, nt * rows, BLOCK), lambda j: (jnp.minimum(j, held - 1), 0, 0)
            ),
        ],
        out_specs=pl.BlockSpec((nt * rows, BLOCK), lambda j: (0, j)),
        scratch_shapes=[pltpu.VMEM((rows, nt, BLOCK), jnp.bfloat16)],
        compiler_params=pltpu.CompilerParams(vmem_limit_bytes=60 << 20),
        name="traces",
    )(level, taken, table_of(mz), spectra.reshape(blocks, groups, 2 * fi, BLOCK), given)
    return traces.reshape(nt, rows, width)


def make_pairs(spec, b, table, lv, gain, rows, t_group, sparse, out, at):
    groups = spec.shape[0]
    part = 2 * GF * PAIR
    nt = table.shape[0] // PAIR
    for p in range(rows // PAIR):
        up = jnp.concatenate(
            [
                spec[:, b + h, p * part:(p + 1) * part].reshape(groups * part, TILE)
                for h in range(2)
            ],
            axis=1,
        )
        tr = jnp.dot(table[...], up, preferred_element_type=jnp.float32) * gain
        sparse[p] = (jnp.maximum(tr - lv, 0.0) + jnp.minimum(tr + lv, 0.0)).astype(jnp.bfloat16)
    lined = sparse.reshape(rows, nt, 2 * TILE)
    n = t_group * rows
    dst, src = iota((n, n), 0), iota((n, n), 1)
    perm = (src == (dst % rows) * t_group + dst // rows).astype(jnp.bfloat16)
    for g in range(nt // t_group):
        x = lined[:, g * t_group:(g + 1) * t_group, :].reshape(n, 2 * TILE)
        y = jnp.dot(perm, x, preferred_element_type=jnp.float32).astype(jnp.bfloat16)
        for h in range(2):
            out[at + h, g * n:(g + 1) * n, :] = y[:, h * TILE:(h + 1) * TILE]


def relay_kernel(
    nx, nz, nchunk, rows, lines, shots, norm, blocks, plain, early, gain, t_group,
    data, est, win_in, wav_in, pos_in, bins_in, thr_in, step_in, out,
    win, wav, pos, bins, thr, step, i_sem,
    dbuf, ebuf, down, spec, mod_mine, mod_other, tables, sparse, made,
    d_sem, e_sem, x_send, x_recv, c_send, c_recv, z_send, z_recv,
):
    mx = lax.axis_index("shot")
    mz = lax.axis_index("freq")
    mc = lax.axis_index("rcv")
    width = data.shape[2]
    fl = GF * lines
    fi = GF * rows
    n = 2 * fi
    end = jnp.where(mz < 2, 0, 3)
    inner = jnp.where(mz < 2, 1, 2)
    is_end = mz == end
    wide = mc == 0
    first = plain + wide.astype(jnp.int32)
    is_inner = jnp.logical_not(is_end)

    smalls = [
        pltpu.make_async_copy(src, dst, i_sem.at[i])
        for i, (src, dst) in enumerate(
            ((pos_in, pos), (wav_in, wav), (win_in, win), (step_in, step), (thr_in, thr),
             (bins_in, bins))
        )
    ]

    def load(ref, buf, sem, k):
        return pltpu.make_async_copy(
            ref.at[:, pl.ds(pl.multiple_of(k * fl, fl), fl)], buf.at[k], sem.at[k]
        )

    for copy in smalls[:2]:
        copy.start()
    load(data, dbuf, d_sem, 0).start()
    for copy in smalls[2:]:
        copy.start()

    barrier = pltpu.get_barrier_semaphore()
    for d in range(1, nx):
        pl.semaphore_signal(
            barrier, inc=1, device_id={"shot": lax.rem(mx + d, nx)}, device_id_type=MESH
        )
    pl.semaphore_signal(barrier, inc=1, device_id={"rcv": 1 - mc}, device_id_type=MESH)
    for z in (jnp.where(is_end, inner, end), jnp.where(is_end, 3 - inner, 3 - end)):
        pl.semaphore_signal(barrier, inc=1, device_id={"freq": z}, device_id_type=MESH)

    @pl.when(is_inner)
    def _():
        pl.semaphore_signal(barrier, inc=1, device_id={"freq": 3 - mz}, device_id_type=MESH)

    def x_copy(d, k, piece):
        here = down.at[k, :, pl.ds(piece * fl, fl)]
        return pltpu.make_async_remote_copy(
            src_ref=here, dst_ref=here,
            send_sem=x_send.at[d, k], recv_sem=x_recv.at[d, k],
            device_id={"shot": lax.rem(mx + d, nx)}, device_id_type=MESH,
        )

    def c_copy(k):
        return pltpu.make_async_remote_copy(
            src_ref=mod_mine.at[k], dst_ref=mod_other.at[k],
            send_sem=c_send.at[k], recv_sem=c_recv.at[k],
            device_id={"rcv": 1 - mc}, device_id_type=MESH,
        )

    def z_copy(kind, at, here, there, to):
        return pltpu.make_async_remote_copy(
            src_ref=here, dst_ref=there,
            send_sem=z_send.at[kind, at], recv_sem=z_recv.at[kind, at],
            device_id={"freq": to}, device_id_type=MESH,
        )

    def chunk_copy(kind, slot, k, count, to):
        here = spec.at[slot * nchunk + k, pl.ds(0, count)]
        return z_copy(kind, k, here, here, to)

    def block_copy(kind, slot, b, to):
        here = spec.at[pl.ds(slot * nchunk, nchunk), b]
        return z_copy(kind, b, here, here, to)

    end_near = lambda k: chunk_copy(0, end, k, early, inner)
    end_far = lambda k, of: chunk_copy(1, of, k, early, 3 - inner)
    across = lambda k, own: chunk_copy(2, own, k, early, 3 - mz)

    def outward(kind, slot, k, act):
        @pl.when(wide)
        def _():
            act(chunk_copy(kind, slot, k, plain + 1, end))

        @pl.when(jnp.logical_not(wide))
        def _():
            act(chunk_copy(kind, slot, k, plain, end))

    out_own = lambda k, act: outward(3, inner, k, act)
    out_opp = lambda k, act: outward(4, 3 - inner, k, act)
    out_far = lambda k, act: outward(5, 3 - end, k, act)
    start = lambda copy: copy.start()
    wait_recv = lambda copy: copy.wait_recv()
    wait_send = lambda copy: copy.wait_send()
    late_near = lambda b: block_copy(6, end, b, inner)
    late_far = lambda b, of: block_copy(7, of, b, 3 - inner)
    late_across = lambda b, own: block_copy(8, own, b, 3 - mz)
    trace_copy = lambda b, at: z_copy(9, b, made.at[at], out.at[b], end)

    for copy in smalls:
        copy.wait()
    level = thr[0].astype(jnp.float32) / 64.0
    line, column = iota((lines, width), 0), mc * width + iota((lines, width), 1)
    select = jnp.zeros((lines, width), jnp.float32)
    for s in range(lines):
        select = jnp.where((line == s) & (column == pos[s]), 1.0, select)

    def make_down(k):
        load(data, dbuf, d_sem, k).wait()
        for c in range(2):
            parts = []
            lines_k = dbuf[k, c].astype(jnp.float32)
            for f in range(GF):
                w = wav[c, k * GF + f]
                parts.append(w * select - lines_k[f * lines:(f + 1) * lines])
            down[k, c, pl.ds(pl.multiple_of(mx * fl, fl), fl)] = jnp.concatenate(
                parts, axis=0
            ).astype(jnp.bfloat16)

    def share_down(k):
        for d in range(1, nx):
            x_copy(d, k, mx).start()

    dst, src = iota((n, n), 0), iota((n, n), 1)
    want = (dst // GF % 2) * fi + (dst % GF) * rows + dst // (2 * GF)
    perm = (src == want).astype(jnp.bfloat16)

    cols = nx * fl
    nf = nchunk * GF
    col3 = iota((2 * rows, shots, cols), 2)
    shot_of = col3 // fl * lines + col3 % lines
    own_shot = iota((2 * rows, shots, cols), 1) == shot_of
    f_row, f_col = iota((nf, cols), 0), iota((nf, cols), 1) % fl // lines
    shape3 = (GF, rows, cols)
    same = iota(shape3, 0) == iota(shape3, 2) % fl // lines
    scale = step[0]

    def make_table(j, z):
        size, nt = nz * nf, sparse.shape[1] // PAIR
        wide = 2 * PAIR * size
        row, col = iota((size, wide), 0), iota((size, wide), 1)
        match = row == col // (2 * GF * PAIR) * GF + col % GF
        to_re = (match & (col // GF % 2 == 0)).astype(jnp.bfloat16)
        to_im = (match & (col // GF % 2 == 1)).astype(jnp.bfloat16)
        times = z * nt + iota((nt, size), 0)
        phase = times * bins[...] % NT
        angle = 2.0 * math.pi / NT * phase.astype(jnp.float32)
        full = jnp.dot(
            jnp.cos(angle).astype(jnp.bfloat16), to_re, preferred_element_type=jnp.float32
        ) + jnp.dot(
            (-jnp.sin(angle)).astype(jnp.bfloat16), to_im, preferred_element_type=jnp.float32
        )
        member = iota((nt, wide), 1) // (2 * GF) % PAIR
        for a in range(PAIR):
            tables[j, a * nt:(a + 1) * nt] = jnp.where(member == a, full, 0.0).astype(
                jnp.bfloat16
            )

    def spectra_of(k):
        return ebuf[k].reshape(n, width)

    def model(k):
        load(est, ebuf, e_sem, k).wait()
        for d in range(1, nx):
            x_copy(d, k, lax.rem(mx + nx - d, nx)).wait_recv()
        m_re, m_im = [
            lax.dot_general(
                spectra_of(k), down[k, c], (((1,), (1,)), ((), ())),
                preferred_element_type=jnp.float32,
            )
            for c in range(2)
        ]
        mod_mine[k, 0] = m_re[:fi] - m_im[fi:]
        mod_mine[k, 1] = m_im[:fi] + m_re[fi:]
        c_copy(k).start()

    def update(k):
        pick = (f_row == k * GF + f_col).astype(jnp.bfloat16)
        w = jnp.dot(win[...], pick, preferred_element_type=jnp.float32)
        w = jnp.where(own_shot, w.reshape(2 * rows, shots, cols), 0.0).sum(axis=1)
        c_copy(k).wait_recv()
        total_re = (mod_mine[k, 0] + mod_other[k, 0]).reshape(shape3)
        total_im = (mod_mine[k, 1] + mod_other[k, 1]).reshape(shape3)
        e_re = jnp.where(same, w[None, :rows] - total_re, 0.0).reshape(fi, cols)
        e_im = jnp.where(same, w[None, rows:] - total_im, 0.0).reshape(fi, cols)
        e = jnp.concatenate(
            [jnp.concatenate([e_re, e_im], axis=1), jnp.concatenate([e_im, -e_re], axis=1)], axis=0
        ).astype(jnp.bfloat16)
        grad = jnp.dot(e, down[k].reshape(2 * cols, width), preferred_element_type=jnp.float32)
        new = (spectra_of(k).astype(jnp.float32) - scale * (grad * norm)).astype(jnp.bfloat16)
        new = jnp.dot(perm, new, preferred_element_type=jnp.float32).astype(jnp.bfloat16)
        for b in range(blocks):
            spec[mz * nchunk + k, b] = new[:, b * TILE:(b + 1) * TILE]

    def send(k):
        @pl.when(is_end)
        def _():
            end_far(k, mz).start()
            end_near(k).start()

        @pl.when(is_inner)
        def _():
            out_own(k, start)
            across(k, mz).start()

    def relay(k):
        across(k, 3 - mz).wait_recv()
        out_opp(k, start)
        end_far(k, 3 - end).wait_recv()
        out_far(k, start)

    make_down(0)
    pl.semaphore_wait(barrier, nx + 2 + is_inner.astype(jnp.int32))
    share_down(0)

    def load_all(k, carry):
        @pl.when(k > 0)
        def _():
            load(data, dbuf, d_sem, k).start()

        load(est, ebuf, e_sem, k).start()
        return carry

    lax.fori_loop(0, nchunk, load_all, 0)
    make_down(1)
    share_down(1)

    def step_of(k, carry):
        @pl.when(k < nchunk - 2)
        def _():
            make_down(k + 2)
            share_down(k + 2)

        for j, z in enumerate((mz, end)):
            @pl.when(k == nchunk // 4 * (j + 1))
            def _():
                make_table(j, z)

        @pl.when(k < nchunk)
        def _():
            model(k)
            update(k)
            send(k)

        @pl.when(is_inner & (k >= 1))
        def _():
            relay(k - 1)

        return carry

    lax.fori_loop(0, nchunk + 1, step_of, 0)

    def own_pair(b):
        make_pairs(spec, b, tables.at[0], level, gain, rows, t_group, sparse, out, b)

    def help_pair(b, at):
        make_pairs(spec, b, tables.at[1], level, gain, rows, t_group, sparse, made, at)

    def arrived(b):
        late_near(b).wait_recv()
        late_far(b, 3 - end).wait_recv()
        late_across(b, 3 - mz).wait_recv()

    def loop(lo, hi, f):
        def one(i, carry):
            f(i)
            return carry

        lax.fori_loop(lo, hi, one, 0)

    @pl.when(is_inner)
    def _():
        loop(early, blocks, lambda b: late_across(b, mz).start())
        loop(0, nchunk, lambda k: end_near(k).wait_recv())
        narrow = 1 - wide.astype(jnp.int32)

        def both(j):
            b = first + 2 * j
            at = jnp.minimum(b, blocks - 2)

            @pl.when(b >= early)
            def _():
                arrived(b)

            @pl.when((b + 1 >= early) & (b + 1 < blocks))
            def _():
                arrived(b + 1)

            help_pair(at, 2 * j)

            @pl.when(at == b)
            def _():
                trace_copy(b, 2 * j).start()

            trace_copy(at + 1, 2 * j + 1).start()
            done = (b - narrow) // 2
            loop(jnp.where(j == 0, 0, done), done + 1, lambda i: own_pair(2 * i))

        loop(0, (blocks - plain) // 2 + narrow, both)

        def drain(k):
            across(k, mz).wait_send()
            out_own(k, wait_send)
            out_opp(k, wait_send)
            out_far(k, wait_send)

        loop(0, nchunk, drain)
        loop(early, blocks, lambda b: late_across(b, mz).wait_send())
        loop(first, blocks, lambda b: trace_copy(b, 0).wait_send())

    @pl.when(is_end)
    def _():
        def late(b):
            late_far(b, mz).start()
            late_near(b).start()

        loop(early, blocks, late)

        def come(k):
            out_own(k, wait_recv)
            out_opp(k, wait_recv)
            out_far(k, wait_recv)

        loop(0, nchunk, come)
        loop(0, (plain + 1) // 2, lambda j: own_pair(jnp.minimum(2 * j, first - 2)))
        loop(first, blocks, lambda b: trace_copy(b, 0).wait_recv())

        def drain(k):
            end_near(k).wait_send()
            end_far(k, mz).wait_send()

        def drain_late(b):
            late_near(b).wait_send()
            late_far(b, mz).wait_send()

        loop(0, nchunk, drain)
        loop(early, blocks, drain_late)

    def drain(k):
        for d in range(1, nx):
            x_copy(d, k, mx).wait_send()
        c_copy(k).wait_send()

    loop(0, nchunk, drain)


def place_kernel(traces, out, sem):
    copies = [
        pltpu.make_async_copy(
            traces.at[b], out.at[:, pl.ds(b * TILE, TILE)], sem.at[b]
        )
        for b in range(traces.shape[0])
    ]
    for copy in copies:
        copy.start()
    for copy in copies:
        copy.wait()


def relay_body(nx, nz, data, estimate, window_data, wavelet, positions, bins, threshold, step):
    _, nf, lines, width = data.shape
    rows = estimate.shape[2]
    shots = window_data.shape[3]
    nchunk = nf // GF
    norm = 1.0 / math.sqrt(shots * RCV)
    fi, cols = GF * rows, nx * GF * lines
    size = nz * nf
    nt = NT // nz
    blocks = width // TILE
    plain = PLAIN * blocks // 16
    early = plain + 3
    gain, t_group = math.sqrt(RCV / NF), 32

    vmem = pl.BlockSpec(memory_space=pltpu.VMEM)
    hbm = pl.BlockSpec(memory_space=pl.ANY)
    dma = pltpu.SemaphoreType.DMA
    traces = pl.pallas_call(
        partial(
            relay_kernel, nx, nz, nchunk, rows, lines, shots, norm, blocks, plain, early,
            gain, t_group,
        ),
        out_shape=pltpu.VMEM((blocks, nt * rows, TILE), jnp.bfloat16),
        in_specs=[hbm] * 8,
        out_specs=vmem,
        scratch_shapes=[
            pltpu.VMEM((2 * rows * shots, nf), jnp.bfloat16),
            pltpu.SMEM((2, nf), jnp.float32),
            pltpu.SMEM((lines,), jnp.int32),
            pltpu.VMEM((1, size), jnp.int32),
            pltpu.SMEM((1,), jnp.int32),
            pltpu.SMEM((1,), jnp.float32),
            dma((6,)),
            pltpu.VMEM((nchunk, 2, GF * lines, width), jnp.bfloat16),
            pltpu.VMEM((nchunk, 2, fi, width), jnp.bfloat16),
            pltpu.VMEM((nchunk, 2, cols, width), jnp.bfloat16),
            pltpu.VMEM((nz * nchunk, blocks, 2 * fi, TILE), jnp.bfloat16),
            pltpu.VMEM((nchunk, 2, fi, cols), jnp.float32),
            pltpu.VMEM((nchunk, 2, fi, cols), jnp.float32),
            pltpu.VMEM((2, PAIR * nt, 2 * PAIR * size), jnp.bfloat16),
            pltpu.VMEM((rows // PAIR, PAIR * nt, 2 * TILE), jnp.bfloat16),
            pltpu.VMEM((blocks - plain + 1, nt * rows, TILE), jnp.bfloat16),
            dma((nchunk,)), dma((nchunk,)),
            dma((nx, nchunk)), dma((nx, nchunk)),
            dma((nchunk,)), dma((nchunk,)),
            dma((10, max(nchunk, blocks))), dma((10, max(nchunk, blocks))),
        ],
        compiler_params=pltpu.CompilerParams(
            collective_id=1, has_side_effects=True, vmem_limit_bytes=48 << 20
        ),
        name="relay",
    )(
        data.reshape(2, nf * lines, width),
        estimate.reshape(2, nf * rows, width),
        window_data.transpose(0, 2, 3, 1).reshape(2 * rows * shots, nf),
        wavelet,
        positions,
        bins.reshape(1, size),
        threshold,
        step,
    )
    placed = pl.pallas_call(
        place_kernel,
        out_shape=jax.ShapeDtypeStruct((nt * rows, width), jnp.bfloat16),
        in_specs=[vmem],
        out_specs=hbm,
        scratch_shapes=[dma((blocks,))],
        compiler_params=pltpu.CompilerParams(vmem_limit_bytes=4 << 20),
        name="place",
    )(traces)
    return placed.reshape(nt, rows, width)


def solution(mesh):
    nz = mesh.shape["freq"]
    return jax.shard_map(
        partial(relay_body if nz == 4 else body, mesh.shape["shot"], nz),
        mesh=mesh,
        in_specs=(
            P(None, "freq", ("grp", "shot"), "rcv"),
            P(None, "freq", ("grp", "shot"), "rcv"),
            P(None, "freq", ("grp", "shot"), None),
            P(None, ("grp", "freq")),
            P(("grp", "shot")),
            P("grp"),
            P("grp"),
            P("grp"),
        ),
        out_specs=P("freq", ("grp", "shot"), "rcv"),
        check_vma=False,
    )
```

```python
from functools import partial
import math

import jax
import jax.numpy as jnp
from jax import lax
from jax.experimental import pallas as pl
from jax.experimental.pallas import tpu as pltpu
from jax.sharding import PartitionSpec as P

NF = 256
RCV = 4096
NT = 1024
FC = 8
GF = 4
PAIR = 2
TILE = 128
PLAIN = 5
AHEAD = 4
BLOCK = 256
LAG = 1
MESH = pl.DeviceIdType.MESH


def iota(shape, dim):
    return lax.broadcasted_iota(jnp.int32, shape, dim)


def make_traces(u, table, lv, gain, rows, t_group, sparse, out):
    groups, _, width = u.shape
    part = 2 * FC
    nt = table.shape[0]
    for i in range(rows):
        ui = u[:, i * part:(i + 1) * part, :].reshape(groups * part, width)
        tr = jnp.dot(table[...], ui, preferred_element_type=jnp.float32) * gain
        sparse[i] = (jnp.maximum(tr - lv, 0.0) + jnp.minimum(tr + lv, 0.0)).astype(jnp.bfloat16)
    n = t_group * rows
    dst, src = iota((n, n), 0), iota((n, n), 1)
    perm = (src == (dst % rows) * t_group + dst // rows).astype(jnp.bfloat16)
    for g in range(nt // t_group):
        x = sparse[:, g * t_group:(g + 1) * t_group, :].reshape(n, width)
        out[g * n:(g + 1) * n, :] = jnp.dot(
            perm, x, preferred_element_type=jnp.float32
        ).astype(jnp.bfloat16)


def update_kernel(
    nx, nz, nchunk, rows, lines, norm, blocks, helped, gain, t_group,
    data, est, win, wav, pos, step, level, table, out, given,
    down, est_p, upd, mod_mine, mod_other, ubuf, sparse, made,
    x_send, x_recv, c_send, c_recv, za_send, za_recv, zb_send, zb_recv,
    zc_send, zc_recv, g_send, g_recv, own_sem, ubuf_sem,
):
    mx = lax.axis_index("shot")
    mz = lax.axis_index("freq")
    mc = lax.axis_index("rcv")
    width = data.shape[2]
    fl = FC * lines
    fi = FC * rows

    barrier = pltpu.get_barrier_semaphore()
    for d in range(1, nx):
        pl.semaphore_signal(
            barrier, inc=1, device_id={"shot": lax.rem(mx + d, nx)}, device_id_type=MESH
        )
    pl.semaphore_signal(barrier, inc=1, device_id={"rcv": 1 - mc}, device_id_type=MESH)

    @pl.when(mz > 0)
    def _():
        pl.semaphore_signal(barrier, inc=1, device_id={"freq": mz - 1}, device_id_type=MESH)

    @pl.when(mz < nz - 1)
    def _():
        pl.semaphore_signal(barrier, inc=1, device_id={"freq": mz + 1}, device_id_type=MESH)

    ends = (mz > 0).astype(jnp.int32) + (mz < nz - 1).astype(jnp.int32)
    pl.semaphore_wait(barrier, nx + ends)

    def x_copy(d, k):
        piece = down.at[k, :, pl.ds(mx * fl, fl)]
        return pltpu.make_async_remote_copy(
            src_ref=piece, dst_ref=piece,
            send_sem=x_send.at[d, k], recv_sem=x_recv.at[d, k],
            device_id={"shot": lax.rem(mx + d, nx)}, device_id_type=MESH,
        )

    def c_copy(k):
        return pltpu.make_async_remote_copy(
            src_ref=mod_mine.at[k], dst_ref=mod_other.at[k],
            send_sem=c_send.at[k], recv_sem=c_recv.at[k],
            device_id={"rcv": 1 - mc}, device_id_type=MESH,
        )

    def w_of(way):
        return 0 if way > 0 else 1

    def last(z, way):
        return z == (nz - 1 if way > 0 else 0)

    def a_copy(src, slot, k, way):
        return pltpu.make_async_remote_copy(
            src_ref=src, dst_ref=out.at[pl.ds(0, helped), slot, k],
            send_sem=za_send.at[w_of(way), slot, k], recv_sem=za_recv.at[w_of(way), slot, k],
            device_id={"freq": mz + way}, device_id_type=MESH,
        )

    def b_copy(src, slot, k, way):
        return pltpu.make_async_remote_copy(
            src_ref=src, dst_ref=out.at[pl.ds(helped, blocks - helped), slot, k],
            send_sem=zb_send.at[w_of(way), slot, k], recv_sem=zb_recv.at[w_of(way), slot, k],
            device_id={"freq": mz + way}, device_id_type=MESH,
        )

    def block_copy(slot, b, way):
        piece = out.at[b, slot]
        return pltpu.make_async_remote_copy(
            src_ref=piece, dst_ref=piece,
            send_sem=zc_send.at[w_of(way), slot, b], recv_sem=zc_recv.at[w_of(way), slot, b],
            device_id={"freq": mz + way}, device_id_type=MESH,
        )

    def given_copy(b, way):
        return pltpu.make_async_remote_copy(
            src_ref=made.at[b], dst_ref=given.at[b],
            send_sem=g_send.at[b], recv_sem=g_recv.at[b],
            device_id={"freq": mz + way}, device_id_type=MESH,
        )

    a_own = lambda k: upd.at[k, pl.ds(0, helped)]
    b_own = lambda k: upd.at[k, pl.ds(helped, blocks - helped)]
    a_out = lambda slot, k: out.at[pl.ds(0, helped), slot, k]
    b_out = lambda slot, k: out.at[pl.ds(helped, blocks - helped), slot, k]

    def own_copy(k):
        return pltpu.make_async_copy(upd.at[k], out.at[:, mz, k], own_sem.at[k])

    column = mc * width + iota((lines, width), 1)
    select = (column == pos[:, :]).astype(jnp.float32)

    def make_down(k, carry):
        for c in range(2):
            parts = []
            lines_k = data[c, pl.ds(pl.multiple_of(k * fl, fl), fl)].astype(jnp.float32)
            for f in range(FC):
                w = wav[c, k * FC + f]
                parts.append(w * select - lines_k[f * lines:(f + 1) * lines])
            down[k, c, pl.ds(pl.multiple_of(mx * fl, fl), fl)] = jnp.concatenate(
                parts, axis=0
            ).astype(jnp.bfloat16)
        for d in range(1, nx):
            x_copy(d, k).start()
        return carry

    lax.fori_loop(0, nchunk, make_down, 0)

    n = 2 * fi
    dst, src = iota((n, n), 0), iota((n, n), 1)
    want = (dst // FC % 2) * fi + (dst % FC) * rows + dst // (2 * FC)
    perm = (src == want).astype(jnp.bfloat16)

    def chunk_of(ref, k):
        part = pl.ds(pl.multiple_of(k * fi, fi), fi)
        return jnp.concatenate([ref[0, part], ref[1, part]], axis=0)

    def permute(k, carry):
        est_p[k] = jnp.dot(
            perm, chunk_of(est, k), preferred_element_type=jnp.float32
        ).astype(jnp.bfloat16)
        return carry

    lax.fori_loop(0, nchunk, permute, 0)

    cols = nx * fl
    shots = win.shape[2]
    s_row, s_col = iota((shots, cols), 0), iota((shots, cols), 1)
    spread = (s_row == (s_col // fl) * lines + s_col % lines).astype(jnp.bfloat16)
    shape3 = (rows, FC, cols)
    same = iota(shape3, 1) == iota(shape3, 2) % fl // lines
    scale = step[0]

    def model(k):
        for d in range(1, nx):
            here = down.at[k, :, pl.ds(lax.rem(mx + nx - d, nx) * fl, fl)]
            pltpu.make_async_remote_copy(
                src_ref=here, dst_ref=here,
                send_sem=x_send.at[d, k], recv_sem=x_recv.at[d, k],
                device_id={"shot": lax.rem(mx + d, nx)}, device_id_type=MESH,
            ).wait_recv()
        lines_k = down[k].reshape(2 * cols, width)
        m = lax.dot_general(
            est_p[k], lines_k, (((1,), (1,)), ((), ())), preferred_element_type=jnp.float32
        ).reshape(rows, 2, FC, 2 * cols)
        mod_mine[k, 0] = m[:, 0, :, :cols] - m[:, 1, :, cols:]
        mod_mine[k, 1] = m[:, 0, :, cols:] + m[:, 1, :, :cols]
        c_copy(k).start()

    def update(k):
        c_copy(k).wait_recv()
        total_re = mod_mine[k, 0] + mod_other[k, 0]
        total_im = mod_mine[k, 1] + mod_other[k, 1]
        w = jnp.dot(perm, chunk_of(win, k), preferred_element_type=jnp.float32).astype(jnp.bfloat16)
        w = jnp.dot(w, spread, preferred_element_type=jnp.float32).reshape(rows, 2, FC, cols)
        e_re = jnp.where(same, w[:, 0] - total_re, 0.0)
        e_im = jnp.where(same, w[:, 1] - total_im, 0.0)
        e = jnp.stack(
            [jnp.concatenate([e_re, e_im], axis=2), jnp.concatenate([e_im, -e_re], axis=2)], axis=1
        ).reshape(n, 2 * cols).astype(jnp.bfloat16)
        grad = jnp.dot(e, down[k].reshape(2 * cols, width), preferred_element_type=jnp.float32)
        new = (est_p[k].astype(jnp.float32) - scale * (grad * norm)).astype(jnp.bfloat16)
        for b in range(blocks):
            upd[k, b] = new[:, b * BLOCK:(b + 1) * BLOCK]
        own_copy(k).start()
        for way in (1, -1):
            @pl.when(jnp.logical_not(last(mz, way)))
            def _():
                b_copy(b_own(k), mz, k, way).start()

                if helped:
                    @pl.when(jnp.logical_not(last(mz + way, way)))
                    def _():
                        a_copy(a_own(k), mz, k, way).start()

    def near(k):
        for way in (1, -1):
            slot = mz - way

            @pl.when((slot >= 0) & (slot < nz))
            def _():
                b_copy(b_out(slot, k), slot, k, way).wait_recv()

                if helped:
                    @pl.when(jnp.logical_not(last(mz, way)))
                    def _():
                        a_copy(a_out(slot, k), slot, k, way).wait_recv()

                @pl.when(last(mz + way, way))
                def _():
                    b_copy(b_out(slot, k), slot, k, way).start()

    def step_of(k, carry):
        @pl.when(k < nchunk)
        def _():
            model(k)
            update(k)

        @pl.when(k >= LAG)
        def _():
            near(k - LAG)

        return carry

    lax.fori_loop(0, nchunk + LAG, step_of, 0)

    def own_done(k, carry):
        own_copy(k).wait()
        return carry

    lax.fori_loop(0, nchunk, own_done, 0)

    def hand_on(b, carry):
        for way in (1, -1):
            slot = mz - way
            inside = (slot >= 0) & (slot < nz)
            nxt = mz + way

            @pl.when(inside & (nxt > 0) & (nxt < nz - 1))
            def _():
                block_copy(slot, b, way).start()

        return carry

    lax.fori_loop(0, blocks, hand_on, 0)

    def far(h, carry):
        def one(b, carry):
            for way in (1, -1):
                slot = mz - way * h
                nxt = mz + way
                inside = (slot >= 0) & (slot < nz)
                at_end = last(mz, way)

                @pl.when(inside & jnp.logical_not(at_end))
                def _():
                    block_copy(slot, b, way).wait_recv()

                    @pl.when(jnp.logical_not(last(nxt, way)) | (b >= helped))
                    def _():
                        block_copy(slot, b, way).start()

                    if helped:
                        @pl.when(last(nxt, way) & (b < helped) & last(slot, -way))
                        def _():
                            load = pltpu.make_async_copy(out.at[b], ubuf, ubuf_sem)
                            load.start()
                            load.wait()
                            make_traces(
                                ubuf.reshape(nz * nchunk, ubuf.shape[2], BLOCK), table, level[0],
                                gain, rows, t_group, sparse, made.at[b],
                            )
                            given_copy(b, way).start()

                @pl.when(inside & at_end & (b >= helped))
                def _():
                    if not near_by:
                        block_copy(slot, b, way).wait_recv()

            return carry

        near_by = isinstance(h, int)
        return lax.fori_loop(0, blocks, one, carry)

    def end_chunk(k, carry):
        for way in (1, -1):
            slot = mz - 2 * way

            @pl.when((slot >= 0) & (slot < nz) & last(mz, way))
            def _():
                b_copy(b_out(slot, k), slot, k, way).wait_recv()

        return carry

    if nz > 2:
        lax.fori_loop(0, nchunk, end_chunk, 0)
        far(2, 0)
    lax.fori_loop(3, nz, far, 0)

    if helped:
        def take(b, carry):
            for way in (1, -1):
                @pl.when(last(mz, way))
                def _():
                    given_copy(b, way).wait_recv()

                @pl.when(last(mz + way, way))
                def _():
                    given_copy(b, way).wait_send()

            return carry

        lax.fori_loop(0, helped, take, 0)

    def drain(k, carry):
        for d in range(1, nx):
            x_copy(d, k).wait_send()
        c_copy(k).wait_send()
        for way in (1, -1):
            nxt = mz + way

            @pl.when(jnp.logical_not(last(mz, way)))
            def _():
                b_copy(b_own(k), mz, k, way).wait_send()

                if helped:
                    @pl.when(jnp.logical_not(last(nxt, way)))
                    def _():
                        a_copy(a_own(k), mz, k, way).wait_send()

            slot = mz - way

            @pl.when((slot >= 0) & (slot < nz) & last(nxt, way))
            def _():
                b_copy(b_own(k), slot, k, way).wait_send()

        return carry

    lax.fori_loop(0, nchunk, drain, 0)

    def drain_far(h, carry):
        def one(b, carry):
            for way in (1, -1):
                slot = mz - way * h
                nxt = mz + way
                inside = (slot >= 0) & (slot < nz) & (nxt >= 0) & (nxt < nz)
                to_end = last(nxt, way)

                @pl.when(inside & (jnp.logical_not(to_end) | ((b >= helped) & (h > 1))))
                def _():
                    block_copy(slot, b, way).wait_send()

            return carry

        return lax.fori_loop(0, blocks, one, carry)

    lax.fori_loop(1, nz, drain_far, 0)


def trace_kernel(rows, t_group, gain, helped, level, taken, table, u, given, out, sparse):
    ready = (pl.program_id(0) < helped) & (taken[0] > 0)

    @pl.when(ready)
    def _():
        out[...] = given[...]

    @pl.when(jnp.logical_not(ready))
    def _():
        make_traces(u, table, level[0], gain, rows, t_group, sparse, out)


def body(nx, nz, data, estimate, window_data, wavelet, positions, bins, threshold, step):
    _, nf, lines, width = data.shape
    rows = estimate.shape[2]
    shots = window_data.shape[3]
    nchunk = nf // FC
    norm = 1.0 / math.sqrt(shots * RCV)
    fi, cols = FC * rows, nx * FC * lines
    mz = lax.axis_index("freq")
    nt = NT // nz
    blocks, groups = width // BLOCK, nz * nchunk
    helped = 3 * blocks // 8 if nz >= 4 else 0
    held = max(helped, 1)
    gain, t_group = math.sqrt(RCV / NF), 32
    level = threshold.astype(jnp.float32) / 64.0

    def table_of(z):
        times = z * nt + lax.iota(jnp.int32, nt)
        phase = times[:, None] * bins[None, :] % NT
        angle = 2.0 * math.pi / NT * phase.astype(jnp.float32)
        table = jnp.stack([jnp.cos(angle), -jnp.sin(angle)], axis=1).astype(jnp.bfloat16)
        table = table.reshape(nt, 2, groups, FC).transpose(0, 2, 1, 3)
        return table.reshape(nt, 2 * nz * nf)

    vmem = pl.BlockSpec(memory_space=pltpu.VMEM)
    smem = pl.BlockSpec(memory_space=pltpu.SMEM)
    hbm = pl.BlockSpec(memory_space=pl.ANY)
    dma = pltpu.SemaphoreType.DMA
    spectra, given = pl.pallas_call(
        partial(
            update_kernel, nx, nz, nchunk, rows, lines, norm, blocks, helped, gain, t_group
        ),
        out_shape=(
            jax.ShapeDtypeStruct((blocks, nz, nchunk, 2 * fi, BLOCK), jnp.bfloat16),
            jax.ShapeDtypeStruct((held, nt * rows, BLOCK), jnp.bfloat16),
        ),
        in_specs=[vmem, vmem, vmem, smem, vmem, smem, smem, vmem],
        out_specs=(hbm, hbm),
        scratch_shapes=[
            pltpu.VMEM((nchunk, 2, cols, width), jnp.bfloat16),
            pltpu.VMEM((nchunk, 2 * fi, width), jnp.bfloat16),
            pltpu.VMEM((nchunk, blocks, 2 * fi, BLOCK), jnp.bfloat16),
            pltpu.VMEM((nchunk, 2, rows, FC, cols), jnp.float32),
            pltpu.VMEM((nchunk, 2, rows, FC, cols), jnp.float32),
            pltpu.VMEM((nz, nchunk, 2 * fi, BLOCK), jnp.bfloat16),
            pltpu.VMEM((rows, nt, BLOCK), jnp.bfloat16),
            pltpu.VMEM((held, nt * rows, BLOCK), jnp.bfloat16),
            dma((nx, nchunk)), dma((nx, nchunk)),
            dma((nchunk,)), dma((nchunk,)),
            dma((2, nz, nchunk)), dma((2, nz, nchunk)),
            dma((2, nz, nchunk)), dma((2, nz, nchunk)),
            dma((2, nz, blocks)), dma((2, nz, blocks)),
            dma((held,)), dma((held,)),
            dma((nchunk,)), dma,
        ],
        compiler_params=pltpu.CompilerParams(
            collective_id=0, has_side_effects=True, vmem_limit_bytes=58 << 20
        ),
        name="update",
    )(
        data.reshape(2, nf * lines, width),
        estimate.reshape(2, nf * rows, width),
        window_data.reshape(2, nf * rows, shots),
        wavelet,
        positions[:, None],
        step,
        level,
        table_of(jnp.where(mz < nz // 2, 0, nz - 1)),
    )
    taken = ((mz == 0) | (mz == nz - 1)).astype(jnp.int32)[None]
    traces = pl.pallas_call(
        partial(trace_kernel, rows, t_group, gain, helped),
        out_shape=jax.ShapeDtypeStruct((nt * rows, width), jnp.bfloat16),
        grid=(blocks,),
        in_specs=[
            smem,
            smem,
            pl.BlockSpec((nt, 2 * nz * nf), lambda j: (0, 0)),
            pl.BlockSpec((None, groups, 2 * fi, BLOCK), lambda j: (j, 0, 0, 0)),
            pl.BlockSpec(
                (None, nt * rows, BLOCK), lambda j: (jnp.minimum(j, held - 1), 0, 0)
            ),
        ],
        out_specs=pl.BlockSpec((nt * rows, BLOCK), lambda j: (0, j)),
        scratch_shapes=[pltpu.VMEM((rows, nt, BLOCK), jnp.bfloat16)],
        compiler_params=pltpu.CompilerParams(vmem_limit_bytes=60 << 20),
        name="traces",
    )(level, taken, table_of(mz), spectra.reshape(blocks, groups, 2 * fi, BLOCK), given)
    return traces.reshape(nt, rows, width)


def make_pairs(spec, b, table, lv, gain, rows, t_group, sparse, out, at):
    groups = spec.shape[0]
    part = 2 * GF * PAIR
    nt = table.shape[0] // PAIR
    for p in range(rows // PAIR):
        up = jnp.concatenate(
            [
                spec[:, b + h, p * part:(p + 1) * part].reshape(groups * part, TILE)
                for h in range(2)
            ],
            axis=1,
        )
        tr = jnp.dot(table[...], up, preferred_element_type=jnp.float32) * gain
        sparse[p] = (jnp.maximum(tr - lv, 0.0) + jnp.minimum(tr + lv, 0.0)).astype(jnp.bfloat16)
    lined = sparse.reshape(rows, nt, 2 * TILE)
    n = t_group * rows
    dst, src = iota((n, n), 0), iota((n, n), 1)
    perm = (src == (dst % rows) * t_group + dst // rows).astype(jnp.bfloat16)
    for g in range(nt // t_group):
        x = lined[:, g * t_group:(g + 1) * t_group, :].reshape(n, 2 * TILE)
        y = jnp.dot(perm, x, preferred_element_type=jnp.float32).astype(jnp.bfloat16)
        for h in range(2):
            out[at + h, g * n:(g + 1) * n, :] = y[:, h * TILE:(h + 1) * TILE]


def relay_kernel(
    nx, nz, nchunk, rows, lines, shots, norm, blocks, plain, early, gain, t_group,
    data, est, win_in, wav_in, pos_in, bins_in, thr_in, step_in, out,
    win, wav, pos, bins, thr, step, i_sem,
    dbuf, ebuf, down, spec, mod_mine, mod_other, tables, sparse, made,
    d_sem, e_sem, x_send, x_recv, c_send, c_recv, z_send, near_recv, far_recv, across_recv,
    out_recv, late_recv, trace_recv,
):
    mx = lax.axis_index("shot")
    mz = lax.axis_index("freq")
    mc = lax.axis_index("rcv")
    width = data.shape[2]
    fl = GF * lines
    fi = GF * rows
    n = 2 * fi
    end = jnp.where(mz < 2, 0, 3)
    inner = jnp.where(mz < 2, 1, 2)
    is_end = mz == end
    wide = mc == 0
    first = plain + wide.astype(jnp.int32)
    is_inner = jnp.logical_not(is_end)

    smalls = [
        pltpu.make_async_copy(src, dst, i_sem.at[i])
        for i, (src, dst) in enumerate(
            ((pos_in, pos), (wav_in, wav), (win_in, win), (step_in, step), (thr_in, thr),
             (bins_in, bins))
        )
    ]

    def load(ref, buf, sem, k):
        return pltpu.make_async_copy(
            ref.at[:, pl.ds(pl.multiple_of(k * fl, fl), fl)], buf.at[k], sem.at[k % AHEAD]
        )

    for copy in smalls[:2]:
        copy.start()
    for k in range(AHEAD):
        load(data, dbuf, d_sem, k).start()
    for copy in smalls[2:]:
        copy.start()

    barrier = pltpu.get_barrier_semaphore()
    for d in range(1, nx):
        pl.semaphore_signal(
            barrier, inc=1, device_id={"shot": lax.rem(mx + d, nx)}, device_id_type=MESH
        )
    pl.semaphore_signal(barrier, inc=1, device_id={"rcv": 1 - mc}, device_id_type=MESH)
    for z in (jnp.where(is_end, inner, end), jnp.where(is_end, 3 - inner, 3 - end)):
        pl.semaphore_signal(barrier, inc=1, device_id={"freq": z}, device_id_type=MESH)

    @pl.when(is_inner)
    def _():
        pl.semaphore_signal(barrier, inc=1, device_id={"freq": 3 - mz}, device_id_type=MESH)

    def x_copy(d, k, piece):
        here = down.at[k, :, pl.ds(piece * fl, fl)] if k is not None else (
            down.at[:, :, pl.ds(piece * fl, fl)]
        )
        return pltpu.make_async_remote_copy(
            src_ref=here, dst_ref=here,
            send_sem=x_send.at[d - 1], recv_sem=x_recv.at[d - 1, 0 if k is None else k],
            device_id={"shot": lax.rem(mx + d, nx)}, device_id_type=MESH,
        )

    def c_copy(k):
        return pltpu.make_async_remote_copy(
            src_ref=mod_mine.at[k], dst_ref=mod_other.at[k],
            send_sem=c_send.at[0], recv_sem=c_recv.at[k % 2],
            device_id={"rcv": 1 - mc}, device_id_type=MESH,
        )

    c_all = pltpu.make_async_remote_copy(
        src_ref=mod_mine, dst_ref=mod_other, send_sem=c_send.at[0], recv_sem=c_recv.at[0],
        device_id={"rcv": 1 - mc}, device_id_type=MESH,
    )

    def z_copy(kind, here, there, recv, to):
        return pltpu.make_async_remote_copy(
            src_ref=here, dst_ref=there, send_sem=z_send.at[kind], recv_sem=recv,
            device_id={"freq": to}, device_id_type=MESH,
        )

    def chunk_copy(kind, slot, k, count, recv, to):
        at = slot * nchunk + k if k is not None else pl.ds(slot * nchunk, nchunk)
        here = spec.at[at, pl.ds(0, count)]
        return z_copy(kind, here, here, recv, to)

    def block_copy(kind, slot, b, to):
        at = b if b is not None else pl.ds(early, blocks - early)
        here = spec.at[pl.ds(slot * nchunk, nchunk), at]
        recv = late_recv.at[kind - 6, b - early if b is not None else 0]
        return z_copy(kind, here, here, recv, to)

    which = lambda k: 0 if k is None else k
    end_near = lambda k: chunk_copy(0, end, k, early, near_recv.at[0], inner)
    end_far = lambda k, of: chunk_copy(1, of, k, early, far_recv.at[which(k)], 3 - inner)
    across = lambda k, own: chunk_copy(2, own, k, early, across_recv.at[which(k)], 3 - mz)
    late_near = lambda b: block_copy(6, end, b, inner)
    late_far = lambda b, of: block_copy(7, of, b, 3 - inner)
    late_across = lambda b, own: block_copy(8, own, b, 3 - mz)
    trace_copy = lambda b, at: z_copy(9, made.at[at], out.at[b], trace_recv.at[0], end)

    def by_core(act):
        @pl.when(wide)
        def _():
            act(plain + 1)

        @pl.when(jnp.logical_not(wide))
        def _():
            act(plain)

    def traces_done(act):
        by_core(lambda count: act(z_copy(
            9, made.at[pl.ds(0, blocks - count)], out.at[pl.ds(0, blocks - count)], trace_recv.at[0],
            end,
        )))

    def outward(kind, slot, k, act):
        by_core(lambda count: act(chunk_copy(kind, slot, k, count, out_recv.at[kind - 3], end)))

    out_own = lambda k, act: outward(3, inner, k, act)
    out_opp = lambda k, act: outward(4, 3 - inner, k, act)
    out_far = lambda k, act: outward(5, 3 - end, k, act)
    start = lambda copy: copy.start()
    wait_recv = lambda copy: copy.wait_recv()
    wait_send = lambda copy: copy.wait_send()

    for copy in smalls:
        copy.wait()
    level = thr[0].astype(jnp.float32) / 64.0
    line, column = iota((lines, width), 0), mc * width + iota((lines, width), 1)
    select = jnp.zeros((lines, width), jnp.float32)
    for s in range(lines):
        select = jnp.where((line == s) & (column == pos[s]), 1.0, select)

    def make_down(k):
        load(data, dbuf, d_sem, k).wait()

        @pl.when(k + AHEAD < nchunk)
        def _():
            load(data, dbuf, d_sem, k + AHEAD).start()

        for c in range(2):
            parts = []
            lines_k = dbuf[k, c].astype(jnp.float32)
            for f in range(GF):
                w = wav[c, k * GF + f]
                parts.append(w * select - lines_k[f * lines:(f + 1) * lines])
            down[k, c, pl.ds(pl.multiple_of(mx * fl, fl), fl)] = jnp.concatenate(
                parts, axis=0
            ).astype(jnp.bfloat16)

    def share_down(k):
        for d in range(1, nx):
            x_copy(d, k, mx).start()

    dst, src = iota((n, n), 0), iota((n, n), 1)
    want = (dst // GF % 2) * fi + (dst % GF) * rows + dst // (2 * GF)
    perm = (src == want).astype(jnp.bfloat16)

    cols = nx * fl
    nf = nchunk * GF
    col3 = iota((2 * rows, shots, cols), 2)
    shot_of = col3 // fl * lines + col3 % lines
    own_shot = iota((2 * rows, shots, cols), 1) == shot_of
    f_row, f_col = iota((nf, cols), 0), iota((nf, cols), 1) % fl // lines
    shape3 = (GF, rows, cols)
    same = iota(shape3, 0) == iota(shape3, 2) % fl // lines
    scale = step[0]

    def make_table(j, z):
        size, nt = nz * nf, sparse.shape[1] // PAIR
        wide = 2 * PAIR * size
        row, col = iota((size, wide), 0), iota((size, wide), 1)
        match = row == col // (2 * GF * PAIR) * GF + col % GF
        to_re = (match & (col // GF % 2 == 0)).astype(jnp.bfloat16)
        to_im = (match & (col // GF % 2 == 1)).astype(jnp.bfloat16)
        times = z * nt + iota((nt, size), 0)
        phase = times * bins[...] % NT
        angle = 2.0 * math.pi / NT * phase.astype(jnp.float32)
        full = jnp.dot(
            jnp.cos(angle).astype(jnp.bfloat16), to_re, preferred_element_type=jnp.float32
        ) + jnp.dot(
            (-jnp.sin(angle)).astype(jnp.bfloat16), to_im, preferred_element_type=jnp.float32
        )
        member = iota((nt, wide), 1) // (2 * GF) % PAIR
        for a in range(PAIR):
            tables[j, a * nt:(a + 1) * nt] = jnp.where(member == a, full, 0.0).astype(
                jnp.bfloat16
            )

    def spectra_of(k):
        return ebuf[k].reshape(n, width)

    def model(k):
        load(est, ebuf, e_sem, k).wait()

        @pl.when(k + AHEAD < nchunk)
        def _():
            load(est, ebuf, e_sem, k + AHEAD).start()

        for d in range(1, nx):
            x_copy(d, k, lax.rem(mx + nx - d, nx)).wait_recv()
        m_re, m_im = [
            lax.dot_general(
                spectra_of(k), down[k, c], (((1,), (1,)), ((), ())),
                preferred_element_type=jnp.float32,
            )
            for c in range(2)
        ]
        mod_mine[k, 0] = m_re[:fi] - m_im[fi:]
        mod_mine[k, 1] = m_im[:fi] + m_re[fi:]
        c_copy(k).start()

    def update(k):
        pick = (f_row == k * GF + f_col).astype(jnp.bfloat16)
        w = jnp.dot(win[...], pick, preferred_element_type=jnp.float32)
        w = jnp.where(own_shot, w.reshape(2 * rows, shots, cols), 0.0).sum(axis=1)
        c_copy(k).wait_recv()
        total_re = (mod_mine[k, 0] + mod_other[k, 0]).reshape(shape3)
        total_im = (mod_mine[k, 1] + mod_other[k, 1]).reshape(shape3)
        e_re = jnp.where(same, w[None, :rows] - total_re, 0.0).reshape(fi, cols)
        e_im = jnp.where(same, w[None, rows:] - total_im, 0.0).reshape(fi, cols)
        e = jnp.concatenate(
            [jnp.concatenate([e_re, e_im], axis=1), jnp.concatenate([e_im, -e_re], axis=1)], axis=0
        ).astype(jnp.bfloat16)
        grad = jnp.dot(e, down[k].reshape(2 * cols, width), preferred_element_type=jnp.float32)
        new = (spectra_of(k).astype(jnp.float32) - scale * (grad * norm)).astype(jnp.bfloat16)
        new = jnp.dot(perm, new, preferred_element_type=jnp.float32).astype(jnp.bfloat16)
        for b in range(blocks):
            spec[mz * nchunk + k, b] = new[:, b * TILE:(b + 1) * TILE]

    def send(k):
        @pl.when(is_end)
        def _():
            end_far(k, mz).start()
            end_near(k).start()

        @pl.when(is_inner)
        def _():
            out_own(k, start)
            across(k, mz).start()

    def relay(k):
        across(k, 3 - mz).wait_recv()
        out_opp(k, start)
        end_far(k, 3 - end).wait_recv()
        out_far(k, start)

    make_down(0)
    pl.semaphore_wait(barrier, nx + 2 + is_inner.astype(jnp.int32))
    share_down(0)

    for k in range(AHEAD):
        load(est, ebuf, e_sem, k).start()
    make_down(1)
    share_down(1)

    def step_of(k, carry):
        @pl.when(k < nchunk - 2)
        def _():
            make_down(k + 2)
            share_down(k + 2)

        for j, z in enumerate((mz, end)):
            @pl.when(k == nchunk // 4 * (j + 1))
            def _():
                make_table(j, z)

        @pl.when(k < nchunk)
        def _():
            model(k)
            update(k)
            send(k)

        @pl.when(is_inner & (k >= 1))
        def _():
            relay(k - 1)

        return carry

    lax.fori_loop(0, nchunk + 1, step_of, 0)

    def own_pair(b):
        make_pairs(spec, b, tables.at[0], level, gain, rows, t_group, sparse, out, b)

    def help_pair(b, at):
        make_pairs(spec, b, tables.at[1], level, gain, rows, t_group, sparse, made, at)

    def arrived(b):
        late_near(b).wait_recv()
        late_far(b, 3 - end).wait_recv()
        late_across(b, 3 - mz).wait_recv()

    def loop(lo, hi, f):
        def one(i, carry):
            f(i)
            return carry

        lax.fori_loop(lo, hi, one, 0)

    @pl.when(is_inner)
    def _():
        loop(early, blocks, lambda b: late_across(b, mz).start())
        end_near(None).wait_recv()
        narrow = 1 - wide.astype(jnp.int32)

        def both(j):
            b = first + 2 * j

            @pl.when(b >= early)
            def _():
                arrived(b)

            @pl.when(b + 1 >= early)
            def _():
                arrived(b + 1)

            help_pair(b, 2 * j)
            trace_copy(b, 2 * j).start()
            trace_copy(b + 1, 2 * j + 1).start()
            done = (b - narrow) // 2
            loop(jnp.where(j == 0, 0, done), done + 1, lambda i: own_pair(2 * i))

        loop(0, (blocks - plain) // 2, both)

        @pl.when(jnp.logical_not(wide))
        def _():
            last = blocks - 1
            arrived(last)
            help_pair(last - 1, last - plain)
            trace_copy(last, last - plain + 1).start()
            own_pair(last - 1)

        across(None, mz).wait_send()
        late_across(None, mz).wait_send()
        for copies in (out_own, out_opp, out_far):
            copies(None, wait_send)
        traces_done(wait_send)

    @pl.when(is_end)
    def _():
        def late(b):
            late_far(b, mz).start()
            late_near(b).start()

        loop(early, blocks, late)

        for copies in (out_own, out_opp, out_far):
            copies(None, wait_recv)
        loop(0, (plain + 1) // 2, lambda j: own_pair(jnp.minimum(2 * j, first - 2)))
        traces_done(wait_recv)
        end_near(None).wait_send()
        end_far(None, mz).wait_send()
        late_near(None).wait_send()
        late_far(None, mz).wait_send()

    for d in range(1, nx):
        x_copy(d, None, mx).wait_send()
    c_all.wait_send()


def place_kernel(traces, out, sem):
    copies = [
        pltpu.make_async_copy(
            traces.at[b], out.at[:, pl.ds(b * TILE, TILE)], sem.at[b]
        )
        for b in range(traces.shape[0])
    ]
    for copy in copies:
        copy.start()
    for copy in copies:
        copy.wait()


def relay_body(nx, nz, data, estimate, window_data, wavelet, positions, bins, threshold, step):
    _, nf, lines, width = data.shape
    rows = estimate.shape[2]
    shots = window_data.shape[3]
    nchunk = nf // GF
    norm = 1.0 / math.sqrt(shots * RCV)
    fi, cols = GF * rows, nx * GF * lines
    size = nz * nf
    nt = NT // nz
    blocks = width // TILE
    plain = PLAIN * blocks // 16
    early = plain + 3
    gain, t_group = math.sqrt(RCV / NF), 32

    vmem = pl.BlockSpec(memory_space=pltpu.VMEM)
    hbm = pl.BlockSpec(memory_space=pl.ANY)
    dma = pltpu.SemaphoreType.DMA
    traces = pl.pallas_call(
        partial(
            relay_kernel, nx, nz, nchunk, rows, lines, shots, norm, blocks, plain, early,
            gain, t_group,
        ),
        out_shape=pltpu.VMEM((blocks, nt * rows, TILE), jnp.bfloat16),
        in_specs=[hbm] * 8,
        out_specs=vmem,
        scratch_shapes=[
            pltpu.VMEM((2 * rows * shots, nf), jnp.bfloat16),
            pltpu.SMEM((2, nf), jnp.float32),
            pltpu.SMEM((lines,), jnp.int32),
            pltpu.VMEM((1, size), jnp.int32),
            pltpu.SMEM((1,), jnp.int32),
            pltpu.SMEM((1,), jnp.float32),
            dma((6,)),
            pltpu.VMEM((nchunk, 2, GF * lines, width), jnp.bfloat16),
            pltpu.VMEM((nchunk, 2, fi, width), jnp.bfloat16),
            pltpu.VMEM((nchunk, 2, cols, width), jnp.bfloat16),
            pltpu.VMEM((nz * nchunk, blocks, 2 * fi, TILE), jnp.bfloat16),
            pltpu.VMEM((nchunk, 2, fi, cols), jnp.float32),
            pltpu.VMEM((nchunk, 2, fi, cols), jnp.float32),
            pltpu.VMEM((2, PAIR * nt, 2 * PAIR * size), jnp.bfloat16),
            pltpu.VMEM((rows // PAIR, PAIR * nt, 2 * TILE), jnp.bfloat16),
            pltpu.VMEM((blocks - plain + 1, nt * rows, TILE), jnp.bfloat16),
            dma((AHEAD,)), dma((AHEAD,)),
            dma((nx - 1,)), dma((nx - 1, nchunk)),
            dma((1,)), dma((2,)),
            dma((10,)), dma((1,)), dma((nchunk,)), dma((nchunk,)),
            dma((3,)), dma((3, blocks - early)), dma((1,)),
        ],
        compiler_params=pltpu.CompilerParams(
            collective_id=1, has_side_effects=True, vmem_limit_bytes=48 << 20
        ),
        name="relay",
    )(
        data.reshape(2, nf * lines, width),
        estimate.reshape(2, nf * rows, width),
        window_data.transpose(0, 2, 3, 1).reshape(2 * rows * shots, nf),
        wavelet,
        positions,
        bins.reshape(1, size),
        threshold,
        step,
    )
    placed = pl.pallas_call(
        place_kernel,
        out_shape=jax.ShapeDtypeStruct((nt * rows, width), jnp.bfloat16),
        in_specs=[vmem],
        out_specs=hbm,
        scratch_shapes=[dma((blocks,))],
        compiler_params=pltpu.CompilerParams(vmem_limit_bytes=4 << 20),
        name="place",
    )(traces)
    return placed.reshape(nt, rows, width)


def solution(mesh):
    nz = mesh.shape["freq"]
    return jax.shard_map(
        partial(relay_body if nz == 4 else body, mesh.shape["shot"], nz),
        mesh=mesh,
        in_specs=(
            P(None, "freq", ("grp", "shot"), "rcv"),
            P(None, "freq", ("grp", "shot"), "rcv"),
            P(None, "freq", ("grp", "shot"), None),
            P(None, ("grp", "freq")),
            P(("grp", "shot")),
            P("grp"),
            P("grp"),
            P("grp"),
        ),
        out_specs=P("freq", ("grp", "shot"), "rcv"),
        check_vma=False,
    )
```

```python
from functools import partial
import math

import jax
import jax.numpy as jnp
from jax import lax
from jax.experimental import pallas as pl
from jax.experimental.pallas import tpu as pltpu
from jax.sharding import PartitionSpec as P

NF = 256
RCV = 4096
NT = 1024
FC = 8
GF = 4
PAIR = 2
TILE = 128
PLAIN = 5
AHEAD = 4
BLOCK = 256
LAG = 1
MESH = pl.DeviceIdType.MESH


def iota(shape, dim):
    return lax.broadcasted_iota(jnp.int32, shape, dim)


def make_traces(u, table, lv, gain, rows, t_group, sparse, out):
    groups, _, width = u.shape
    part = 2 * FC
    nt = table.shape[0]
    for i in range(rows):
        ui = u[:, i * part:(i + 1) * part, :].reshape(groups * part, width)
        tr = jnp.dot(table[...], ui, preferred_element_type=jnp.float32) * gain
        sparse[i] = (jnp.maximum(tr - lv, 0.0) + jnp.minimum(tr + lv, 0.0)).astype(jnp.bfloat16)
    n = t_group * rows
    dst, src = iota((n, n), 0), iota((n, n), 1)
    perm = (src == (dst % rows) * t_group + dst // rows).astype(jnp.bfloat16)
    for g in range(nt // t_group):
        x = sparse[:, g * t_group:(g + 1) * t_group, :].reshape(n, width)
        out[g * n:(g + 1) * n, :] = jnp.dot(
            perm, x, preferred_element_type=jnp.float32
        ).astype(jnp.bfloat16)


def update_kernel(
    nx, nz, nchunk, rows, lines, norm, blocks, helped, gain, t_group,
    data, est, win, wav, pos, step, level, table, out, given,
    down, est_p, upd, mod_mine, mod_other, ubuf, sparse, made,
    x_send, x_recv, c_send, c_recv, za_send, za_recv, zb_send, zb_recv,
    zc_send, zc_recv, g_send, g_recv, own_sem, ubuf_sem,
):
    mx = lax.axis_index("shot")
    mz = lax.axis_index("freq")
    mc = lax.axis_index("rcv")
    width = data.shape[2]
    fl = FC * lines
    fi = FC * rows

    barrier = pltpu.get_barrier_semaphore()
    for d in range(1, nx):
        pl.semaphore_signal(
            barrier, inc=1, device_id={"shot": lax.rem(mx + d, nx)}, device_id_type=MESH
        )
    pl.semaphore_signal(barrier, inc=1, device_id={"rcv": 1 - mc}, device_id_type=MESH)

    @pl.when(mz > 0)
    def _():
        pl.semaphore_signal(barrier, inc=1, device_id={"freq": mz - 1}, device_id_type=MESH)

    @pl.when(mz < nz - 1)
    def _():
        pl.semaphore_signal(barrier, inc=1, device_id={"freq": mz + 1}, device_id_type=MESH)

    ends = (mz > 0).astype(jnp.int32) + (mz < nz - 1).astype(jnp.int32)
    pl.semaphore_wait(barrier, nx + ends)

    def x_copy(d, k):
        piece = down.at[k, :, pl.ds(mx * fl, fl)]
        return pltpu.make_async_remote_copy(
            src_ref=piece, dst_ref=piece,
            send_sem=x_send.at[d, k], recv_sem=x_recv.at[d, k],
            device_id={"shot": lax.rem(mx + d, nx)}, device_id_type=MESH,
        )

    def c_copy(k):
        return pltpu.make_async_remote_copy(
            src_ref=mod_mine.at[k], dst_ref=mod_other.at[k],
            send_sem=c_send.at[k], recv_sem=c_recv.at[k],
            device_id={"rcv": 1 - mc}, device_id_type=MESH,
        )

    def w_of(way):
        return 0 if way > 0 else 1

    def last(z, way):
        return z == (nz - 1 if way > 0 else 0)

    def a_copy(src, slot, k, way):
        return pltpu.make_async_remote_copy(
            src_ref=src, dst_ref=out.at[pl.ds(0, helped), slot, k],
            send_sem=za_send.at[w_of(way), slot, k], recv_sem=za_recv.at[w_of(way), slot, k],
            device_id={"freq": mz + way}, device_id_type=MESH,
        )

    def b_copy(src, slot, k, way):
        return pltpu.make_async_remote_copy(
            src_ref=src, dst_ref=out.at[pl.ds(helped, blocks - helped), slot, k],
            send_sem=zb_send.at[w_of(way), slot, k], recv_sem=zb_recv.at[w_of(way), slot, k],
            device_id={"freq": mz + way}, device_id_type=MESH,
        )

    def block_copy(slot, b, way):
        piece = out.at[b, slot]
        return pltpu.make_async_remote_copy(
            src_ref=piece, dst_ref=piece,
            send_sem=zc_send.at[w_of(way), slot, b], recv_sem=zc_recv.at[w_of(way), slot, b],
            device_id={"freq": mz + way}, device_id_type=MESH,
        )

    def given_copy(b, way):
        return pltpu.make_async_remote_copy(
            src_ref=made.at[b], dst_ref=given.at[b],
            send_sem=g_send.at[b], recv_sem=g_recv.at[b],
            device_id={"freq": mz + way}, device_id_type=MESH,
        )

    a_own = lambda k: upd.at[k, pl.ds(0, helped)]
    b_own = lambda k: upd.at[k, pl.ds(helped, blocks - helped)]
    a_out = lambda slot, k: out.at[pl.ds(0, helped), slot, k]
    b_out = lambda slot, k: out.at[pl.ds(helped, blocks - helped), slot, k]

    def own_copy(k):
        return pltpu.make_async_copy(upd.at[k], out.at[:, mz, k], own_sem.at[k])

    column = mc * width + iota((lines, width), 1)
    select = (column == pos[:, :]).astype(jnp.float32)

    def make_down(k, carry):
        for c in range(2):
            parts = []
            lines_k = data[c, pl.ds(pl.multiple_of(k * fl, fl), fl)].astype(jnp.float32)
            for f in range(FC):
                w = wav[c, k * FC + f]
                parts.append(w * select - lines_k[f * lines:(f + 1) * lines])
            down[k, c, pl.ds(pl.multiple_of(mx * fl, fl), fl)] = jnp.concatenate(
                parts, axis=0
            ).astype(jnp.bfloat16)
        for d in range(1, nx):
            x_copy(d, k).start()
        return carry

    lax.fori_loop(0, nchunk, make_down, 0)

    n = 2 * fi
    dst, src = iota((n, n), 0), iota((n, n), 1)
    want = (dst // FC % 2) * fi + (dst % FC) * rows + dst // (2 * FC)
    perm = (src == want).astype(jnp.bfloat16)

    def chunk_of(ref, k):
        part = pl.ds(pl.multiple_of(k * fi, fi), fi)
        return jnp.concatenate([ref[0, part], ref[1, part]], axis=0)

    def permute(k, carry):
        est_p[k] = jnp.dot(
            perm, chunk_of(est, k), preferred_element_type=jnp.float32
        ).astype(jnp.bfloat16)
        return carry

    lax.fori_loop(0, nchunk, permute, 0)

    cols = nx * fl
    shots = win.shape[2]
    s_row, s_col = iota((shots, cols), 0), iota((shots, cols), 1)
    spread = (s_row == (s_col // fl) * lines + s_col % lines).astype(jnp.bfloat16)
    shape3 = (rows, FC, cols)
    same = iota(shape3, 1) == iota(shape3, 2) % fl // lines
    scale = step[0]

    def model(k):
        for d in range(1, nx):
            here = down.at[k, :, pl.ds(lax.rem(mx + nx - d, nx) * fl, fl)]
            pltpu.make_async_remote_copy(
                src_ref=here, dst_ref=here,
                send_sem=x_send.at[d, k], recv_sem=x_recv.at[d, k],
                device_id={"shot": lax.rem(mx + d, nx)}, device_id_type=MESH,
            ).wait_recv()
        lines_k = down[k].reshape(2 * cols, width)
        m = lax.dot_general(
            est_p[k], lines_k, (((1,), (1,)), ((), ())), preferred_element_type=jnp.float32
        ).reshape(rows, 2, FC, 2 * cols)
        mod_mine[k, 0] = m[:, 0, :, :cols] - m[:, 1, :, cols:]
        mod_mine[k, 1] = m[:, 0, :, cols:] + m[:, 1, :, :cols]
        c_copy(k).start()

    def update(k):
        c_copy(k).wait_recv()
        total_re = mod_mine[k, 0] + mod_other[k, 0]
        total_im = mod_mine[k, 1] + mod_other[k, 1]
        w = jnp.dot(perm, chunk_of(win, k), preferred_element_type=jnp.float32).astype(jnp.bfloat16)
        w = jnp.dot(w, spread, preferred_element_type=jnp.float32).reshape(rows, 2, FC, cols)
        e_re = jnp.where(same, w[:, 0] - total_re, 0.0)
        e_im = jnp.where(same, w[:, 1] - total_im, 0.0)
        e = jnp.stack(
            [jnp.concatenate([e_re, e_im], axis=2), jnp.concatenate([e_im, -e_re], axis=2)], axis=1
        ).reshape(n, 2 * cols).astype(jnp.bfloat16)
        grad = jnp.dot(e, down[k].reshape(2 * cols, width), preferred_element_type=jnp.float32)
        new = (est_p[k].astype(jnp.float32) - scale * (grad * norm)).astype(jnp.bfloat16)
        for b in range(blocks):
            upd[k, b] = new[:, b * BLOCK:(b + 1) * BLOCK]
        own_copy(k).start()
        for way in (1, -1):
            @pl.when(jnp.logical_not(last(mz, way)))
            def _():
                b_copy(b_own(k), mz, k, way).start()

                if helped:
                    @pl.when(jnp.logical_not(last(mz + way, way)))
                    def _():
                        a_copy(a_own(k), mz, k, way).start()

    def near(k):
        for way in (1, -1):
            slot = mz - way

            @pl.when((slot >= 0) & (slot < nz))
            def _():
                b_copy(b_out(slot, k), slot, k, way).wait_recv()

                if helped:
                    @pl.when(jnp.logical_not(last(mz, way)))
                    def _():
                        a_copy(a_out(slot, k), slot, k, way).wait_recv()

                @pl.when(last(mz + way, way))
                def _():
                    b_copy(b_out(slot, k), slot, k, way).start()

    def step_of(k, carry):
        @pl.when(k < nchunk)
        def _():
            model(k)
            update(k)

        @pl.when(k >= LAG)
        def _():
            near(k - LAG)

        return carry

    lax.fori_loop(0, nchunk + LAG, step_of, 0)

    def own_done(k, carry):
        own_copy(k).wait()
        return carry

    lax.fori_loop(0, nchunk, own_done, 0)

    def hand_on(b, carry):
        for way in (1, -1):
            slot = mz - way
            inside = (slot >= 0) & (slot < nz)
            nxt = mz + way

            @pl.when(inside & (nxt > 0) & (nxt < nz - 1))
            def _():
                block_copy(slot, b, way).start()

        return carry

    lax.fori_loop(0, blocks, hand_on, 0)

    def far(h, carry):
        def one(b, carry):
            for way in (1, -1):
                slot = mz - way * h
                nxt = mz + way
                inside = (slot >= 0) & (slot < nz)
                at_end = last(mz, way)

                @pl.when(inside & jnp.logical_not(at_end))
                def _():
                    block_copy(slot, b, way).wait_recv()

                    @pl.when(jnp.logical_not(last(nxt, way)) | (b >= helped))
                    def _():
                        block_copy(slot, b, way).start()

                    if helped:
                        @pl.when(last(nxt, way) & (b < helped) & last(slot, -way))
                        def _():
                            load = pltpu.make_async_copy(out.at[b], ubuf, ubuf_sem)
                            load.start()
                            load.wait()
                            make_traces(
                                ubuf.reshape(nz * nchunk, ubuf.shape[2], BLOCK), table, level[0],
                                gain, rows, t_group, sparse, made.at[b],
                            )
                            given_copy(b, way).start()

                @pl.when(inside & at_end & (b >= helped))
                def _():
                    if not near_by:
                        block_copy(slot, b, way).wait_recv()

            return carry

        near_by = isinstance(h, int)
        return lax.fori_loop(0, blocks, one, carry)

    def end_chunk(k, carry):
        for way in (1, -1):
            slot = mz - 2 * way

            @pl.when((slot >= 0) & (slot < nz) & last(mz, way))
            def _():
                b_copy(b_out(slot, k), slot, k, way).wait_recv()

        return carry

    if nz > 2:
        lax.fori_loop(0, nchunk, end_chunk, 0)
        far(2, 0)
    lax.fori_loop(3, nz, far, 0)

    if helped:
        def take(b, carry):
            for way in (1, -1):
                @pl.when(last(mz, way))
                def _():
                    given_copy(b, way).wait_recv()

                @pl.when(last(mz + way, way))
                def _():
                    given_copy(b, way).wait_send()

            return carry

        lax.fori_loop(0, helped, take, 0)

    def drain(k, carry):
        for d in range(1, nx):
            x_copy(d, k).wait_send()
        c_copy(k).wait_send()
        for way in (1, -1):
            nxt = mz + way

            @pl.when(jnp.logical_not(last(mz, way)))
            def _():
                b_copy(b_own(k), mz, k, way).wait_send()

                if helped:
                    @pl.when(jnp.logical_not(last(nxt, way)))
                    def _():
                        a_copy(a_own(k), mz, k, way).wait_send()

            slot = mz - way

            @pl.when((slot >= 0) & (slot < nz) & last(nxt, way))
            def _():
                b_copy(b_own(k), slot, k, way).wait_send()

        return carry

    lax.fori_loop(0, nchunk, drain, 0)

    def drain_far(h, carry):
        def one(b, carry):
            for way in (1, -1):
                slot = mz - way * h
                nxt = mz + way
                inside = (slot >= 0) & (slot < nz) & (nxt >= 0) & (nxt < nz)
                to_end = last(nxt, way)

                @pl.when(inside & (jnp.logical_not(to_end) | ((b >= helped) & (h > 1))))
                def _():
                    block_copy(slot, b, way).wait_send()

            return carry

        return lax.fori_loop(0, blocks, one, carry)

    lax.fori_loop(1, nz, drain_far, 0)


def trace_kernel(rows, t_group, gain, helped, level, taken, table, u, given, out, sparse):
    ready = (pl.program_id(0) < helped) & (taken[0] > 0)

    @pl.when(ready)
    def _():
        out[...] = given[...]

    @pl.when(jnp.logical_not(ready))
    def _():
        make_traces(u, table, level[0], gain, rows, t_group, sparse, out)


def body(nx, nz, data, estimate, window_data, wavelet, positions, bins, threshold, step):
    _, nf, lines, width = data.shape
    rows = estimate.shape[2]
    shots = window_data.shape[3]
    nchunk = nf // FC
    norm = 1.0 / math.sqrt(shots * RCV)
    fi, cols = FC * rows, nx * FC * lines
    mz = lax.axis_index("freq")
    nt = NT // nz
    blocks, groups = width // BLOCK, nz * nchunk
    helped = 3 * blocks // 8 if nz >= 4 else 0
    held = max(helped, 1)
    gain, t_group = math.sqrt(RCV / NF), 32
    level = threshold.astype(jnp.float32) / 64.0

    def table_of(z):
        times = z * nt + lax.iota(jnp.int32, nt)
        phase = times[:, None] * bins[None, :] % NT
        angle = 2.0 * math.pi / NT * phase.astype(jnp.float32)
        table = jnp.stack([jnp.cos(angle), -jnp.sin(angle)], axis=1).astype(jnp.bfloat16)
        table = table.reshape(nt, 2, groups, FC).transpose(0, 2, 1, 3)
        return table.reshape(nt, 2 * nz * nf)

    vmem = pl.BlockSpec(memory_space=pltpu.VMEM)
    smem = pl.BlockSpec(memory_space=pltpu.SMEM)
    hbm = pl.BlockSpec(memory_space=pl.ANY)
    dma = pltpu.SemaphoreType.DMA
    spectra, given = pl.pallas_call(
        partial(
            update_kernel, nx, nz, nchunk, rows, lines, norm, blocks, helped, gain, t_group
        ),
        out_shape=(
            jax.ShapeDtypeStruct((blocks, nz, nchunk, 2 * fi, BLOCK), jnp.bfloat16),
            jax.ShapeDtypeStruct((held, nt * rows, BLOCK), jnp.bfloat16),
        ),
        in_specs=[vmem, vmem, vmem, smem, vmem, smem, smem, vmem],
        out_specs=(hbm, hbm),
        scratch_shapes=[
            pltpu.VMEM((nchunk, 2, cols, width), jnp.bfloat16),
            pltpu.VMEM((nchunk, 2 * fi, width), jnp.bfloat16),
            pltpu.VMEM((nchunk, blocks, 2 * fi, BLOCK), jnp.bfloat16),
            pltpu.VMEM((nchunk, 2, rows, FC, cols), jnp.float32),
            pltpu.VMEM((nchunk, 2, rows, FC, cols), jnp.float32),
            pltpu.VMEM((nz, nchunk, 2 * fi, BLOCK), jnp.bfloat16),
            pltpu.VMEM((rows, nt, BLOCK), jnp.bfloat16),
            pltpu.VMEM((held, nt * rows, BLOCK), jnp.bfloat16),
            dma((nx, nchunk)), dma((nx, nchunk)),
            dma((nchunk,)), dma((nchunk,)),
            dma((2, nz, nchunk)), dma((2, nz, nchunk)),
            dma((2, nz, nchunk)), dma((2, nz, nchunk)),
            dma((2, nz, blocks)), dma((2, nz, blocks)),
            dma((held,)), dma((held,)),
            dma((nchunk,)), dma,
        ],
        compiler_params=pltpu.CompilerParams(
            collective_id=0, has_side_effects=True, vmem_limit_bytes=58 << 20
        ),
        name="update",
    )(
        data.reshape(2, nf * lines, width),
        estimate.reshape(2, nf * rows, width),
        window_data.reshape(2, nf * rows, shots),
        wavelet,
        positions[:, None],
        step,
        level,
        table_of(jnp.where(mz < nz // 2, 0, nz - 1)),
    )
    taken = ((mz == 0) | (mz == nz - 1)).astype(jnp.int32)[None]
    traces = pl.pallas_call(
        partial(trace_kernel, rows, t_group, gain, helped),
        out_shape=jax.ShapeDtypeStruct((nt * rows, width), jnp.bfloat16),
        grid=(blocks,),
        in_specs=[
            smem,
            smem,
            pl.BlockSpec((nt, 2 * nz * nf), lambda j: (0, 0)),
            pl.BlockSpec((None, groups, 2 * fi, BLOCK), lambda j: (j, 0, 0, 0)),
            pl.BlockSpec(
                (None, nt * rows, BLOCK), lambda j: (jnp.minimum(j, held - 1), 0, 0)
            ),
        ],
        out_specs=pl.BlockSpec((nt * rows, BLOCK), lambda j: (0, j)),
        scratch_shapes=[pltpu.VMEM((rows, nt, BLOCK), jnp.bfloat16)],
        compiler_params=pltpu.CompilerParams(vmem_limit_bytes=60 << 20),
        name="traces",
    )(level, taken, table_of(mz), spectra.reshape(blocks, groups, 2 * fi, BLOCK), given)
    return traces.reshape(nt, rows, width)


def make_pairs(spec, b, table, lv, gain, rows, t_group, sparse, out, at):
    groups = spec.shape[0]
    part = 2 * GF * PAIR
    nt = table.shape[0] // PAIR
    for p in range(rows // PAIR):
        up = jnp.concatenate(
            [
                spec[:, b + h, p * part:(p + 1) * part].reshape(groups * part, TILE)
                for h in range(2)
            ],
            axis=1,
        )
        tr = jnp.dot(table[...], up, preferred_element_type=jnp.float32) * gain
        sparse[p] = (jnp.maximum(tr - lv, 0.0) + jnp.minimum(tr + lv, 0.0)).astype(jnp.bfloat16)
    lined = sparse.reshape(rows, nt, 2 * TILE)
    n = t_group * rows
    dst, src = iota((n, n), 0), iota((n, n), 1)
    perm = (src == (dst % rows) * t_group + dst // rows).astype(jnp.bfloat16)
    for g in range(nt // t_group):
        x = lined[:, g * t_group:(g + 1) * t_group, :].reshape(n, 2 * TILE)
        y = jnp.dot(perm, x, preferred_element_type=jnp.float32).astype(jnp.bfloat16)
        for h in range(2):
            out[at + h, g * n:(g + 1) * n, :] = y[:, h * TILE:(h + 1) * TILE]


def relay_kernel(
    nx, nz, nchunk, rows, lines, shots, norm, blocks, plain, early, gain, t_group,
    data, est, win_in, wav_in, pos_in, bins_in, thr_in, step_in, out,
    win, wav, pos, bins, thr, step, i_sem,
    dbuf, ebuf, down, spec, mod_mine, mod_other, tables, sparse, made,
    d_sem, e_sem, x_send, x_recv, c_send, c_recv, z_send, near_recv, pair_recv,
    out_recv, late_recv, trace_recv,
):
    mx = lax.axis_index("shot")
    mz = lax.axis_index("freq")
    mc = lax.axis_index("rcv")
    width = data.shape[2]
    fl = GF * lines
    fi = GF * rows
    n = 2 * fi
    end = jnp.where(mz < 2, 0, 3)
    inner = jnp.where(mz < 2, 1, 2)
    is_end = mz == end
    wide = mc == 0
    first = plain + wide.astype(jnp.int32)
    is_inner = jnp.logical_not(is_end)

    smalls = [
        pltpu.make_async_copy(src, dst, i_sem.at[i])
        for i, (src, dst) in enumerate(
            ((pos_in, pos), (wav_in, wav), (win_in, win), (step_in, step), (thr_in, thr),
             (bins_in, bins))
        )
    ]

    def load(ref, buf, sem, k):
        return pltpu.make_async_copy(
            ref.at[:, pl.ds(pl.multiple_of(k * fl, fl), fl)], buf.at[k], sem.at[k % AHEAD]
        )

    for copy in smalls[:2]:
        copy.start()
    for k in range(AHEAD):
        load(data, dbuf, d_sem, k).start()
    for copy in smalls[2:]:
        copy.start()

    barrier = pltpu.get_barrier_semaphore()
    for d in range(1, nx):
        pl.semaphore_signal(
            barrier, inc=1, device_id={"shot": lax.rem(mx + d, nx)}, device_id_type=MESH
        )
    pl.semaphore_signal(barrier, inc=1, device_id={"rcv": 1 - mc}, device_id_type=MESH)
    for z in (jnp.where(is_end, inner, end), jnp.where(is_end, 3 - inner, 3 - end)):
        pl.semaphore_signal(barrier, inc=1, device_id={"freq": z}, device_id_type=MESH)

    @pl.when(is_inner)
    def _():
        pl.semaphore_signal(barrier, inc=1, device_id={"freq": 3 - mz}, device_id_type=MESH)

    def x_copy(d, k, piece):
        here = down.at[k, :, pl.ds(piece * fl, fl)] if k is not None else (
            down.at[:, :, pl.ds(piece * fl, fl)]
        )
        return pltpu.make_async_remote_copy(
            src_ref=here, dst_ref=here,
            send_sem=x_send.at[d - 1], recv_sem=x_recv.at[d - 1, 0 if k is None else k],
            device_id={"shot": lax.rem(mx + d, nx)}, device_id_type=MESH,
        )

    def c_copy(k):
        return pltpu.make_async_remote_copy(
            src_ref=mod_mine.at[k], dst_ref=mod_other.at[k],
            send_sem=c_send.at[0], recv_sem=c_recv.at[k % 2],
            device_id={"rcv": 1 - mc}, device_id_type=MESH,
        )

    c_all = pltpu.make_async_remote_copy(
        src_ref=mod_mine, dst_ref=mod_other, send_sem=c_send.at[0], recv_sem=c_recv.at[0],
        device_id={"rcv": 1 - mc}, device_id_type=MESH,
    )

    def z_copy(kind, here, there, recv, to):
        return pltpu.make_async_remote_copy(
            src_ref=here, dst_ref=there, send_sem=z_send.at[kind], recv_sem=recv,
            device_id={"freq": to}, device_id_type=MESH,
        )

    def chunk_copy(kind, slot, k, count, recv, to):
        at = slot * nchunk + k if k is not None else pl.ds(slot * nchunk, nchunk)
        here = spec.at[at, pl.ds(0, count)]
        return z_copy(kind, here, here, recv, to)

    def block_copy(kind, slot, b, to):
        at = b if b is not None else pl.ds(early, blocks - early)
        here = spec.at[pl.ds(slot * nchunk, nchunk), at]
        recv = late_recv.at[b - early if b is not None else 0]
        return z_copy(kind, here, here, recv, to)

    which = lambda k: 0 if k is None else k
    end_near = lambda k: chunk_copy(0, end, k, early, near_recv.at[0], inner)
    end_far = lambda k, of: chunk_copy(1, of, k, early, pair_recv.at[which(k)], 3 - inner)
    across = lambda k, own: chunk_copy(2, own, k, early, pair_recv.at[which(k)], 3 - mz)
    late_near = lambda b: block_copy(6, end, b, inner)
    late_far = lambda b, of: block_copy(7, of, b, 3 - inner)
    late_across = lambda b, own: block_copy(8, own, b, 3 - mz)
    trace_copy = lambda b, at: z_copy(9, made.at[at], out.at[b], trace_recv.at[0], end)

    def by_core(act):
        @pl.when(wide)
        def _():
            act(plain + 1)

        @pl.when(jnp.logical_not(wide))
        def _():
            act(plain)

    def traces_done(act):
        by_core(lambda count: act(z_copy(
            9, made.at[pl.ds(0, blocks - count)], out.at[pl.ds(0, blocks - count)], trace_recv.at[0],
            end,
        )))

    def outward(kind, slot, k, act):
        by_core(lambda count: act(chunk_copy(kind, slot, k, count, out_recv.at[kind - 3], end)))

    out_own = lambda k, act: outward(3, inner, k, act)
    out_opp = lambda k, act: outward(4, 3 - inner, k, act)
    out_far = lambda k, act: outward(5, 3 - end, k, act)
    start = lambda copy: copy.start()
    wait_recv = lambda copy: copy.wait_recv()
    wait_send = lambda copy: copy.wait_send()

    for copy in smalls:
        copy.wait()
    level = thr[0].astype(jnp.float32) / 64.0
    line, column = iota((lines, width), 0), mc * width + iota((lines, width), 1)
    select = jnp.zeros((lines, width), jnp.float32)
    for s in range(lines):
        select = jnp.where((line == s) & (column == pos[s]), 1.0, select)

    def make_down(k):
        load(data, dbuf, d_sem, k).wait()

        @pl.when(k + AHEAD < nchunk)
        def _():
            load(data, dbuf, d_sem, k + AHEAD).start()

        for c in range(2):
            parts = []
            lines_k = dbuf[k, c].astype(jnp.float32)
            for f in range(GF):
                w = wav[c, k * GF + f]
                parts.append(w * select - lines_k[f * lines:(f + 1) * lines])
            down[k, c, pl.ds(pl.multiple_of(mx * fl, fl), fl)] = jnp.concatenate(
                parts, axis=0
            ).astype(jnp.bfloat16)

    def share_down(k):
        for d in range(1, nx):
            x_copy(d, k, mx).start()

    dst, src = iota((n, n), 0), iota((n, n), 1)
    want = (dst // GF % 2) * fi + (dst % GF) * rows + dst // (2 * GF)
    perm = (src == want).astype(jnp.bfloat16)

    cols = nx * fl
    nf = nchunk * GF
    col3 = iota((2 * rows, shots, cols), 2)
    shot_of = col3 // fl * lines + col3 % lines
    own_shot = iota((2 * rows, shots, cols), 1) == shot_of
    f_row, f_col = iota((nf, cols), 0), iota((nf, cols), 1) % fl // lines
    shape3 = (GF, rows, cols)
    same = iota(shape3, 0) == iota(shape3, 2) % fl // lines
    scale = step[0]

    def make_table(j, z):
        size, nt = nz * nf, sparse.shape[1] // PAIR
        wide = 2 * PAIR * size
        row, col = iota((size, wide), 0), iota((size, wide), 1)
        match = row == col // (2 * GF * PAIR) * GF + col % GF
        to_re = (match & (col // GF % 2 == 0)).astype(jnp.bfloat16)
        to_im = (match & (col // GF % 2 == 1)).astype(jnp.bfloat16)
        times = z * nt + iota((nt, size), 0)
        phase = times * bins[...] % NT
        angle = 2.0 * math.pi / NT * phase.astype(jnp.float32)
        full = jnp.dot(
            jnp.cos(angle).astype(jnp.bfloat16), to_re, preferred_element_type=jnp.float32
        ) + jnp.dot(
            (-jnp.sin(angle)).astype(jnp.bfloat16), to_im, preferred_element_type=jnp.float32
        )
        member = iota((nt, wide), 1) // (2 * GF) % PAIR
        for a in range(PAIR):
            tables[j, a * nt:(a + 1) * nt] = jnp.where(member == a, full, 0.0).astype(
                jnp.bfloat16
            )

    def spectra_of(k):
        return ebuf[k].reshape(n, width)

    def model(k):
        load(est, ebuf, e_sem, k).wait()

        @pl.when(k + AHEAD < nchunk)
        def _():
            load(est, ebuf, e_sem, k + AHEAD).start()

        for d in range(1, nx):
            x_copy(d, k, lax.rem(mx + nx - d, nx)).wait_recv()
        m_re, m_im = [
            lax.dot_general(
                spectra_of(k), down[k, c], (((1,), (1,)), ((), ())),
                preferred_element_type=jnp.float32,
            )
            for c in range(2)
        ]
        mod_mine[k, 0] = m_re[:fi] - m_im[fi:]
        mod_mine[k, 1] = m_im[:fi] + m_re[fi:]
        c_copy(k).start()

    def update(k):
        pick = (f_row == k * GF + f_col).astype(jnp.bfloat16)
        w = jnp.dot(win[...], pick, preferred_element_type=jnp.float32)
        w = jnp.where(own_shot, w.reshape(2 * rows, shots, cols), 0.0).sum(axis=1)
        c_copy(k).wait_recv()
        total_re = (mod_mine[k, 0] + mod_other[k, 0]).reshape(shape3)
        total_im = (mod_mine[k, 1] + mod_other[k, 1]).reshape(shape3)
        e_re = jnp.where(same, w[None, :rows] - total_re, 0.0).reshape(fi, cols)
        e_im = jnp.where(same, w[None, rows:] - total_im, 0.0).reshape(fi, cols)
        e = jnp.concatenate(
            [jnp.concatenate([e_re, e_im], axis=1), jnp.concatenate([e_im, -e_re], axis=1)], axis=0
        ).astype(jnp.bfloat16)
        grad = jnp.dot(e, down[k].reshape(2 * cols, width), preferred_element_type=jnp.float32)
        new = (spectra_of(k).astype(jnp.float32) - scale * (grad * norm)).astype(jnp.bfloat16)
        new = jnp.dot(perm, new, preferred_element_type=jnp.float32).astype(jnp.bfloat16)
        for b in range(blocks):
            spec[mz * nchunk + k, b] = new[:, b * TILE:(b + 1) * TILE]

    def send(k):
        @pl.when(is_end)
        def _():
            end_far(k, mz).start()
            end_near(k).start()

        @pl.when(is_inner)
        def _():
            out_own(k, start)
            across(k, mz).start()

    def relay(k):
        two = spec.at[pl.ds(0, 2), pl.ds(0, early)]
        z_copy(2, two, two, pair_recv.at[k], 3 - mz).wait_recv()
        out_opp(k, start)
        out_far(k, start)

    make_down(0)
    pl.semaphore_wait(barrier, nx + 2 + is_inner.astype(jnp.int32))
    share_down(0)

    for k in range(AHEAD):
        load(est, ebuf, e_sem, k).start()
    make_down(1)
    share_down(1)

    def step_of(k, carry):
        @pl.when(k < nchunk - 2)
        def _():
            make_down(k + 2)
            share_down(k + 2)

        for j, z in enumerate((mz, end)):
            @pl.when(k == nchunk // 4 * (j + 1))
            def _():
                make_table(j, z)

        @pl.when(k < nchunk)
        def _():
            model(k)
            update(k)
            send(k)

        @pl.when(is_inner & (k >= 1))
        def _():
            relay(k - 1)

        return carry

    lax.fori_loop(0, nchunk + 1, step_of, 0)

    def own_pair(b):
        make_pairs(spec, b, tables.at[0], level, gain, rows, t_group, sparse, out, b)

    def help_pair(b, at):
        make_pairs(spec, b, tables.at[1], level, gain, rows, t_group, sparse, made, at)

    def arrived(b):
        three = spec.at[pl.ds(0, nchunk), pl.ds(0, 3)]
        z_copy(8, three, three, late_recv.at[b - early], 3 - mz).wait_recv()

    def loop(lo, hi, f):
        def one(i, carry):
            f(i)
            return carry

        lax.fori_loop(lo, hi, one, 0)

    @pl.when(is_inner)
    def _():
        loop(early, blocks, lambda b: late_across(b, mz).start())
        end_near(None).wait_recv()
        narrow = 1 - wide.astype(jnp.int32)

        def both(j):
            b = first + 2 * j

            @pl.when(b >= early)
            def _():
                arrived(b)

            @pl.when(b + 1 >= early)
            def _():
                arrived(b + 1)

            help_pair(b, 2 * j)
            trace_copy(b, 2 * j).start()
            trace_copy(b + 1, 2 * j + 1).start()
            done = (b - narrow) // 2
            loop(jnp.where(j == 0, 0, done), done + 1, lambda i: own_pair(2 * i))

        loop(0, (blocks - plain) // 2, both)

        @pl.when(jnp.logical_not(wide))
        def _():
            last = blocks - 1
            arrived(last)
            help_pair(last - 1, last - plain)
            trace_copy(last, last - plain + 1).start()
            own_pair(last - 1)

        across(None, mz).wait_send()
        late_across(None, mz).wait_send()
        for copies in (out_own, out_opp, out_far):
            copies(None, wait_send)
        traces_done(wait_send)

    @pl.when(is_end)
    def _():
        def late(b):
            late_far(b, mz).start()
            late_near(b).start()

        loop(early, blocks, late)

        for copies in (out_own, out_opp, out_far):
            copies(None, wait_recv)
        loop(0, (plain + 1) // 2, lambda j: own_pair(jnp.minimum(2 * j, first - 2)))
        traces_done(wait_recv)
        end_near(None).wait_send()
        end_far(None, mz).wait_send()
        late_near(None).wait_send()
        late_far(None, mz).wait_send()

    for d in range(1, nx):
        x_copy(d, None, mx).wait_send()
    c_all.wait_send()


def place_kernel(traces, out, sem):
    copies = [
        pltpu.make_async_copy(
            traces.at[b], out.at[:, pl.ds(b * TILE, TILE)], sem.at[b]
        )
        for b in range(traces.shape[0])
    ]
    for copy in copies:
        copy.start()
    for copy in copies:
        copy.wait()


def relay_body(nx, nz, data, estimate, window_data, wavelet, positions, bins, threshold, step):
    _, nf, lines, width = data.shape
    rows = estimate.shape[2]
    shots = window_data.shape[3]
    nchunk = nf // GF
    norm = 1.0 / math.sqrt(shots * RCV)
    fi, cols = GF * rows, nx * GF * lines
    size = nz * nf
    nt = NT // nz
    blocks = width // TILE
    plain = PLAIN * blocks // 16
    early = plain + 3
    gain, t_group = math.sqrt(RCV / NF), 32

    vmem = pl.BlockSpec(memory_space=pltpu.VMEM)
    hbm = pl.BlockSpec(memory_space=pl.ANY)
    dma = pltpu.SemaphoreType.DMA
    traces = pl.pallas_call(
        partial(
            relay_kernel, nx, nz, nchunk, rows, lines, shots, norm, blocks, plain, early,
            gain, t_group,
        ),
        out_shape=pltpu.VMEM((blocks, nt * rows, TILE), jnp.bfloat16),
        in_specs=[hbm] * 8,
        out_specs=vmem,
        scratch_shapes=[
            pltpu.VMEM((2 * rows * shots, nf), jnp.bfloat16),
            pltpu.SMEM((2, nf), jnp.float32),
            pltpu.SMEM((lines,), jnp.int32),
            pltpu.VMEM((1, size), jnp.int32),
            pltpu.SMEM((1,), jnp.int32),
            pltpu.SMEM((1,), jnp.float32),
            dma((6,)),
            pltpu.VMEM((nchunk, 2, GF * lines, width), jnp.bfloat16),
            pltpu.VMEM((nchunk, 2, fi, width), jnp.bfloat16),
            pltpu.VMEM((nchunk, 2, cols, width), jnp.bfloat16),
            pltpu.VMEM((nz * nchunk, blocks, 2 * fi, TILE), jnp.bfloat16),
            pltpu.VMEM((nchunk, 2, fi, cols), jnp.float32),
            pltpu.VMEM((nchunk, 2, fi, cols), jnp.float32),
            pltpu.VMEM((2, PAIR * nt, 2 * PAIR * size), jnp.bfloat16),
            pltpu.VMEM((rows // PAIR, PAIR * nt, 2 * TILE), jnp.bfloat16),
            pltpu.VMEM((blocks - plain + 1, nt * rows, TILE), jnp.bfloat16),
            dma((AHEAD,)), dma((AHEAD,)),
            dma((nx - 1,)), dma((nx - 1, nchunk)),
            dma((1,)), dma((2,)),
            dma((10,)), dma((1,)), dma((nchunk,)),
            dma((3,)), dma((blocks - early,)), dma((1,)),
        ],
        compiler_params=pltpu.CompilerParams(
            collective_id=1, has_side_effects=True, vmem_limit_bytes=48 << 20
        ),
        name="relay",
    )(
        data.reshape(2, nf * lines, width),
        estimate.reshape(2, nf * rows, width),
        window_data.transpose(0, 2, 3, 1).reshape(2 * rows * shots, nf),
        wavelet,
        positions,
        bins.reshape(1, size),
        threshold,
        step,
    )
    placed = pl.pallas_call(
        place_kernel,
        out_shape=jax.ShapeDtypeStruct((nt * rows, width), jnp.bfloat16),
        in_specs=[vmem],
        out_specs=hbm,
        scratch_shapes=[dma((blocks,))],
        compiler_params=pltpu.CompilerParams(vmem_limit_bytes=4 << 20),
        name="place",
    )(traces)
    return placed.reshape(nt, rows, width)


def solution(mesh):
    nz = mesh.shape["freq"]
    return jax.shard_map(
        partial(relay_body if nz == 4 else body, mesh.shape["shot"], nz),
        mesh=mesh,
        in_specs=(
            P(None, "freq", ("grp", "shot"), "rcv"),
            P(None, "freq", ("grp", "shot"), "rcv"),
            P(None, "freq", ("grp", "shot"), None),
            P(None, ("grp", "freq")),
            P(("grp", "shot")),
            P("grp"),
            P("grp"),
            P("grp"),
        ),
        out_specs=P("freq", ("grp", "shot"), "rcv"),
        check_vma=False,
    )
```

```python
from functools import partial
import math

import jax
import jax.numpy as jnp
from jax import lax
from jax.experimental import pallas as pl
from jax.experimental.pallas import tpu as pltpu
from jax.sharding import PartitionSpec as P

NF = 256
RCV = 4096
NT = 1024
FC = 8
GF = 4
PAIR = 2
TILE = 128
PLAIN = 5
AHEAD = 4
BLOCK = 256
LAG = 1
MESH = pl.DeviceIdType.MESH


def iota(shape, dim):
    return lax.broadcasted_iota(jnp.int32, shape, dim)


def make_traces(u, table, lv, gain, rows, t_group, sparse, out):
    groups, _, width = u.shape
    part = 2 * FC
    nt = table.shape[0]
    for i in range(rows):
        ui = u[:, i * part:(i + 1) * part, :].reshape(groups * part, width)
        tr = jnp.dot(table[...], ui, preferred_element_type=jnp.float32) * gain
        sparse[i] = (jnp.maximum(tr - lv, 0.0) + jnp.minimum(tr + lv, 0.0)).astype(jnp.bfloat16)
    n = t_group * rows
    dst, src = iota((n, n), 0), iota((n, n), 1)
    perm = (src == (dst % rows) * t_group + dst // rows).astype(jnp.bfloat16)
    for g in range(nt // t_group):
        x = sparse[:, g * t_group:(g + 1) * t_group, :].reshape(n, width)
        out[g * n:(g + 1) * n, :] = jnp.dot(
            perm, x, preferred_element_type=jnp.float32
        ).astype(jnp.bfloat16)


def update_kernel(
    nx, nz, nchunk, rows, lines, norm, blocks, helped, gain, t_group,
    data, est, win, wav, pos, step, level, table, out, given,
    down, est_p, upd, mod_mine, mod_other, ubuf, sparse, made,
    x_send, x_recv, c_send, c_recv, za_send, za_recv, zb_send, zb_recv,
    zc_send, zc_recv, g_send, g_recv, own_sem, ubuf_sem,
):
    mx = lax.axis_index("shot")
    mz = lax.axis_index("freq")
    mc = lax.axis_index("rcv")
    width = data.shape[2]
    fl = FC * lines
    fi = FC * rows

    barrier = pltpu.get_barrier_semaphore()
    for d in range(1, nx):
        pl.semaphore_signal(
            barrier, inc=1, device_id={"shot": lax.rem(mx + d, nx)}, device_id_type=MESH
        )
    pl.semaphore_signal(barrier, inc=1, device_id={"rcv": 1 - mc}, device_id_type=MESH)

    @pl.when(mz > 0)
    def _():
        pl.semaphore_signal(barrier, inc=1, device_id={"freq": mz - 1}, device_id_type=MESH)

    @pl.when(mz < nz - 1)
    def _():
        pl.semaphore_signal(barrier, inc=1, device_id={"freq": mz + 1}, device_id_type=MESH)

    ends = (mz > 0).astype(jnp.int32) + (mz < nz - 1).astype(jnp.int32)
    pl.semaphore_wait(barrier, nx + ends)

    def x_copy(d, k):
        piece = down.at[k, :, pl.ds(mx * fl, fl)]
        return pltpu.make_async_remote_copy(
            src_ref=piece, dst_ref=piece,
            send_sem=x_send.at[d, k], recv_sem=x_recv.at[d, k],
            device_id={"shot": lax.rem(mx + d, nx)}, device_id_type=MESH,
        )

    def c_copy(k):
        return pltpu.make_async_remote_copy(
            src_ref=mod_mine.at[k], dst_ref=mod_other.at[k],
            send_sem=c_send.at[k], recv_sem=c_recv.at[k],
            device_id={"rcv": 1 - mc}, device_id_type=MESH,
        )

    def w_of(way):
        return 0 if way > 0 else 1

    def last(z, way):
        return z == (nz - 1 if way > 0 else 0)

    def a_copy(src, slot, k, way):
        return pltpu.make_async_remote_copy(
            src_ref=src, dst_ref=out.at[pl.ds(0, helped), slot, k],
            send_sem=za_send.at[w_of(way), slot, k], recv_sem=za_recv.at[w_of(way), slot, k],
            device_id={"freq": mz + way}, device_id_type=MESH,
        )

    def b_copy(src, slot, k, way):
        return pltpu.make_async_remote_copy(
            src_ref=src, dst_ref=out.at[pl.ds(helped, blocks - helped), slot, k],
            send_sem=zb_send.at[w_of(way), slot, k], recv_sem=zb_recv.at[w_of(way), slot, k],
            device_id={"freq": mz + way}, device_id_type=MESH,
        )

    def block_copy(slot, b, way):
        piece = out.at[b, slot]
        return pltpu.make_async_remote_copy(
            src_ref=piece, dst_ref=piece,
            send_sem=zc_send.at[w_of(way), slot, b], recv_sem=zc_recv.at[w_of(way), slot, b],
            device_id={"freq": mz + way}, device_id_type=MESH,
        )

    def given_copy(b, way):
        return pltpu.make_async_remote_copy(
            src_ref=made.at[b], dst_ref=given.at[b],
            send_sem=g_send.at[b], recv_sem=g_recv.at[b],
            device_id={"freq": mz + way}, device_id_type=MESH,
        )

    a_own = lambda k: upd.at[k, pl.ds(0, helped)]
    b_own = lambda k: upd.at[k, pl.ds(helped, blocks - helped)]
    a_out = lambda slot, k: out.at[pl.ds(0, helped), slot, k]
    b_out = lambda slot, k: out.at[pl.ds(helped, blocks - helped), slot, k]

    def own_copy(k):
        return pltpu.make_async_copy(upd.at[k], out.at[:, mz, k], own_sem.at[k])

    column = mc * width + iota((lines, width), 1)
    select = (column == pos[:, :]).astype(jnp.float32)

    def make_down(k, carry):
        for c in range(2):
            parts = []
            lines_k = data[c, pl.ds(pl.multiple_of(k * fl, fl), fl)].astype(jnp.float32)
            for f in range(FC):
                w = wav[c, k * FC + f]
                parts.append(w * select - lines_k[f * lines:(f + 1) * lines])
            down[k, c, pl.ds(pl.multiple_of(mx * fl, fl), fl)] = jnp.concatenate(
                parts, axis=0
            ).astype(jnp.bfloat16)
        for d in range(1, nx):
            x_copy(d, k).start()
        return carry

    lax.fori_loop(0, nchunk, make_down, 0)

    n = 2 * fi
    dst, src = iota((n, n), 0), iota((n, n), 1)
    want = (dst // FC % 2) * fi + (dst % FC) * rows + dst // (2 * FC)
    perm = (src == want).astype(jnp.bfloat16)

    def chunk_of(ref, k):
        part = pl.ds(pl.multiple_of(k * fi, fi), fi)
        return jnp.concatenate([ref[0, part], ref[1, part]], axis=0)

    def permute(k, carry):
        est_p[k] = jnp.dot(
            perm, chunk_of(est, k), preferred_element_type=jnp.float32
        ).astype(jnp.bfloat16)
        return carry

    lax.fori_loop(0, nchunk, permute, 0)

    cols = nx * fl
    shots = win.shape[2]
    s_row, s_col = iota((shots, cols), 0), iota((shots, cols), 1)
    spread = (s_row == (s_col // fl) * lines + s_col % lines).astype(jnp.bfloat16)
    shape3 = (rows, FC, cols)
    same = iota(shape3, 1) == iota(shape3, 2) % fl // lines
    scale = step[0]

    def model(k):
        for d in range(1, nx):
            here = down.at[k, :, pl.ds(lax.rem(mx + nx - d, nx) * fl, fl)]
            pltpu.make_async_remote_copy(
                src_ref=here, dst_ref=here,
                send_sem=x_send.at[d, k], recv_sem=x_recv.at[d, k],
                device_id={"shot": lax.rem(mx + d, nx)}, device_id_type=MESH,
            ).wait_recv()
        lines_k = down[k].reshape(2 * cols, width)
        m = lax.dot_general(
            est_p[k], lines_k, (((1,), (1,)), ((), ())), preferred_element_type=jnp.float32
        ).reshape(rows, 2, FC, 2 * cols)
        mod_mine[k, 0] = m[:, 0, :, :cols] - m[:, 1, :, cols:]
        mod_mine[k, 1] = m[:, 0, :, cols:] + m[:, 1, :, :cols]
        c_copy(k).start()

    def update(k):
        c_copy(k).wait_recv()
        total_re = mod_mine[k, 0] + mod_other[k, 0]
        total_im = mod_mine[k, 1] + mod_other[k, 1]
        w = jnp.dot(perm, chunk_of(win, k), preferred_element_type=jnp.float32).astype(jnp.bfloat16)
        w = jnp.dot(w, spread, preferred_element_type=jnp.float32).reshape(rows, 2, FC, cols)
        e_re = jnp.where(same, w[:, 0] - total_re, 0.0)
        e_im = jnp.where(same, w[:, 1] - total_im, 0.0)
        e = jnp.stack(
            [jnp.concatenate([e_re, e_im], axis=2), jnp.concatenate([e_im, -e_re], axis=2)], axis=1
        ).reshape(n, 2 * cols).astype(jnp.bfloat16)
        grad = jnp.dot(e, down[k].reshape(2 * cols, width), preferred_element_type=jnp.float32)
        new = (est_p[k].astype(jnp.float32) - scale * (grad * norm)).astype(jnp.bfloat16)
        for b in range(blocks):
            upd[k, b] = new[:, b * BLOCK:(b + 1) * BLOCK]
        own_copy(k).start()
        for way in (1, -1):
            @pl.when(jnp.logical_not(last(mz, way)))
            def _():
                b_copy(b_own(k), mz, k, way).start()

                if helped:
                    @pl.when(jnp.logical_not(last(mz + way, way)))
                    def _():
                        a_copy(a_own(k), mz, k, way).start()

    def near(k):
        for way in (1, -1):
            slot = mz - way

            @pl.when((slot >= 0) & (slot < nz))
            def _():
                b_copy(b_out(slot, k), slot, k, way).wait_recv()

                if helped:
                    @pl.when(jnp.logical_not(last(mz, way)))
                    def _():
                        a_copy(a_out(slot, k), slot, k, way).wait_recv()

                @pl.when(last(mz + way, way))
                def _():
                    b_copy(b_out(slot, k), slot, k, way).start()

    def step_of(k, carry):
        @pl.when(k < nchunk)
        def _():
            model(k)
            update(k)

        @pl.when(k >= LAG)
        def _():
            near(k - LAG)

        return carry

    lax.fori_loop(0, nchunk + LAG, step_of, 0)

    def own_done(k, carry):
        own_copy(k).wait()
        return carry

    lax.fori_loop(0, nchunk, own_done, 0)

    def hand_on(b, carry):
        for way in (1, -1):
            slot = mz - way
            inside = (slot >= 0) & (slot < nz)
            nxt = mz + way

            @pl.when(inside & (nxt > 0) & (nxt < nz - 1))
            def _():
                block_copy(slot, b, way).start()

        return carry

    lax.fori_loop(0, blocks, hand_on, 0)

    def far(h, carry):
        def one(b, carry):
            for way in (1, -1):
                slot = mz - way * h
                nxt = mz + way
                inside = (slot >= 0) & (slot < nz)
                at_end = last(mz, way)

                @pl.when(inside & jnp.logical_not(at_end))
                def _():
                    block_copy(slot, b, way).wait_recv()

                    @pl.when(jnp.logical_not(last(nxt, way)) | (b >= helped))
                    def _():
                        block_copy(slot, b, way).start()

                    if helped:
                        @pl.when(last(nxt, way) & (b < helped) & last(slot, -way))
                        def _():
                            load = pltpu.make_async_copy(out.at[b], ubuf, ubuf_sem)
                            load.start()
                            load.wait()
                            make_traces(
                                ubuf.reshape(nz * nchunk, ubuf.shape[2], BLOCK), table, level[0],
                                gain, rows, t_group, sparse, made.at[b],
                            )
                            given_copy(b, way).start()

                @pl.when(inside & at_end & (b >= helped))
                def _():
                    if not near_by:
                        block_copy(slot, b, way).wait_recv()

            return carry

        near_by = isinstance(h, int)
        return lax.fori_loop(0, blocks, one, carry)

    def end_chunk(k, carry):
        for way in (1, -1):
            slot = mz - 2 * way

            @pl.when((slot >= 0) & (slot < nz) & last(mz, way))
            def _():
                b_copy(b_out(slot, k), slot, k, way).wait_recv()

        return carry

    if nz > 2:
        lax.fori_loop(0, nchunk, end_chunk, 0)
        far(2, 0)
    lax.fori_loop(3, nz, far, 0)

    if helped:
        def take(b, carry):
            for way in (1, -1):
                @pl.when(last(mz, way))
                def _():
                    given_copy(b, way).wait_recv()

                @pl.when(last(mz + way, way))
                def _():
                    given_copy(b, way).wait_send()

            return carry

        lax.fori_loop(0, helped, take, 0)

    def drain(k, carry):
        for d in range(1, nx):
            x_copy(d, k).wait_send()
        c_copy(k).wait_send()
        for way in (1, -1):
            nxt = mz + way

            @pl.when(jnp.logical_not(last(mz, way)))
            def _():
                b_copy(b_own(k), mz, k, way).wait_send()

                if helped:
                    @pl.when(jnp.logical_not(last(nxt, way)))
                    def _():
                        a_copy(a_own(k), mz, k, way).wait_send()

            slot = mz - way

            @pl.when((slot >= 0) & (slot < nz) & last(nxt, way))
            def _():
                b_copy(b_own(k), slot, k, way).wait_send()

        return carry

    lax.fori_loop(0, nchunk, drain, 0)

    def drain_far(h, carry):
        def one(b, carry):
            for way in (1, -1):
                slot = mz - way * h
                nxt = mz + way
                inside = (slot >= 0) & (slot < nz) & (nxt >= 0) & (nxt < nz)
                to_end = last(nxt, way)

                @pl.when(inside & (jnp.logical_not(to_end) | ((b >= helped) & (h > 1))))
                def _():
                    block_copy(slot, b, way).wait_send()

            return carry

        return lax.fori_loop(0, blocks, one, carry)

    lax.fori_loop(1, nz, drain_far, 0)


def trace_kernel(rows, t_group, gain, helped, level, taken, table, u, given, out, sparse):
    ready = (pl.program_id(0) < helped) & (taken[0] > 0)

    @pl.when(ready)
    def _():
        out[...] = given[...]

    @pl.when(jnp.logical_not(ready))
    def _():
        make_traces(u, table, level[0], gain, rows, t_group, sparse, out)


def body(nx, nz, data, estimate, window_data, wavelet, positions, bins, threshold, step):
    _, nf, lines, width = data.shape
    rows = estimate.shape[2]
    shots = window_data.shape[3]
    nchunk = nf // FC
    norm = 1.0 / math.sqrt(shots * RCV)
    fi, cols = FC * rows, nx * FC * lines
    mz = lax.axis_index("freq")
    nt = NT // nz
    blocks, groups = width // BLOCK, nz * nchunk
    helped = 3 * blocks // 8 if nz >= 4 else 0
    held = max(helped, 1)
    gain, t_group = math.sqrt(RCV / NF), 32
    level = threshold.astype(jnp.float32) / 64.0

    def table_of(z):
        times = z * nt + lax.iota(jnp.int32, nt)
        phase = times[:, None] * bins[None, :] % NT
        angle = 2.0 * math.pi / NT * phase.astype(jnp.float32)
        table = jnp.stack([jnp.cos(angle), -jnp.sin(angle)], axis=1).astype(jnp.bfloat16)
        table = table.reshape(nt, 2, groups, FC).transpose(0, 2, 1, 3)
        return table.reshape(nt, 2 * nz * nf)

    vmem = pl.BlockSpec(memory_space=pltpu.VMEM)
    smem = pl.BlockSpec(memory_space=pltpu.SMEM)
    hbm = pl.BlockSpec(memory_space=pl.ANY)
    dma = pltpu.SemaphoreType.DMA
    spectra, given = pl.pallas_call(
        partial(
            update_kernel, nx, nz, nchunk, rows, lines, norm, blocks, helped, gain, t_group
        ),
        out_shape=(
            jax.ShapeDtypeStruct((blocks, nz, nchunk, 2 * fi, BLOCK), jnp.bfloat16),
            jax.ShapeDtypeStruct((held, nt * rows, BLOCK), jnp.bfloat16),
        ),
        in_specs=[vmem, vmem, vmem, smem, vmem, smem, smem, vmem],
        out_specs=(hbm, hbm),
        scratch_shapes=[
            pltpu.VMEM((nchunk, 2, cols, width), jnp.bfloat16),
            pltpu.VMEM((nchunk, 2 * fi, width), jnp.bfloat16),
            pltpu.VMEM((nchunk, blocks, 2 * fi, BLOCK), jnp.bfloat16),
            pltpu.VMEM((nchunk, 2, rows, FC, cols), jnp.float32),
            pltpu.VMEM((nchunk, 2, rows, FC, cols), jnp.float32),
            pltpu.VMEM((nz, nchunk, 2 * fi, BLOCK), jnp.bfloat16),
            pltpu.VMEM((rows, nt, BLOCK), jnp.bfloat16),
            pltpu.VMEM((held, nt * rows, BLOCK), jnp.bfloat16),
            dma((nx, nchunk)), dma((nx, nchunk)),
            dma((nchunk,)), dma((nchunk,)),
            dma((2, nz, nchunk)), dma((2, nz, nchunk)),
            dma((2, nz, nchunk)), dma((2, nz, nchunk)),
            dma((2, nz, blocks)), dma((2, nz, blocks)),
            dma((held,)), dma((held,)),
            dma((nchunk,)), dma,
        ],
        compiler_params=pltpu.CompilerParams(
            collective_id=0, has_side_effects=True, vmem_limit_bytes=58 << 20
        ),
        name="update",
    )(
        data.reshape(2, nf * lines, width),
        estimate.reshape(2, nf * rows, width),
        window_data.reshape(2, nf * rows, shots),
        wavelet,
        positions[:, None],
        step,
        level,
        table_of(jnp.where(mz < nz // 2, 0, nz - 1)),
    )
    taken = ((mz == 0) | (mz == nz - 1)).astype(jnp.int32)[None]
    traces = pl.pallas_call(
        partial(trace_kernel, rows, t_group, gain, helped),
        out_shape=jax.ShapeDtypeStruct((nt * rows, width), jnp.bfloat16),
        grid=(blocks,),
        in_specs=[
            smem,
            smem,
            pl.BlockSpec((nt, 2 * nz * nf), lambda j: (0, 0)),
            pl.BlockSpec((None, groups, 2 * fi, BLOCK), lambda j: (j, 0, 0, 0)),
            pl.BlockSpec(
                (None, nt * rows, BLOCK), lambda j: (jnp.minimum(j, held - 1), 0, 0)
            ),
        ],
        out_specs=pl.BlockSpec((nt * rows, BLOCK), lambda j: (0, j)),
        scratch_shapes=[pltpu.VMEM((rows, nt, BLOCK), jnp.bfloat16)],
        compiler_params=pltpu.CompilerParams(vmem_limit_bytes=60 << 20),
        name="traces",
    )(level, taken, table_of(mz), spectra.reshape(blocks, groups, 2 * fi, BLOCK), given)
    return traces.reshape(nt, rows, width)


def make_pairs(spec, b, table, lv, gain, rows, t_group, sparse, out, at):
    groups = spec.shape[0]
    part = 2 * GF * PAIR
    nt = table.shape[0] // PAIR
    for p in range(rows // PAIR):
        up = jnp.concatenate(
            [
                spec[:, b + h, p * part:(p + 1) * part].reshape(groups * part, TILE)
                for h in range(2)
            ],
            axis=1,
        )
        tr = jnp.dot(table[...], up, preferred_element_type=jnp.float32) * gain
        sparse[p] = (jnp.maximum(tr - lv, 0.0) + jnp.minimum(tr + lv, 0.0)).astype(jnp.bfloat16)
    lined = sparse.reshape(rows, nt, 2 * TILE)
    n = t_group * rows
    dst, src = iota((n, n), 0), iota((n, n), 1)
    perm = (src == (dst % rows) * t_group + dst // rows).astype(jnp.bfloat16)
    for g in range(nt // t_group):
        x = lined[:, g * t_group:(g + 1) * t_group, :].reshape(n, 2 * TILE)
        y = jnp.dot(perm, x, preferred_element_type=jnp.float32).astype(jnp.bfloat16)
        for h in range(2):
            out[at + h, g * n:(g + 1) * n, :] = y[:, h * TILE:(h + 1) * TILE]


def relay_kernel(
    nx, nz, nchunk, rows, lines, shots, norm, blocks, plain, early, gain, t_group,
    data, est, win_in, wav_in, pos_in, bins_in, thr_in, step_in, out,
    win, wav, pos, bins, thr, step, i_sem,
    dbuf, ebuf, down, spec, mod_mine, mod_other, tables, sparse, made,
    d_sem, e_sem, x_send, x_recv, c_send, c_recv, z_send, near_recv, pair_recv,
    out_recv, late_recv, trace_recv,
):
    mx = lax.axis_index("shot")
    mz = lax.axis_index("freq")
    mc = lax.axis_index("rcv")
    width = data.shape[2]
    fl = GF * lines
    fi = GF * rows
    n = 2 * fi
    end = jnp.where(mz < 2, 0, 3)
    inner = jnp.where(mz < 2, 1, 2)
    is_end = mz == end
    wide = mc == 0
    first = plain + wide.astype(jnp.int32)
    is_inner = jnp.logical_not(is_end)

    smalls = [
        pltpu.make_async_copy(src, dst, i_sem.at[i])
        for i, (src, dst) in enumerate(
            ((pos_in, pos), (wav_in, wav), (win_in, win), (step_in, step), (thr_in, thr),
             (bins_in, bins))
        )
    ]

    def load(ref, buf, sem, k):
        return pltpu.make_async_copy(
            ref.at[:, pl.ds(pl.multiple_of(k * fl, fl), fl)], buf.at[k], sem.at[k % AHEAD]
        )

    for copy in smalls[:2]:
        copy.start()
    for k in range(AHEAD):
        load(data, dbuf, d_sem, k).start()
    for copy in smalls[2:]:
        copy.start()

    barrier = pltpu.get_barrier_semaphore()
    for d in range(1, nx):
        pl.semaphore_signal(
            barrier, inc=1, device_id={"shot": lax.rem(mx + d, nx)}, device_id_type=MESH
        )
    pl.semaphore_signal(barrier, inc=1, device_id={"rcv": 1 - mc}, device_id_type=MESH)
    for z in (jnp.where(is_end, inner, end), jnp.where(is_end, 3 - inner, 3 - end)):
        pl.semaphore_signal(barrier, inc=1, device_id={"freq": z}, device_id_type=MESH)

    @pl.when(is_inner)
    def _():
        pl.semaphore_signal(barrier, inc=1, device_id={"freq": 3 - mz}, device_id_type=MESH)

    def x_copy(d, k, piece):
        here = down.at[k, :, pl.ds(piece * fl, fl)] if k is not None else (
            down.at[:, :, pl.ds(piece * fl, fl)]
        )
        return pltpu.make_async_remote_copy(
            src_ref=here, dst_ref=here,
            send_sem=x_send.at[d - 1], recv_sem=x_recv.at[d - 1, 0 if k is None else k],
            device_id={"shot": lax.rem(mx + d, nx)}, device_id_type=MESH,
        )

    def c_copy(k):
        return pltpu.make_async_remote_copy(
            src_ref=mod_mine.at[k], dst_ref=mod_other.at[k],
            send_sem=c_send.at[0], recv_sem=c_recv.at[k % 2],
            device_id={"rcv": 1 - mc}, device_id_type=MESH,
        )

    c_all = pltpu.make_async_remote_copy(
        src_ref=mod_mine, dst_ref=mod_other, send_sem=c_send.at[0], recv_sem=c_recv.at[0],
        device_id={"rcv": 1 - mc}, device_id_type=MESH,
    )

    def z_copy(kind, here, there, recv, to):
        return pltpu.make_async_remote_copy(
            src_ref=here, dst_ref=there, send_sem=z_send.at[kind], recv_sem=recv,
            device_id={"freq": to}, device_id_type=MESH,
        )

    def chunk_copy(kind, slot, k, count, recv, to):
        at = slot * nchunk + k if k is not None else pl.ds(slot * nchunk, nchunk)
        here = spec.at[at, pl.ds(0, count)]
        return z_copy(kind, here, here, recv, to)

    def block_copy(kind, slot, b, to):
        at = b if b is not None else pl.ds(early, blocks - early)
        here = spec.at[pl.ds(slot * nchunk, nchunk), at]
        recv = late_recv.at[b - early if b is not None else 0]
        return z_copy(kind, here, here, recv, to)

    which = lambda k: 0 if k is None else k
    end_near = lambda k: chunk_copy(0, end, k, early, near_recv.at[0], inner)
    end_far = lambda k, of: chunk_copy(1, of, k, early, pair_recv.at[which(k)], 3 - inner)
    across = lambda k, own: chunk_copy(2, own, k, early, pair_recv.at[which(k)], 3 - mz)
    late_near = lambda b: block_copy(6, end, b, inner)
    late_far = lambda b, of: block_copy(7, of, b, 3 - inner)
    late_across = lambda b, own: block_copy(8, own, b, 3 - mz)
    trace_copy = lambda b, at: z_copy(9, made.at[at], out.at[b], trace_recv.at[0], end)

    def by_core(act):
        @pl.when(wide)
        def _():
            act(plain + 1)

        @pl.when(jnp.logical_not(wide))
        def _():
            act(plain)

    def traces_done(act):
        by_core(lambda count: act(z_copy(
            9, made.at[pl.ds(0, blocks - count)], out.at[pl.ds(0, blocks - count)], trace_recv.at[0],
            end,
        )))

    def outward(kind, slot, k, act):
        by_core(lambda count: act(chunk_copy(kind, slot, k, count, out_recv.at[kind - 3], end)))

    out_own = lambda k, act: outward(3, inner, k, act)
    out_opp = lambda k, act: outward(4, 3 - inner, k, act)
    out_far = lambda k, act: outward(5, 3 - end, k, act)
    start = lambda copy: copy.start()
    wait_recv = lambda copy: copy.wait_recv()
    wait_send = lambda copy: copy.wait_send()

    for copy in smalls:
        copy.wait()
    level = thr[0].astype(jnp.float32) / 64.0
    line, column = iota((lines, width), 0), mc * width + iota((lines, width), 1)
    select = jnp.zeros((lines, width), jnp.float32)
    for s in range(lines):
        select = jnp.where((line == s) & (column == pos[s]), 1.0, select)

    def make_down(k):
        load(data, dbuf, d_sem, k).wait()

        @pl.when(k + AHEAD < nchunk)
        def _():
            load(data, dbuf, d_sem, k + AHEAD).start()

        for c in range(2):
            parts = []
            lines_k = dbuf[k, c].astype(jnp.float32)
            for f in range(GF):
                w = wav[c, k * GF + f]
                parts.append(w * select - lines_k[f * lines:(f + 1) * lines])
            down[k, c, pl.ds(pl.multiple_of(mx * fl, fl), fl)] = jnp.concatenate(
                parts, axis=0
            ).astype(jnp.bfloat16)

    def share_down(k):
        for d in range(1, nx):
            x_copy(d, k, mx).start()

    dst, src = iota((n, n), 0), iota((n, n), 1)
    want = (dst // GF % 2) * fi + (dst % GF) * rows + dst // (2 * GF)
    perm = (src == want).astype(jnp.bfloat16)

    cols = nx * fl
    nf = nchunk * GF
    col3 = iota((2 * rows, shots, cols), 2)
    shot_of = col3 // fl * lines + col3 % lines
    own_shot = iota((2 * rows, shots, cols), 1) == shot_of
    f_row, f_col = iota((nf, cols), 0), iota((nf, cols), 1) % fl // lines
    shape3 = (GF, rows, cols)
    same = iota(shape3, 0) == iota(shape3, 2) % fl // lines
    scale = step[0]

    def make_table(j, z):
        size, nt = nz * nf, sparse.shape[1] // PAIR
        wide = 2 * PAIR * size
        row, col = iota((size, wide), 0), iota((size, wide), 1)
        match = row == col // (2 * GF * PAIR) * GF + col % GF
        to_re = (match & (col // GF % 2 == 0)).astype(jnp.bfloat16)
        to_im = (match & (col // GF % 2 == 1)).astype(jnp.bfloat16)
        times = z * nt + iota((nt, size), 0)
        phase = times * bins[...] % NT
        angle = 2.0 * math.pi / NT * phase.astype(jnp.float32)
        full = jnp.dot(
            jnp.cos(angle).astype(jnp.bfloat16), to_re, preferred_element_type=jnp.float32
        ) + jnp.dot(
            (-jnp.sin(angle)).astype(jnp.bfloat16), to_im, preferred_element_type=jnp.float32
        )
        member = iota((nt, wide), 1) // (2 * GF) % PAIR
        for a in range(PAIR):
            tables[j, a * nt:(a + 1) * nt] = jnp.where(member == a, full, 0.0).astype(
                jnp.bfloat16
            )

    def spectra_of(k):
        return ebuf[k].reshape(n, width)

    def model(k):
        load(est, ebuf, e_sem, k).wait()

        @pl.when(k + AHEAD < nchunk)
        def _():
            load(est, ebuf, e_sem, k + AHEAD).start()

        for d in range(1, nx):
            x_copy(d, k, lax.rem(mx + nx - d, nx)).wait_recv()
        m_re, m_im = [
            lax.dot_general(
                spectra_of(k), down[k, c], (((1,), (1,)), ((), ())),
                preferred_element_type=jnp.float32,
            )
            for c in range(2)
        ]
        mod_mine[k, 0] = m_re[:fi] - m_im[fi:]
        mod_mine[k, 1] = m_im[:fi] + m_re[fi:]
        c_copy(k).start()

    def update(k):
        pick = (f_row == k * GF + f_col).astype(jnp.bfloat16)
        w = jnp.dot(win[...], pick, preferred_element_type=jnp.float32)
        w = jnp.where(own_shot, w.reshape(2 * rows, shots, cols), 0.0).sum(axis=1)
        c_copy(k).wait_recv()
        total_re = (mod_mine[k, 0] + mod_other[k, 0]).reshape(shape3)
        total_im = (mod_mine[k, 1] + mod_other[k, 1]).reshape(shape3)
        e_re = jnp.where(same, w[None, :rows] - total_re, 0.0).reshape(fi, cols)
        e_im = jnp.where(same, w[None, rows:] - total_im, 0.0).reshape(fi, cols)
        e = jnp.concatenate(
            [jnp.concatenate([e_re, e_im], axis=1), jnp.concatenate([e_im, -e_re], axis=1)], axis=0
        ).astype(jnp.bfloat16)
        for lo, hi in ((0, early), (early, blocks)):
            at = slice(lo * TILE, hi * TILE)
            wide_part = (hi - lo) * TILE
            grad = jnp.dot(
                e, down[k, :, :, at].reshape(2 * cols, wide_part),
                preferred_element_type=jnp.float32,
            )
            old = ebuf[k, :, :, at].reshape(n, wide_part)
            new = (old.astype(jnp.float32) - scale * (grad * norm)).astype(jnp.bfloat16)
            new = jnp.dot(perm, new, preferred_element_type=jnp.float32).astype(jnp.bfloat16)
            for b in range(lo, hi):
                spec[mz * nchunk + k, b] = new[:, (b - lo) * TILE:(b - lo + 1) * TILE]
            if lo == 0:
                send(k)

    def send(k):
        @pl.when(is_end)
        def _():
            end_far(k, mz).start()
            end_near(k).start()

        @pl.when(is_inner)
        def _():
            out_own(k, start)
            across(k, mz).start()

    def relay(k):
        two = spec.at[pl.ds(0, 2), pl.ds(0, early)]
        z_copy(2, two, two, pair_recv.at[k], 3 - mz).wait_recv()
        out_opp(k, start)
        out_far(k, start)

    make_down(0)
    pl.semaphore_wait(barrier, nx + 2 + is_inner.astype(jnp.int32))
    share_down(0)

    for k in range(AHEAD):
        load(est, ebuf, e_sem, k).start()
    make_down(1)
    share_down(1)

    def step_of(k, carry):
        @pl.when(k < nchunk - 2)
        def _():
            make_down(k + 2)
            share_down(k + 2)

        for j, z in enumerate((mz, end)):
            @pl.when(k == nchunk // 4 * (j + 1))
            def _():
                make_table(j, z)

        @pl.when(k < nchunk)
        def _():
            model(k)
            update(k)

        @pl.when(is_inner & (k >= 1))
        def _():
            relay(k - 1)

        return carry

    lax.fori_loop(0, nchunk + 1, step_of, 0)

    def own_pair(b):
        make_pairs(spec, b, tables.at[0], level, gain, rows, t_group, sparse, out, b)

    def help_pair(b, at):
        make_pairs(spec, b, tables.at[1], level, gain, rows, t_group, sparse, made, at)

    def arrived(b):
        three = spec.at[pl.ds(0, nchunk), pl.ds(0, 3)]
        z_copy(8, three, three, late_recv.at[b - early], 3 - mz).wait_recv()

    def loop(lo, hi, f):
        def one(i, carry):
            f(i)
            return carry

        lax.fori_loop(lo, hi, one, 0)

    @pl.when(is_inner)
    def _():
        loop(early, blocks, lambda b: late_across(b, mz).start())
        end_near(None).wait_recv()
        narrow = 1 - wide.astype(jnp.int32)

        def both(j):
            b = first + 2 * j

            @pl.when(b >= early)
            def _():
                arrived(b)

            @pl.when(b + 1 >= early)
            def _():
                arrived(b + 1)

            help_pair(b, 2 * j)
            trace_copy(b, 2 * j).start()
            trace_copy(b + 1, 2 * j + 1).start()
            done = (b - narrow) // 2
            loop(jnp.where(j == 0, 0, done), done + 1, lambda i: own_pair(2 * i))

        loop(0, (blocks - plain) // 2, both)

        @pl.when(jnp.logical_not(wide))
        def _():
            last = blocks - 1
            arrived(last)
            help_pair(last - 1, last - plain)
            trace_copy(last, last - plain + 1).start()
            own_pair(last - 1)

        across(None, mz).wait_send()
        late_across(None, mz).wait_send()
        for copies in (out_own, out_opp, out_far):
            copies(None, wait_send)
        traces_done(wait_send)

    @pl.when(is_end)
    def _():
        def late(b):
            late_far(b, mz).start()
            late_near(b).start()

        loop(early, blocks, late)

        for copies in (out_own, out_opp, out_far):
            copies(None, wait_recv)
        loop(0, (plain + 1) // 2, lambda j: own_pair(jnp.minimum(2 * j, first - 2)))
        traces_done(wait_recv)
        end_near(None).wait_send()
        end_far(None, mz).wait_send()
        late_near(None).wait_send()
        late_far(None, mz).wait_send()

    for d in range(1, nx):
        x_copy(d, None, mx).wait_send()
    c_all.wait_send()


def place_kernel(traces, out, sem):
    copies = [
        pltpu.make_async_copy(
            traces.at[b], out.at[:, pl.ds(b * TILE, TILE)], sem.at[b]
        )
        for b in range(traces.shape[0])
    ]
    for copy in copies:
        copy.start()
    for copy in copies:
        copy.wait()


def relay_body(nx, nz, data, estimate, window_data, wavelet, positions, bins, threshold, step):
    _, nf, lines, width = data.shape
    rows = estimate.shape[2]
    shots = window_data.shape[3]
    nchunk = nf // GF
    norm = 1.0 / math.sqrt(shots * RCV)
    fi, cols = GF * rows, nx * GF * lines
    size = nz * nf
    nt = NT // nz
    blocks = width // TILE
    plain = PLAIN * blocks // 16
    early = plain + 3
    gain, t_group = math.sqrt(RCV / NF), 32

    vmem = pl.BlockSpec(memory_space=pltpu.VMEM)
    hbm = pl.BlockSpec(memory_space=pl.ANY)
    dma = pltpu.SemaphoreType.DMA
    traces = pl.pallas_call(
        partial(
            relay_kernel, nx, nz, nchunk, rows, lines, shots, norm, blocks, plain, early,
            gain, t_group,
        ),
        out_shape=pltpu.VMEM((blocks, nt * rows, TILE), jnp.bfloat16),
        in_specs=[hbm] * 8,
        out_specs=vmem,
        scratch_shapes=[
            pltpu.VMEM((2 * rows * shots, nf), jnp.bfloat16),
            pltpu.SMEM((2, nf), jnp.float32),
            pltpu.SMEM((lines,), jnp.int32),
            pltpu.VMEM((1, size), jnp.int32),
            pltpu.SMEM((1,), jnp.int32),
            pltpu.SMEM((1,), jnp.float32),
            dma((6,)),
            pltpu.VMEM((nchunk, 2, GF * lines, width), jnp.bfloat16),
            pltpu.VMEM((nchunk, 2, fi, width), jnp.bfloat16),
            pltpu.VMEM((nchunk, 2, cols, width), jnp.bfloat16),
            pltpu.VMEM((nz * nchunk, blocks, 2 * fi, TILE), jnp.bfloat16),
            pltpu.VMEM((nchunk, 2, fi, cols), jnp.float32),
            pltpu.VMEM((nchunk, 2, fi, cols), jnp.float32),
            pltpu.VMEM((2, PAIR * nt, 2 * PAIR * size), jnp.bfloat16),
            pltpu.VMEM((rows // PAIR, PAIR * nt, 2 * TILE), jnp.bfloat16),
            pltpu.VMEM((blocks - plain + 1, nt * rows, TILE), jnp.bfloat16),
            dma((AHEAD,)), dma((AHEAD,)),
            dma((nx - 1,)), dma((nx - 1, nchunk)),
            dma((1,)), dma((2,)),
            dma((10,)), dma((1,)), dma((nchunk,)),
            dma((3,)), dma((blocks - early,)), dma((1,)),
        ],
        compiler_params=pltpu.CompilerParams(
            collective_id=1, has_side_effects=True, vmem_limit_bytes=48 << 20
        ),
        name="relay",
    )(
        data.reshape(2, nf * lines, width),
        estimate.reshape(2, nf * rows, width),
        window_data.transpose(0, 2, 3, 1).reshape(2 * rows * shots, nf),
        wavelet,
        positions,
        bins.reshape(1, size),
        threshold,
        step,
    )
    placed = pl.pallas_call(
        place_kernel,
        out_shape=jax.ShapeDtypeStruct((nt * rows, width), jnp.bfloat16),
        in_specs=[vmem],
        out_specs=hbm,
        scratch_shapes=[dma((blocks,))],
        compiler_params=pltpu.CompilerParams(vmem_limit_bytes=4 << 20),
        name="place",
    )(traces)
    return placed.reshape(nt, rows, width)


def solution(mesh):
    nz = mesh.shape["freq"]
    return jax.shard_map(
        partial(relay_body if nz == 4 else body, mesh.shape["shot"], nz),
        mesh=mesh,
        in_specs=(
            P(None, "freq", ("grp", "shot"), "rcv"),
            P(None, "freq", ("grp", "shot"), "rcv"),
            P(None, "freq", ("grp", "shot"), None),
            P(None, ("grp", "freq")),
            P(("grp", "shot")),
            P("grp"),
            P("grp"),
            P("grp"),
        ),
        out_specs=P("freq", ("grp", "shot"), "rcv"),
        check_vma=False,
    )
```
